32 devices in a mesh: row: 2 (over core), bulk: 16 (over z, y, x).
Axes of the slice: x: 2, y: 2, z: 4, core: 2. Of those that a mesh axis runs over, the one named last changes fastest.
Arguments:
- residual_in: float32 [512, 16384], P('row', 'bulk'), may hold values from -6 to 6
- amplitudes: float32 [512, 2048], P('row', 'bulk'), may hold values from -6 to 6
- integral_tiles: float32 [256, 128, 128], P('bulk', 'row'), may hold values from -0.375 to 0.375
- tile_reader: int32 [256, 1], P('bulk'), may hold values from 0 to 15; in each aligned block of 16 rows (0 to 15, 16 to 31, ...) at most 2 rows name the same one
- tile_k: int32 [256], P('bulk'), may hold values from 0 to 15
- tile_column: int32 [256], P('bulk'), may hold values from 0 to 7
Outputs:
- residual_out: float32 [512, 16384], P('row', 'bulk')
The draws below stay inside these ranges and needn't reach their ends.
Inputs may be any that keep to these rules, and one draw needn't show every extreme that they name: `tile_reader`: among the 16 tiles stored on one index of bulk (aligned blocks of 16 entries), at most 2 name the same reader; some block has exactly 2 for some reader.
All inputs are finite; a program needn't handle non-finite values.
Results may differ from the reference program's by a relative error of at most 0.0003.
Values sent between devices are 32-bit elements; how exact they have to be, the bound alone decides.
No kernel may reach another device: no remote copies, remote signals or barrier semaphores. Data moves between devices by JAX's collectives and lax.ppermute only.
A program may use at most 64 MiB of HBM per device.

```python
import math
import jax
import jax.numpy as jnp
import numpy as np
from jax import lax

TILE = 128
KT = 16
CT = 8
SLOT = 2
NS = 16
ROWS = 512
COLS = 128
NTILES = 256
N_BULK = 16


def set_ends(entries, stream_key, smallest, largest):
    place = [jax.random.randint(jax.random.fold_in(stream_key, axis), (), 0, length) for axis, length in enumerate(entries.shape)]
    main_axis = entries.shape.index(max(entries.shape))
    beside = place[:main_axis] + [(place[main_axis] + 1) % entries.shape[main_axis]] + place[main_axis + 1:]
    return entries.at[tuple(place)].set(smallest).at[tuple(beside)].set(largest)


def block_levels(key, shape, pieces, low, largest):
    gain = 1.0
    for dim, parts in pieces:
        draws = jax.random.uniform(jax.random.fold_in(jax.random.fold_in(key, 6), dim), (parts,), jnp.float32, low / len(pieces), largest / len(pieces))
        gain = gain * jnp.repeat(jnp.exp(draws), shape[dim] // parts).reshape((-1,) + (1,) * (len(shape) - 1 - dim))
    return gain


def routed_block(rng, own, number, rows, number_of, top, bound, lean):
    ranking = jax.random.permutation(rng, number_of)
    heavy_load, ordinary = load_shares(number_of, rows * top, bound, lean, True), load_shares(number_of, rows * top, bound, lean, False)
    places = jnp.arange(number_of)

    def named(lengths, rotation):
        used = int((lengths > 0).sum())
        fixed = max(1, used // 4)
        moved = fixed + (places - fixed + rotation * (used - fixed)) % max(1, number_of - fixed)
        return jnp.zeros((number_of,), jnp.int32).at[ranking[jnp.where(places < fixed, places, moved)]].set(jnp.asarray(lengths, jnp.int32))

    lengths = jnp.where(number % 4 == 0, named(heavy_load, number // 4), named(ordinary, number - number // 4 - 1))
    mixed = jax.random.permutation(jax.random.fold_in(own, 3), number_of)
    giver, receiver = mixed[0:number_of // 2 * 2:2], mixed[1:number_of // 2 * 2:2]
    margin = jnp.minimum(lengths[giver] - 1, bound - lengths[receiver]) // 2
    margin = jnp.where((giver == ranking[0]) | (receiver == ranking[0]) | (lengths[receiver] == 0), 0, jnp.maximum(margin, 0))
    moved = jax.random.randint(jax.random.fold_in(own, 4), (number_of // 2,), 0, 1 << 20) % (margin + 1)
    lengths = lengths.at[giver].add(-moved).at[receiver].add(moved)
    items = jnp.searchsorted(jnp.cumsum(lengths), jnp.arange(rows * top), side="right").astype(jnp.int32)
    grid = items.reshape(top, rows).T
    grid = grid[jax.random.permutation(jax.random.fold_in(own, 1), rows)]
    rotation = jax.random.randint(jax.random.fold_in(own, 2), (rows, 1), 0, top)
    return jnp.take_along_axis(grid, (jnp.arange(top)[None, :] + rotation) % top, axis=1)


def load_shares(count, total, bound, slope, full):
    loads = [(1 << 20) // math.isqrt(rank ** slope) + 1 for rank in range(1, count + 1)]
    largest = bound if full else min(bound, max(-(-total // count), total * loads[0] // sum(loads)))
    least = 1 if total - largest >= count - 1 else 0
    given, surplus = [largest] + [least] * (count - 1), total - largest - least * (count - 1)
    while surplus > 0:
        movable = [i for i in range(1, count) if given[i] < largest] or [i for i in range(1, count) if given[i] < bound]
        pool, remaining = sum([loads[i] for i in movable]), surplus
        for i in movable:
            extra = min(bound - given[i], max(1, remaining * loads[i] // pool), surplus)
            given[i] = given[i] + extra
            surplus = surplus - extra
    return np.array(given)


def scatter_about(rng, extent, width, most, cuts=(), held_as=jnp.bfloat16):
    factor_of = block_levels(rng, extent, cuts, -0.22, 0.18) if cuts else 1.0
    result = jax.random.normal(rng, extent, jnp.float32) * width * factor_of
    return jnp.minimum(jnp.maximum(result, -most), most).astype(held_as)


def setup_inputs(seed: int = 0) -> dict:
    splits = jax.random.split(jax.random.key(seed), 7)
    residual_in = scatter_about(splits[0], (ROWS, COLS * TILE), 1.0, 6.0, ((0, 2), (1, 16)), jnp.float32)
    amplitudes = scatter_about(splits[1], (ROWS, KT * TILE), 1.0, 6.0, ((0, 2), (1, 16)), jnp.float32)
    integral_tiles = scatter_about(splits[2], (NTILES, TILE, TILE), (NS * TILE // CT) ** -0.5, 0.375, ((0, 16), (1, 2)), jnp.float32)
    tile_reader_keys = jax.random.split(jax.random.fold_in(splits[3], 1), NTILES // NS)
    tile_reader_turns = jax.random.permutation(jax.random.fold_in(splits[3], 3), NTILES // NS)
    tile_reader = jax.vmap(lambda own, number: routed_block(jax.random.fold_in(splits[3], 2), own, number, NS, N_BULK, 1, SLOT, 1))(tile_reader_keys, tile_reader_turns).reshape((NTILES, 1))
    tile_k = set_ends(jax.random.randint(splits[4], (NTILES,), 0, KT), jax.random.fold_in(splits[4], 1), 0, KT - 1).astype(jnp.int32)
    tile_column = set_ends(jax.random.randint(splits[5], (NTILES,), 0, CT), jax.random.fold_in(splits[5], 1), 0, CT - 1).astype(jnp.int32)
    return dict(residual_in=residual_in, amplitudes=amplitudes, integral_tiles=integral_tiles, tile_reader=tile_reader, tile_k=tile_k, tile_column=tile_column)


def reference(residual_in, amplitudes, integral_tiles, tile_reader, tile_k, tile_column):
    readers = tile_reader[:, 0]

    def per_reader(target):
        chosen = readers == target
        blocks = jnp.where(chosen[:, None, None], integral_tiles, jnp.zeros_like(integral_tiles))
        placed = jnp.zeros((KT, CT, TILE, TILE), integral_tiles.dtype).at[tile_k, tile_column].add(blocks)
        dense_block = placed.transpose(0, 2, 1, 3).reshape(KT * TILE, CT * TILE)
        return jnp.dot(amplitudes, dense_block, precision=lax.Precision.HIGHEST)

    columns = lax.map(per_reader, jnp.arange(N_BULK, dtype=jnp.int32))
    columns = columns.transpose(1, 0, 2).reshape(ROWS, N_BULK * CT * TILE)
    return residual_in + columns
```

```python
import functools

import jax
import jax.numpy as jnp
from jax import lax
from jax.experimental import pallas as pl
from jax.experimental.pallas import tpu as pltpu
from jax.sharding import PartitionSpec as P

KT = 16
CT = 8
SLOT = 2
META = 8


def pack_kernel(reader_ref, k_ref, column_ref, tiles_ref, out_ref, count_ref):
    count, height, _ = tiles_ref.shape
    targets = out_ref.shape[0]
    out_ref[:, SLOT * height :, :] = jnp.full((targets, META, out_ref.shape[2]), -1.0, jnp.float32)
    for target in range(targets):
        count_ref[target] = 0
    lane = lax.broadcasted_iota(jnp.int32, (META, out_ref.shape[2]), 1)

    def place(j, carry):
        target = reader_ref[j, 0]
        slot = count_ref[target]
        count_ref[target] = slot + 1
        out_ref[target, pl.ds(pl.multiple_of(slot * height, height), height), :] = tiles_ref[j]
        code = (k_ref[j] * CT + column_ref[j]).astype(jnp.float32)
        codes = out_ref[target, SLOT * height :, :]
        out_ref[target, SLOT * height :, :] = jnp.where(lane == slot, code, codes)
        return carry

    lax.fori_loop(0, count, place, 0)


def pack(tiles, readers, tile_k, tile_column, targets):
    _, height, width = tiles.shape
    smem = pl.BlockSpec(memory_space=pltpu.SMEM)
    vmem = pl.BlockSpec(memory_space=pltpu.VMEM)
    return pl.pallas_call(
        pack_kernel,
        out_shape=jax.ShapeDtypeStruct((targets, SLOT * height + META, width), jnp.float32),
        in_specs=[smem, smem, smem, vmem],
        out_specs=vmem,
        scratch_shapes=[pltpu.SMEM((targets,), jnp.int32)],
        cost_estimate=pl.CostEstimate(flops=0, bytes_accessed=4 * tiles.size * 3, transcendentals=0),
    )(readers, tile_k, tile_column, tiles)


def contract_kernel(positions, parts_count, *refs):
    pieces = refs[: len(positions)]
    parts = refs[len(positions) : len(positions) + parts_count]
    residual_ref, out_ref, split_ref, codes_ref, sem = refs[len(positions) + parts_count :]
    targets = parts[0].shape[0]
    height = (parts[0].shape[1] - META) // SLOT
    width = parts[0].shape[2]
    row = lax.axis_index("row")
    me = lax.axis_index("bulk")
    fetch = pltpu.make_async_copy(parts[0].at[:, pl.ds(SLOT * height, META), :], codes_ref, sem)
    fetch.start()
    for piece, held in zip(pieces, positions):
        for at, position in enumerate(held):
            block = piece[at]
            high = block.astype(jnp.bfloat16)
            low = (block - high.astype(jnp.float32)).astype(jnp.bfloat16)
            k = position if position is None else jnp.bitwise_xor(me, position)
            k = at if k is None else k
            split_ref[k] = jnp.concatenate([high, low], axis=1)
    out_ref[...] = residual_ref[...]
    fetch.wait()

    def add(owner, carry):
        for slot in range(SLOT):
            code = codes_ref[owner, 0, slot].astype(jnp.int32)

            @pl.when(code >= 0)
            def _():
                k = code // CT
                column = code - k * CT
                ordered = []
                for place in range(parts_count):
                    piece = parts[0][owner, slot * height : (slot + 1) * height, :]
                    for q in range(1, parts_count):
                        other = parts[q][owner, slot * height : (slot + 1) * height, :]
                        piece = jnp.where(lax.rem(place + q, parts_count) == row, other, piece)
                    ordered.append(piece)
                tile = jnp.concatenate(ordered, axis=0)
                high = tile.astype(jnp.bfloat16)
                low = (tile - high.astype(jnp.float32)).astype(jnp.bfloat16)
                both = jnp.concatenate([high, low], axis=1)
                weights = jnp.concatenate([both, both], axis=0)
                product = jnp.dot(split_ref[k], weights, preferred_element_type=jnp.float32)
                lanes = pl.ds(pl.multiple_of(column * width, width), width)
                out_ref[:, lanes] += product[:, :width] + product[:, width:]

        return carry

    lax.fori_loop(0, targets, add, 0)


def contract(pieces, positions, parts, residual):
    rows = residual.shape[0]
    targets, _, width = parts[0].shape
    vmem = pl.BlockSpec(memory_space=pltpu.VMEM)
    return pl.pallas_call(
        functools.partial(contract_kernel, positions, len(parts)),
        out_shape=jax.ShapeDtypeStruct(residual.shape, jnp.float32),
        in_specs=[vmem] * (len(pieces) + len(parts) + 1),
        out_specs=vmem,
        scratch_shapes=[
            pltpu.VMEM((KT, rows, 2 * width), jnp.bfloat16),
            pltpu.SMEM((targets, META, width), jnp.float32),
            pltpu.SemaphoreType.DMA,
        ],
        compiler_params=pltpu.CompilerParams(vmem_limit_bytes=40 * 1024 * 1024),
    )(*pieces, *parts, residual)


def send(x, axis, partner):
    size = lax.axis_size(axis)
    return lax.ppermute(x, axis, [(i, partner(i)) for i in range(size)])


def gather(block, axis):
    size = lax.axis_size(axis)
    held, at = block[None], [0]
    bit = size // 2
    while bit > 2:
        come = send(held, axis, lambda i, b=bit: i ^ b)
        if bit > 4:
            held, at = jnp.concatenate([held, come], axis=0), at + [p ^ bit for p in at]
        else:
            late, late_at = come, [p ^ bit for p in at]
        bit //= 2
    out, out_at = [], []
    for part, part_at, first, second in ((held, at, 2, 1), (late, late_at, 1, 2)):
        come = send(part, axis, lambda i: i ^ first)
        whole, whole_at = jnp.concatenate([part, come], axis=0), part_at + [p ^ first for p in part_at]
        out += [whole, send(whole, axis, lambda i: i ^ second)]
        out_at += [tuple(whole_at), tuple(p ^ second for p in whole_at)]
    return out, out_at


def local(residual_in, amplitudes, integral_tiles, tile_reader, tile_k, tile_column):
    targets = lax.axis_size("bulk")
    rows_axis = lax.axis_size("row")
    width = integral_tiles.shape[2]
    outgoing = pack(integral_tiles, tile_reader, tile_k, tile_column, targets)
    pieces, positions = gather(amplitudes, "bulk")
    arrived = lax.all_to_all(outgoing, "bulk", split_axis=0, concat_axis=0, tiled=True)
    parts = [arrived]
    for q in range(1, rows_axis):
        parts.append(send(arrived, "row", lambda i: (i + q) % rows_axis))
    if amplitudes.shape[1] != width:
        stacked = jnp.concatenate(pieces, axis=0)
        order = [p for held in positions for p in held]
        place = jnp.asarray([order.index(p) for p in range(targets)], jnp.int32)
        wanted = jnp.bitwise_xor(jnp.arange(targets, dtype=jnp.int32), lax.axis_index("bulk"))
        stacked = stacked[place[wanted]]
        stacked = stacked.transpose(1, 0, 2).reshape(amplitudes.shape[0], KT, width).transpose(1, 0, 2)
        pieces, positions = [stacked], [(None,) * KT]
    return contract(pieces, positions, parts, residual_in)


def solution(mesh):
    placed = (
        P("row", "bulk"),
        P("row", "bulk"),
        P("bulk", "row", None),
        P("bulk", None),
        P("bulk"),
        P("bulk"),
    )
    return jax.shard_map(
        local, mesh=mesh, in_specs=placed, out_specs=P("row", "bulk"), check_vma=False
    )
```

```python
import functools

import jax
import jax.numpy as jnp
from jax import lax
from jax.experimental import pallas as pl
from jax.experimental.pallas import tpu as pltpu
from jax.sharding import PartitionSpec as P

KT = 16
CT = 8
SLOT = 2
GROUPS = 4
META = 8


def pack_kernel(reader_ref, k_ref, column_ref, tiles_ref, out_ref, count_ref):
    count, height, _ = tiles_ref.shape
    targets = out_ref.shape[0]
    me = lax.axis_index("bulk")
    out_ref[:, SLOT * height :, :] = jnp.full((targets, META, out_ref.shape[2]), -1.0, jnp.float32)
    for target in range(targets):
        count_ref[target] = 0
    lane = lax.broadcasted_iota(jnp.int32, (META, out_ref.shape[2]), 1)

    def place(j, carry):
        target = jnp.bitwise_xor(reader_ref[j, 0], me)
        slot = count_ref[target]
        count_ref[target] = slot + 1
        out_ref[target, pl.ds(pl.multiple_of(slot * height, height), height), :] = tiles_ref[j]
        code = (k_ref[j] * CT + column_ref[j]).astype(jnp.float32)
        codes = out_ref[target, SLOT * height :, :]
        out_ref[target, SLOT * height :, :] = jnp.where(lane == slot, code, codes)
        return carry

    lax.fori_loop(0, count, place, 0)


def pack(tiles, readers, tile_k, tile_column, targets):
    _, height, width = tiles.shape
    smem = pl.BlockSpec(memory_space=pltpu.SMEM)
    vmem = pl.BlockSpec(memory_space=pltpu.VMEM)
    return pl.pallas_call(
        pack_kernel,
        out_shape=jax.ShapeDtypeStruct((targets, SLOT * height + META, width), jnp.float32),
        in_specs=[smem, smem, smem, vmem],
        out_specs=vmem,
        scratch_shapes=[pltpu.SMEM((targets,), jnp.int32)],
        cost_estimate=pl.CostEstimate(flops=0, bytes_accessed=4 * tiles.size * 3, transcendentals=0),
    )(readers, tile_k, tile_column, tiles)


def contract_kernel(positions, groups_count, parts_count, *refs):
    pieces = refs[: len(positions)]
    end = len(positions) + groups_count * parts_count
    groups = [
        refs[len(positions) + g * parts_count : len(positions) + (g + 1) * parts_count]
        for g in range(groups_count)
    ]
    residual_ref, out_ref, split_ref = refs[end : end + 3]
    codes = refs[end + 3 : end + 3 + groups_count]
    sem = refs[-1]
    height = (groups[0][0].shape[1] - META) // SLOT
    width = groups[0][0].shape[2]
    row = lax.axis_index("row")
    me = lax.axis_index("bulk")
    fetches = [
        pltpu.make_async_copy(parts[0].at[:, pl.ds(SLOT * height, META), :], codes[g], sem.at[g])
        for g, parts in enumerate(groups)
    ]
    for fetch in fetches:
        fetch.start()
    for piece, held in zip(pieces, positions):
        for at, position in enumerate(held):
            block = piece[at]
            high = block.astype(jnp.bfloat16)
            low = (block - high.astype(jnp.float32)).astype(jnp.bfloat16)
            k = at if position is None else jnp.bitwise_xor(me, position)
            split_ref[k] = jnp.concatenate([high, low], axis=1)
    out_ref[...] = residual_ref[...]
    for fetch in fetches:
        fetch.wait()

    def add_group(parts, codes_ref):
        def add(owner, carry):
            for slot in range(SLOT):
                code = codes_ref[owner, 0, slot].astype(jnp.int32)

                @pl.when(code >= 0)
                def _():
                    k = code // CT
                    column = code - k * CT
                    ordered = []
                    for place in range(parts_count):
                        piece = parts[0][owner, slot * height : (slot + 1) * height, :]
                        for q in range(1, parts_count):
                            other = parts[q][owner, slot * height : (slot + 1) * height, :]
                            piece = jnp.where(lax.rem(place + q, parts_count) == row, other, piece)
                        ordered.append(piece)
                    tile = jnp.concatenate(ordered, axis=0)
                    high = tile.astype(jnp.bfloat16)
                    low = (tile - high.astype(jnp.float32)).astype(jnp.bfloat16)
                    both = jnp.concatenate([high, low], axis=1)
                    weights = jnp.concatenate([both, both], axis=0)
                    product = jnp.dot(split_ref[k], weights, preferred_element_type=jnp.float32)
                    lanes = pl.ds(pl.multiple_of(column * width, width), width)
                    out_ref[:, lanes] += product[:, :width] + product[:, width:]

            return carry

        lax.fori_loop(0, parts[0].shape[0], add, 0)

    for parts, codes_ref in zip(groups, codes):
        add_group(parts, codes_ref)


def contract(pieces, positions, groups, residual):
    rows = residual.shape[0]
    width = groups[0][0].shape[2]
    vmem = pl.BlockSpec(memory_space=pltpu.VMEM)
    arrays = [*pieces, *[part for parts in groups for part in parts], residual]
    return pl.pallas_call(
        functools.partial(contract_kernel, positions, len(groups), len(groups[0])),
        out_shape=jax.ShapeDtypeStruct(residual.shape, jnp.float32),
        in_specs=[vmem] * len(arrays),
        out_specs=vmem,
        scratch_shapes=[
            pltpu.VMEM((KT, rows, 2 * width), jnp.bfloat16),
            *[pltpu.SMEM((parts[0].shape[0], META, width), jnp.float32) for parts in groups],
            pltpu.SemaphoreType.DMA((len(groups),)),
        ],
        compiler_params=pltpu.CompilerParams(vmem_limit_bytes=40 * 1024 * 1024),
    )(*arrays)


def send(x, axis, partner):
    size = lax.axis_size(axis)
    return lax.ppermute(x, axis, [(i, partner(i)) for i in range(size)])


def gather(block, axis):
    size = lax.axis_size(axis)
    held, at = block[None], [0]
    bit = size // 2
    while bit > 2:
        come = send(held, axis, lambda i, b=bit: i ^ b)
        if bit > 4:
            held, at = jnp.concatenate([held, come], axis=0), at + [p ^ bit for p in at]
        else:
            late, late_at = come, [p ^ bit for p in at]
        bit //= 2
    out, out_at = [], []
    for part, part_at, first, second in ((held, at, 2, 1), (late, late_at, 1, 2)):
        come = send(part, axis, lambda i: i ^ first)
        whole, whole_at = jnp.concatenate([part, come], axis=0), part_at + [p ^ first for p in part_at]
        out += [whole, send(whole, axis, lambda i: i ^ second)]
        out_at += [tuple(whole_at), tuple(p ^ second for p in whole_at)]
    return out, out_at


def local(residual_in, amplitudes, integral_tiles, tile_reader, tile_k, tile_column):
    targets = lax.axis_size("bulk")
    rows_axis = lax.axis_size("row")
    width = integral_tiles.shape[2]
    outgoing = pack(integral_tiles, tile_reader, tile_k, tile_column, targets)
    pieces, positions = gather(amplitudes, "bulk")
    half = targets // 2
    order = [p for near in range(half) for p in (near + half, near) if p]
    arrived = {0: outgoing[0]}
    for p in order:
        arrived[p] = send(outgoing[p], "bulk", lambda i: i ^ p)
    members = [0] + order
    size = targets // GROUPS
    groups = []
    for g in range(GROUPS):
        mine = jnp.stack([arrived[p] for p in members[g * size : (g + 1) * size]])
        groups.append(
            [mine] + [send(mine, "row", lambda i: (i + q) % rows_axis) for q in range(1, rows_axis)]
        )
    if amplitudes.shape[1] != width:
        stacked = jnp.concatenate(pieces, axis=0)
        listed = [p for held in positions for p in held]
        place = jnp.asarray([listed.index(p) for p in range(targets)], jnp.int32)
        wanted = jnp.bitwise_xor(jnp.arange(targets, dtype=jnp.int32), lax.axis_index("bulk"))
        stacked = stacked[place[wanted]]
        stacked = stacked.transpose(1, 0, 2).reshape(amplitudes.shape[0], KT, width).transpose(1, 0, 2)
        pieces, positions = [stacked], [(None,) * KT]
    return contract(pieces, positions, groups, residual_in)


def solution(mesh):
    placed = (
        P("row", "bulk"),
        P("row", "bulk"),
        P("bulk", "row", None),
        P("bulk", None),
        P("bulk"),
        P("bulk"),
    )
    return jax.shard_map(
        local, mesh=mesh, in_specs=placed, out_specs=P("row", "bulk"), check_vma=False
    )
```

```python
import functools

import jax
import jax.numpy as jnp
from jax import lax
from jax.experimental import pallas as pl
from jax.experimental.pallas import tpu as pltpu
from jax.sharding import PartitionSpec as P

KT = 16
CT = 8
SLOT = 2
META = 8


def pack_kernel(reader_ref, k_ref, column_ref, tiles_ref, after_ref, out_ref, count_ref):
    count, height, _ = tiles_ref.shape
    targets = out_ref.shape[0]
    out_ref[:, SLOT * height :, :] = jnp.full((targets, META, out_ref.shape[2]), -1.0, jnp.float32)
    for target in range(targets):
        count_ref[target] = 0
    lane = lax.broadcasted_iota(jnp.int32, (META, out_ref.shape[2]), 1)

    def place(j, carry):
        target = reader_ref[j]
        slot = count_ref[target]
        count_ref[target] = slot + 1
        out_ref[target, pl.ds(pl.multiple_of(slot * height, height), height), :] = tiles_ref[j]
        code = (k_ref[j] * CT + column_ref[j]).astype(jnp.float32)
        codes = out_ref[target, SLOT * height :, :]
        out_ref[target, SLOT * height :, :] = jnp.where(lane == slot, code, codes)
        return carry

    lax.fori_loop(0, count, place, 0)


def pack(tiles, readers, tile_k, tile_column, targets, after):
    _, height, width = tiles.shape
    smem = pl.BlockSpec(memory_space=pltpu.SMEM)
    vmem = pl.BlockSpec(memory_space=pltpu.VMEM)
    return pl.pallas_call(
        pack_kernel,
        out_shape=jax.ShapeDtypeStruct((targets, SLOT * height + META, width), jnp.float32),
        in_specs=[smem, smem, smem, vmem, pl.BlockSpec(memory_space=pl.ANY)],
        out_specs=vmem,
        scratch_shapes=[pltpu.SMEM((targets,), jnp.int32)],
        cost_estimate=pl.CostEstimate(flops=0, bytes_accessed=4 * tiles.size * 3, transcendentals=0),
    )(readers.reshape(-1), tile_k, tile_column, tiles, after)


def contract_kernel(positions, parts_count, *refs):
    pieces = refs[: len(positions)]
    parts = refs[len(positions) : len(positions) + parts_count]
    residual_ref, out_ref, split_ref, codes_ref, sem = refs[len(positions) + parts_count :]
    targets = parts[0].shape[0]
    height = (parts[0].shape[1] - META) // SLOT
    width = parts[0].shape[2]
    row = lax.axis_index("row")
    me = lax.axis_index("bulk")
    fetch = pltpu.make_async_copy(parts[0].at[:, pl.ds(SLOT * height, META), :], codes_ref, sem)
    fetch.start()
    for piece, held in zip(pieces, positions):
        for at, position in enumerate(held):
            block = piece[at]
            high = block.astype(jnp.bfloat16)
            low = (block - high.astype(jnp.float32)).astype(jnp.bfloat16)
            k = position if position is None else jnp.bitwise_xor(me, position)
            k = at if k is None else k
            split_ref[k] = jnp.concatenate([high, low], axis=1)
    out_ref[...] = residual_ref[...]
    fetch.wait()

    def add(owner, carry):
        for slot in range(SLOT):
            code = codes_ref[owner, 0, slot].astype(jnp.int32)

            @pl.when(code >= 0)
            def _():
                k = code // CT
                column = code - k * CT
                ordered = []
                for place in range(parts_count):
                    piece = parts[0][owner, slot * height : (slot + 1) * height, :]
                    for q in range(1, parts_count):
                        other = parts[q][owner, slot * height : (slot + 1) * height, :]
                        piece = jnp.where(lax.rem(place + q, parts_count) == row, other, piece)
                    ordered.append(piece)
                tile = jnp.concatenate(ordered, axis=0)
                high = tile.astype(jnp.bfloat16)
                low = (tile - high.astype(jnp.float32)).astype(jnp.bfloat16)
                both = jnp.concatenate([high, low], axis=1)
                weights = jnp.concatenate([both, both], axis=0)
                product = jnp.dot(split_ref[k], weights, preferred_element_type=jnp.float32)
                lanes = pl.ds(pl.multiple_of(column * width, width), width)
                out_ref[:, lanes] += product[:, :width] + product[:, width:]

        return carry

    lax.fori_loop(0, targets, add, 0)


def contract(pieces, positions, parts, residual):
    rows = residual.shape[0]
    targets, _, width = parts[0].shape
    vmem = pl.BlockSpec(memory_space=pltpu.VMEM)
    return pl.pallas_call(
        functools.partial(contract_kernel, positions, len(parts)),
        out_shape=jax.ShapeDtypeStruct(residual.shape, jnp.float32),
        in_specs=[vmem] * (len(pieces) + len(parts) + 1),
        out_specs=vmem,
        scratch_shapes=[
            pltpu.VMEM((KT, rows, 2 * width), jnp.bfloat16),
            pltpu.SMEM((targets, META, width), jnp.float32),
            pltpu.SemaphoreType.DMA,
        ],
        compiler_params=pltpu.CompilerParams(vmem_limit_bytes=40 * 1024 * 1024),
    )(*pieces, *parts, residual)


def send(x, axis, partner):
    size = lax.axis_size(axis)
    return lax.ppermute(x, axis, [(i, partner(i)) for i in range(size)])


def gather(block, axis):
    size = lax.axis_size(axis)
    held, at = block[None], [0]
    bit = size // 2
    first_come = None
    while bit > 2:
        come = send(held, axis, lambda i, b=bit: i ^ b)
        first_come = come if first_come is None else first_come
        if bit > 4:
            held, at = jnp.concatenate([held, come], axis=0), at + [p ^ bit for p in at]
        else:
            late, late_at = come, [p ^ bit for p in at]
        bit //= 2
    out, out_at = [], []
    for part, part_at, first, second in ((held, at, 2, 1), (late, late_at, 1, 2)):
        come = send(part, axis, lambda i: i ^ first)
        whole, whole_at = jnp.concatenate([part, come], axis=0), part_at + [p ^ first for p in part_at]
        out += [whole, send(whole, axis, lambda i: i ^ second)]
        out_at += [tuple(whole_at), tuple(p ^ second for p in whole_at)]
    return out, out_at, first_come


def local(residual_in, amplitudes, integral_tiles, tile_reader, tile_k, tile_column):
    targets = lax.axis_size("bulk")
    rows_axis = lax.axis_size("row")
    width = integral_tiles.shape[2]
    pieces, positions, first_come = gather(amplitudes, "bulk")
    outgoing = pack(integral_tiles, tile_reader, tile_k, tile_column, targets, first_come)
    arrived = lax.all_to_all(outgoing, "bulk", split_axis=0, concat_axis=0, tiled=True)
    parts = [arrived]
    for q in range(1, rows_axis):
        parts.append(send(arrived, "row", lambda i: (i + q) % rows_axis))
    if amplitudes.shape[1] != width:
        stacked = jnp.concatenate(pieces, axis=0)
        order = [p for held in positions for p in held]
        place = jnp.asarray([order.index(p) for p in range(targets)], jnp.int32)
        wanted = jnp.bitwise_xor(jnp.arange(targets, dtype=jnp.int32), lax.axis_index("bulk"))
        stacked = stacked[place[wanted]]
        stacked = stacked.transpose(1, 0, 2).reshape(amplitudes.shape[0], KT, width).transpose(1, 0, 2)
        pieces, positions = [stacked], [(None,) * KT]
    return contract(pieces, positions, parts, residual_in)


def solution(mesh):
    placed = (
        P("row", "bulk"),
        P("row", "bulk"),
        P("bulk", "row", None),
        P("bulk", None),
        P("bulk"),
        P("bulk"),
    )
    return jax.shard_map(
        local, mesh=mesh, in_specs=placed, out_specs=P("row", "bulk"), check_vma=False
    )
```

```python
import functools

import jax
import jax.numpy as jnp
from jax import lax
from jax.experimental import pallas as pl
from jax.experimental.pallas import tpu as pltpu
from jax.sharding import PartitionSpec as P

KT = 16
CT = 8
META = 8


def pack_kernel(slot, reader_ref, k_ref, column_ref, tiles_ref, *refs):
    out_ref, count_ref = refs[-2:]
    count, height, width = tiles_ref.shape
    targets = out_ref.shape[0]
    out_ref[:, height:, :] = jnp.full((targets, META, width), -1.0, jnp.float32)
    for target in range(targets):
        count_ref[target] = 0

    def place(j, carry):
        target = reader_ref[j]
        seen = count_ref[target]
        count_ref[target] = seen + 1

        @pl.when(seen == slot)
        def _():
            out_ref[target, :height, :] = tiles_ref[j]
            code = (k_ref[j] * CT + column_ref[j]).astype(jnp.float32)
            out_ref[target, height:, :] = jnp.full((META, width), code, jnp.float32)

        return carry

    lax.fori_loop(0, count, place, 0)


def pack(slot, tiles, readers, tile_k, tile_column, targets, after):
    _, height, width = tiles.shape
    smem = pl.BlockSpec(memory_space=pltpu.SMEM)
    vmem = pl.BlockSpec(memory_space=pltpu.VMEM)
    return pl.pallas_call(
        functools.partial(pack_kernel, slot),
        out_shape=jax.ShapeDtypeStruct((targets, height + META, width), jnp.float32),
        in_specs=[smem, smem, smem, vmem] + [pl.BlockSpec(memory_space=pl.ANY)] * len(after),
        out_specs=vmem,
        scratch_shapes=[pltpu.SMEM((targets,), jnp.int32)],
        cost_estimate=pl.CostEstimate(flops=0, bytes_accessed=4 * tiles.size * 3, transcendentals=0),
    )(readers.reshape(-1), tile_k, tile_column, tiles, *after)


def contract_kernel(positions, groups_count, parts_count, *refs):
    pieces = refs[: len(positions)]
    end = len(positions) + groups_count * parts_count
    groups = [
        refs[len(positions) + g * parts_count : len(positions) + (g + 1) * parts_count]
        for g in range(groups_count)
    ]
    residual_ref, out_ref, split_ref = refs[end : end + 3]
    codes = refs[end + 3 : end + 3 + groups_count]
    sem = refs[-1]
    height = groups[0][0].shape[1] - META
    width = groups[0][0].shape[2]
    row = lax.axis_index("row")
    me = lax.axis_index("bulk")
    fetches = [
        pltpu.make_async_copy(parts[0].at[:, pl.ds(height, META), :], codes[g], sem.at[g])
        for g, parts in enumerate(groups)
    ]
    for fetch in fetches:
        fetch.start()
    for piece, held in zip(pieces, positions):
        for at, position in enumerate(held):
            block = piece[at]
            high = block.astype(jnp.bfloat16)
            low = (block - high.astype(jnp.float32)).astype(jnp.bfloat16)
            k = at if position is None else jnp.bitwise_xor(me, position)
            split_ref[k] = jnp.concatenate([high, low], axis=1)
    out_ref[...] = residual_ref[...]
    for fetch in fetches:
        fetch.wait()

    def add_group(parts, codes_ref):
        def add(owner, carry):
            code = codes_ref[owner, 0, 0].astype(jnp.int32)

            @pl.when(code >= 0)
            def _():
                k = code // CT
                column = code - k * CT
                ordered = []
                for place in range(parts_count):
                    piece = parts[0][owner, :height, :]
                    for q in range(1, parts_count):
                        other = parts[q][owner, :height, :]
                        piece = jnp.where(lax.rem(place + q, parts_count) == row, other, piece)
                    ordered.append(piece)
                tile = jnp.concatenate(ordered, axis=0)
                high = tile.astype(jnp.bfloat16)
                low = (tile - high.astype(jnp.float32)).astype(jnp.bfloat16)
                both = jnp.concatenate([high, low], axis=1)
                weights = jnp.concatenate([both, both], axis=0)
                product = jnp.dot(split_ref[k], weights, preferred_element_type=jnp.float32)
                lanes = pl.ds(pl.multiple_of(column * width, width), width)
                out_ref[:, lanes] += product[:, :width] + product[:, width:]

            return carry

        lax.fori_loop(0, parts[0].shape[0], add, 0)

    for parts, codes_ref in zip(groups, codes):
        add_group(parts, codes_ref)


def contract(pieces, positions, groups, residual):
    rows = residual.shape[0]
    width = groups[0][0].shape[2]
    vmem = pl.BlockSpec(memory_space=pltpu.VMEM)
    arrays = [*pieces, *[part for parts in groups for part in parts], residual]
    return pl.pallas_call(
        functools.partial(contract_kernel, positions, len(groups), len(groups[0])),
        out_shape=jax.ShapeDtypeStruct(residual.shape, jnp.float32),
        in_specs=[vmem] * len(arrays),
        out_specs=vmem,
        scratch_shapes=[
            pltpu.VMEM((KT, rows, 2 * width), jnp.bfloat16),
            *[pltpu.SMEM((parts[0].shape[0], META, width), jnp.float32) for parts in groups],
            pltpu.SemaphoreType.DMA((len(groups),)),
        ],
        compiler_params=pltpu.CompilerParams(vmem_limit_bytes=40 * 1024 * 1024),
    )(*arrays)


def send(x, axis, partner):
    size = lax.axis_size(axis)
    return lax.ppermute(x, axis, [(i, partner(i)) for i in range(size)])


def gather(block, axis):
    held, at = block[None], (0,)
    bit = lax.axis_size(axis) // 2
    while bit > 4:
        come = send(held, axis, lambda i: i ^ bit)
        held, at = jnp.concatenate([held, come], axis=0), at + tuple(p ^ bit for p in at)
        bit //= 2
    hop = lambda x, step: send(x, axis, lambda i: i ^ step)
    pieces = {0: held}
    pieces[4] = hop(held, 4)
    pieces[2] = hop(held, 2)
    pieces[1] = hop(held, 1)
    pieces[5] = hop(pieces[4], 1)
    pieces[6] = hop(pieces[4], 2)
    pieces[3] = hop(pieces[2], 1)
    pieces[7] = hop(pieces[5], 2)
    return list(pieces.values()), [tuple(p ^ step for p in at) for step in pieces], [pieces[step] for step in (4, 2, 1)]


def local(residual_in, amplitudes, integral_tiles, tile_reader, tile_k, tile_column):
    targets = lax.axis_size("bulk")
    rows_axis = lax.axis_size("row")
    width = integral_tiles.shape[2]
    pieces, positions, near = gather(amplitudes, "bulk")
    groups = []
    for slot, after in enumerate(([], near)):
        outgoing = pack(slot, integral_tiles, tile_reader, tile_k, tile_column, targets, after)
        mine = lax.all_to_all(outgoing, "bulk", split_axis=0, concat_axis=0, tiled=True)
        groups.append(
            [mine] + [send(mine, "row", lambda i: (i + q) % rows_axis) for q in range(1, rows_axis)]
        )
    if amplitudes.shape[1] != width:
        stacked = jnp.concatenate(pieces, axis=0)
        listed = [p for held in positions for p in held]
        place = jnp.asarray([listed.index(p) for p in range(targets)], jnp.int32)
        wanted = jnp.bitwise_xor(jnp.arange(targets, dtype=jnp.int32), lax.axis_index("bulk"))
        stacked = stacked[place[wanted]]
        stacked = stacked.transpose(1, 0, 2).reshape(amplitudes.shape[0], KT, width).transpose(1, 0, 2)
        pieces, positions = [stacked], [(None,) * KT]
    return contract(pieces, positions, groups, residual_in)


def solution(mesh):
    placed = (
        P("row", "bulk"),
        P("row", "bulk"),
        P("bulk", "row", None),
        P("bulk", None),
        P("bulk"),
        P("bulk"),
    )
    return jax.shard_map(
        local, mesh=mesh, in_specs=placed, out_specs=P("row", "bulk"), check_vma=False
    )
```

```python
import functools

import jax
import jax.numpy as jnp
from jax import lax
from jax.experimental import pallas as pl
from jax.experimental.pallas import tpu as pltpu
from jax.sharding import PartitionSpec as P

KT = 16
CT = 8
SLOT = 2
GROUPS = 4
META = 8


def pack_kernel(reader_ref, k_ref, column_ref, tiles_ref, *refs):
    out_ref, count_ref = refs[-2:]
    count, height, _ = tiles_ref.shape
    targets = out_ref.shape[0]
    out_ref[:, SLOT * height :, :] = jnp.full((targets, META, out_ref.shape[2]), -1.0, jnp.float32)
    for target in range(targets):
        count_ref[target] = 0
    lane = lax.broadcasted_iota(jnp.int32, (META, out_ref.shape[2]), 1)

    def place(j, carry):
        target = reader_ref[j]
        slot = count_ref[target]
        count_ref[target] = slot + 1
        out_ref[target, pl.ds(pl.multiple_of(slot * height, height), height), :] = tiles_ref[j]
        code = (k_ref[j] * CT + column_ref[j]).astype(jnp.float32)
        codes = out_ref[target, SLOT * height :, :]
        out_ref[target, SLOT * height :, :] = jnp.where(lane == slot, code, codes)
        return carry

    lax.fori_loop(0, count, place, 0)


def pack(tiles, readers, tile_k, tile_column, targets, after):
    _, height, width = tiles.shape
    smem = pl.BlockSpec(memory_space=pltpu.SMEM)
    vmem = pl.BlockSpec(memory_space=pltpu.VMEM)
    return pl.pallas_call(
        pack_kernel,
        out_shape=jax.ShapeDtypeStruct((targets, SLOT * height + META, width), jnp.float32),
        in_specs=[smem, smem, smem, vmem] + [vmem] * len(after),
        out_specs=vmem,
        scratch_shapes=[pltpu.SMEM((targets,), jnp.int32)],
        cost_estimate=pl.CostEstimate(flops=0, bytes_accessed=4 * tiles.size * 3, transcendentals=0),
    )(readers.reshape(-1), tile_k, tile_column, tiles, *after)


def split_kernel(positions, *refs):
    pieces, split_ref = refs[:-1], refs[-1]
    me = lax.axis_index("bulk")
    for piece, held in zip(pieces, positions):
        for at, position in enumerate(held):
            block = piece[at]
            high = block.astype(jnp.bfloat16)
            low = (block - high.astype(jnp.float32)).astype(jnp.bfloat16)
            k = at if position is None else jnp.bitwise_xor(me, position)
            split_ref[k] = jnp.concatenate([high, low], axis=1)


def split(pieces, positions):
    _, rows, width = pieces[0].shape
    vmem = pl.BlockSpec(memory_space=pltpu.VMEM)
    return pl.pallas_call(
        functools.partial(split_kernel, positions),
        out_shape=jax.ShapeDtypeStruct((KT, rows, 2 * width), jnp.bfloat16),
        in_specs=[vmem] * len(pieces),
        out_specs=vmem,
        compiler_params=pltpu.CompilerParams(vmem_limit_bytes=24 * 1024 * 1024),
    )(*pieces)


def contract_kernel(groups_count, parts_count, split_ref, *refs):
    end = groups_count * parts_count
    groups = [refs[g * parts_count : (g + 1) * parts_count] for g in range(groups_count)]
    residual_ref, out_ref = refs[end : end + 2]
    codes = refs[end + 2 : end + 2 + groups_count]
    sem = refs[-1]
    height = (groups[0][0].shape[1] - META) // SLOT
    width = groups[0][0].shape[2]
    row = lax.axis_index("row")
    fetches = [
        pltpu.make_async_copy(parts[0].at[:, pl.ds(SLOT * height, META), :], codes[g], sem.at[g])
        for g, parts in enumerate(groups)
    ]
    for fetch in fetches:
        fetch.start()
    out_ref[...] = residual_ref[...]
    for fetch in fetches:
        fetch.wait()

    def add_group(parts, codes_ref):
        def add(owner, carry):
            for slot in range(SLOT):
                code = codes_ref[owner, 0, slot].astype(jnp.int32)

                @pl.when(code >= 0)
                def _():
                    k = code // CT
                    column = code - k * CT
                    ordered = []
                    for place in range(parts_count):
                        piece = parts[0][owner, slot * height : (slot + 1) * height, :]
                        for q in range(1, parts_count):
                            other = parts[q][owner, slot * height : (slot + 1) * height, :]
                            piece = jnp.where(lax.rem(place + q, parts_count) == row, other, piece)
                        ordered.append(piece)
                    tile = jnp.concatenate(ordered, axis=0)
                    high = tile.astype(jnp.bfloat16)
                    low = (tile - high.astype(jnp.float32)).astype(jnp.bfloat16)
                    both = jnp.concatenate([high, low], axis=1)
                    weights = jnp.concatenate([both, both], axis=0)
                    product = jnp.dot(split_ref[k], weights, preferred_element_type=jnp.float32)
                    lanes = pl.ds(pl.multiple_of(column * width, width), width)
                    out_ref[:, lanes] += product[:, :width] + product[:, width:]

            return carry

        lax.fori_loop(0, parts[0].shape[0], add, 0)

    for parts, codes_ref in zip(groups, codes):
        add_group(parts, codes_ref)


def contract(split_amplitudes, groups, residual):
    width = groups[0][0].shape[2]
    vmem = pl.BlockSpec(memory_space=pltpu.VMEM)
    arrays = [split_amplitudes, *[part for parts in groups for part in parts], residual]
    return pl.pallas_call(
        functools.partial(contract_kernel, len(groups), len(groups[0])),
        out_shape=jax.ShapeDtypeStruct(residual.shape, jnp.float32),
        in_specs=[vmem] * len(arrays),
        out_specs=vmem,
        scratch_shapes=[
            *[pltpu.SMEM((parts[0].shape[0], META, width), jnp.float32) for parts in groups],
            pltpu.SemaphoreType.DMA((len(groups),)),
        ],
        compiler_params=pltpu.CompilerParams(vmem_limit_bytes=40 * 1024 * 1024),
    )(*arrays)


def send(x, axis, partner):
    size = lax.axis_size(axis)
    return lax.ppermute(x, axis, [(i, partner(i)) for i in range(size)])


def gather(block, axis):
    own = block[None]
    hop = lambda x, step: send(x, axis, lambda i: i ^ step)
    far_at = tuple(range(4, lax.axis_size(axis), 4))
    come = [hop(own, p) for p in far_at]
    pieces = [(own, (0,)), (hop(own, 1), (1,)), (hop(own, 2), (2,))]
    far = jnp.concatenate(come, axis=0)
    far_one, far_two = hop(far, 1), hop(far, 2)
    cut = 2 * len(far_at) // 3
    pieces += [
        (hop(pieces[2][0], 1), (3,)),
        (far, far_at),
        (far_one, tuple(p + 1 for p in far_at)),
        (far_two, tuple(p + 2 for p in far_at)),
        (hop(far_one[:cut], 2), tuple(p + 3 for p in far_at[:cut])),
        (hop(far_two[cut:], 1), tuple(p + 3 for p in far_at[cut:])),
    ]
    return [piece for piece, _ in pieces], [held for _, held in pieces], come


def local(residual_in, amplitudes, integral_tiles, tile_reader, tile_k, tile_column):
    targets = lax.axis_size("bulk")
    rows_axis = lax.axis_size("row")
    width = integral_tiles.shape[2]
    pieces, positions, far = gather(amplitudes, "bulk")
    outgoing = pack(integral_tiles, tile_reader, tile_k, tile_column, targets, far)
    arrived = lax.all_to_all(outgoing, "bulk", split_axis=0, concat_axis=0, tiled=True)
    size = targets // GROUPS
    groups = []
    for g in range(GROUPS):
        mine = arrived[g * size : (g + 1) * size]
        groups.append(
            [mine] + [send(mine, "row", lambda i: (i + q) % rows_axis) for q in range(1, rows_axis)]
        )
    if amplitudes.shape[1] != width:
        stacked = jnp.concatenate(pieces, axis=0)
        listed = [p for held in positions for p in held]
        place = jnp.asarray([listed.index(p) for p in range(targets)], jnp.int32)
        wanted = jnp.bitwise_xor(jnp.arange(targets, dtype=jnp.int32), lax.axis_index("bulk"))
        stacked = stacked[place[wanted]]
        stacked = stacked.transpose(1, 0, 2).reshape(amplitudes.shape[0], KT, width).transpose(1, 0, 2)
        pieces, positions = [stacked], [(None,) * KT]
    return contract(split(pieces, positions), groups, residual_in)


def solution(mesh):
    placed = (
        P("row", "bulk"),
        P("row", "bulk"),
        P("bulk", "row", None),
        P("bulk", None),
        P("bulk"),
        P("bulk"),
    )
    return jax.shard_map(
        local, mesh=mesh, in_specs=placed, out_specs=P("row", "bulk"), check_vma=False
    )
```

```python
import functools

import jax
import jax.numpy as jnp
from jax import lax
from jax.experimental import pallas as pl
from jax.experimental.pallas import tpu as pltpu
from jax.sharding import PartitionSpec as P

KT = 16
CT = 8
SLOT = 2
GROUPS = 4
META = 8


def pack_kernel(reader_ref, k_ref, column_ref, tiles_ref, *refs):
    outs, count_ref = refs[:-1], refs[-1]
    count, height, width = tiles_ref.shape
    half = outs[0].shape[0] // 2
    targets = 8 * half
    me = lax.axis_index("bulk")
    for out_ref in outs:
        out_ref[:, SLOT * height :, :] = jnp.full((2 * half, META, width), -1.0, jnp.float32)
    for target in range(targets):
        count_ref[target] = 0
    lane = lax.broadcasted_iota(jnp.int32, (META, width), 1)

    def place(j, carry):
        position = jnp.bitwise_xor(reader_ref[j], me)
        slot = count_ref[position]
        count_ref[position] = slot + 1
        code = (k_ref[j] * CT + column_ref[j]).astype(jnp.float32)
        x, y, z = position % 2, position // 2 % 2, position // 4
        far = z >= half
        first, second = jnp.where(far, y, x), jnp.where(far, x, y)
        which = 2 * far.astype(jnp.int32) + first
        at = second * half + jnp.where(far, z - half, z)
        for number, out_ref in enumerate(outs):

            @pl.when(which == number)
            def _():
                out_ref[at, pl.ds(pl.multiple_of(slot * height, height), height), :] = tiles_ref[j]
                codes = out_ref[at, SLOT * height :, :]
                out_ref[at, SLOT * height :, :] = jnp.where(lane == slot, code, codes)

        return carry

    lax.fori_loop(0, count, place, 0)


def pack(tiles, readers, tile_k, tile_column, targets):
    _, height, width = tiles.shape
    smem = pl.BlockSpec(memory_space=pltpu.SMEM)
    vmem = pl.BlockSpec(memory_space=pltpu.VMEM)
    out = jax.ShapeDtypeStruct((targets // 4, SLOT * height + META, width), jnp.float32)
    return pl.pallas_call(
        pack_kernel,
        out_shape=[out] * 4,
        in_specs=[smem, smem, smem, vmem],
        out_specs=[vmem] * 4,
        scratch_shapes=[pltpu.SMEM((targets,), jnp.int32)],
        cost_estimate=pl.CostEstimate(flops=0, bytes_accessed=4 * tiles.size * 3, transcendentals=0),
    )(readers.reshape(-1), tile_k, tile_column, tiles)


def split_kernel(positions, *refs):
    pieces, split_ref = refs[:-1], refs[-1]
    me = lax.axis_index("bulk")
    for piece, held in zip(pieces, positions):
        for at, position in enumerate(held):
            block = piece[at]
            high = block.astype(jnp.bfloat16)
            low = (block - high.astype(jnp.float32)).astype(jnp.bfloat16)
            k = at if position is None else jnp.bitwise_xor(me, position)
            split_ref[k] = jnp.concatenate([high, low], axis=1)


def split(pieces, positions):
    _, rows, width = pieces[0].shape
    vmem = pl.BlockSpec(memory_space=pltpu.VMEM)
    return pl.pallas_call(
        functools.partial(split_kernel, positions),
        out_shape=jax.ShapeDtypeStruct((KT, rows, 2 * width), jnp.bfloat16),
        in_specs=[vmem] * len(pieces),
        out_specs=vmem,
        compiler_params=pltpu.CompilerParams(vmem_limit_bytes=24 * 1024 * 1024),
    )(*pieces)


def contract_kernel(groups_count, parts_count, split_ref, *refs):
    end = groups_count * parts_count
    groups = [refs[g * parts_count : (g + 1) * parts_count] for g in range(groups_count)]
    residual_ref, out_ref = refs[end : end + 2]
    codes = refs[end + 2 : end + 2 + groups_count]
    sem = refs[-1]
    height = (groups[0][0].shape[1] - META) // SLOT
    width = groups[0][0].shape[2]
    row = lax.axis_index("row")
    fetches = [
        pltpu.make_async_copy(parts[0].at[:, pl.ds(SLOT * height, META), :], codes[g], sem.at[g])
        for g, parts in enumerate(groups)
    ]
    for fetch in fetches:
        fetch.start()
    out_ref[...] = residual_ref[...]
    for fetch in fetches:
        fetch.wait()

    def add_group(parts, codes_ref):
        def add(owner, carry):
            for slot in range(SLOT):
                code = codes_ref[owner, 0, slot].astype(jnp.int32)

                @pl.when(code >= 0)
                def _():
                    k = code // CT
                    column = code - k * CT
                    ordered = []
                    for place in range(parts_count):
                        piece = parts[0][owner, slot * height : (slot + 1) * height, :]
                        for q in range(1, parts_count):
                            other = parts[q][owner, slot * height : (slot + 1) * height, :]
                            piece = jnp.where(lax.rem(place + q, parts_count) == row, other, piece)
                        ordered.append(piece)
                    tile = jnp.concatenate(ordered, axis=0)
                    high = tile.astype(jnp.bfloat16)
                    low = (tile - high.astype(jnp.float32)).astype(jnp.bfloat16)
                    both = jnp.concatenate([high, low], axis=1)
                    weights = jnp.concatenate([both, both], axis=0)
                    product = jnp.dot(split_ref[k], weights, preferred_element_type=jnp.float32)
                    lanes = pl.ds(pl.multiple_of(column * width, width), width)
                    out_ref[:, lanes] += product[:, :width] + product[:, width:]

            return carry

        lax.fori_loop(0, parts[0].shape[0], add, 0)

    for parts, codes_ref in zip(groups, codes):
        add_group(parts, codes_ref)


def contract(split_amplitudes, groups, residual):
    width = groups[0][0].shape[2]
    vmem = pl.BlockSpec(memory_space=pltpu.VMEM)
    arrays = [split_amplitudes, *[part for parts in groups for part in parts], residual]
    return pl.pallas_call(
        functools.partial(contract_kernel, len(groups), len(groups[0])),
        out_shape=jax.ShapeDtypeStruct(residual.shape, jnp.float32),
        in_specs=[vmem] * len(arrays),
        out_specs=vmem,
        scratch_shapes=[
            *[pltpu.SMEM((parts[0].shape[0], META, width), jnp.float32) for parts in groups],
            pltpu.SemaphoreType.DMA((len(groups),)),
        ],
        compiler_params=pltpu.CompilerParams(vmem_limit_bytes=40 * 1024 * 1024),
    )(*arrays)


def send(x, axis, partner):
    size = lax.axis_size(axis)
    return lax.ppermute(x, axis, [(i, partner(i)) for i in range(size)])


def hop(x, step):
    return send(x, "bulk", lambda i: i ^ step)


def gather(block, size):
    held, at = block[None], (0,)
    bit = size // 2
    while bit > 4:
        held, at = jnp.concatenate([held, hop(held, bit)], axis=0), at + tuple(p ^ bit for p in at)
        bit //= 2
    late, late_at = hop(held, 4), tuple(p ^ 4 for p in at)
    out, out_at = [], []
    for part, part_at, first, second in ((held, at, 2, 1), (late, late_at, 1, 2)):
        whole = jnp.concatenate([part, hop(part, first)], axis=0)
        whole_at = part_at + tuple(p ^ first for p in part_at)
        out += [whole, hop(whole, second)]
        out_at += [whole_at, tuple(p ^ second for p in whole_at)]
    return out, out_at


def across(kept, sent, first, second):
    half = kept.shape[0] // 2
    come = hop(sent, first)
    last = hop(jnp.concatenate([kept[half:], come[half:]], axis=0), second)
    return [jnp.stack([kept[z], come[z], last[z], last[half + z]]) for z in range(half)]


def local(residual_in, amplitudes, integral_tiles, tile_reader, tile_k, tile_column):
    targets = lax.axis_size("bulk")
    rows_axis = lax.axis_size("row")
    width = integral_tiles.shape[2]
    pieces, positions = gather(amplitudes, targets)
    near_kept, near_sent, far_kept, far_sent = pack(
        integral_tiles, tile_reader, tile_k, tile_column, targets
    )
    far = across(far_kept, far_sent, 2, 1)
    near = across(near_kept, near_sent, 1, 2)
    planes = near + far
    planes = [planes[0]] + [hop(plane, 4 * z) for z, plane in enumerate(planes) if z]
    size = len(planes) // GROUPS
    groups = []
    for g in range(GROUPS):
        mine = jnp.concatenate(planes[g * size : (g + 1) * size], axis=0)
        groups.append(
            [mine] + [send(mine, "row", lambda i: (i + q) % rows_axis) for q in range(1, rows_axis)]
        )
    if amplitudes.shape[1] != width:
        stacked = jnp.concatenate(pieces, axis=0)
        listed = [p for held in positions for p in held]
        place = jnp.asarray([listed.index(p) for p in range(targets)], jnp.int32)
        wanted = jnp.bitwise_xor(jnp.arange(targets, dtype=jnp.int32), lax.axis_index("bulk"))
        stacked = stacked[place[wanted]]
        stacked = stacked.transpose(1, 0, 2).reshape(amplitudes.shape[0], KT, width).transpose(1, 0, 2)
        pieces, positions = [stacked], [(None,) * KT]
    return contract(split(pieces, positions), groups, residual_in)


def solution(mesh):
    placed = (
        P("row", "bulk"),
        P("row", "bulk"),
        P("bulk", "row", None),
        P("bulk", None),
        P("bulk"),
        P("bulk"),
    )
    return jax.shard_map(
        local, mesh=mesh, in_specs=placed, out_specs=P("row", "bulk"), check_vma=False
    )
```

```python
import functools

import jax
import jax.numpy as jnp
from jax import lax
from jax.experimental import pallas as pl
from jax.experimental.pallas import tpu as pltpu
from jax.sharding import PartitionSpec as P

KT = 16
CT = 8
SLOT = 2
GROUPS = 4
META = 8


def pack_kernel(reader_ref, k_ref, column_ref, tiles_ref, block_ref, *refs):
    copy_ref, outs, count_ref = refs[0], refs[1:-1], refs[-1]
    copy_ref[0] = block_ref[...]
    count, height, width = tiles_ref.shape
    half = outs[0].shape[0] // 2
    targets = 8 * half
    me = lax.axis_index("bulk")
    for out_ref in outs:
        out_ref[:, SLOT * height :, :] = jnp.full((2 * half, META, width), -1.0, jnp.float32)
    for target in range(targets):
        count_ref[target] = 0
    lane = lax.broadcasted_iota(jnp.int32, (META, width), 1)

    def place(j, carry):
        position = jnp.bitwise_xor(reader_ref[j], me)
        slot = count_ref[position]
        count_ref[position] = slot + 1
        code = (k_ref[j] * CT + column_ref[j]).astype(jnp.float32)
        x, y, z = position % 2, position // 2 % 2, position // 4
        odd = z % 2
        first, second = jnp.where(odd == 1, y, x), jnp.where(odd == 1, x, y)
        which = 2 * odd + first
        at = second * half + z // 2
        for number, out_ref in enumerate(outs):

            @pl.when(which == number)
            def _():
                out_ref[at, pl.ds(pl.multiple_of(slot * height, height), height), :] = tiles_ref[j]
                codes = out_ref[at, SLOT * height :, :]
                out_ref[at, SLOT * height :, :] = jnp.where(lane == slot, code, codes)

        return carry

    lax.fori_loop(0, count, place, 0)


def pack(tiles, readers, tile_k, tile_column, block, targets):
    _, height, width = tiles.shape
    smem = pl.BlockSpec(memory_space=pltpu.SMEM)
    vmem = pl.BlockSpec(memory_space=pltpu.VMEM)
    out = jax.ShapeDtypeStruct((targets // 4, SLOT * height + META, width), jnp.float32)
    return pl.pallas_call(
        pack_kernel,
        out_shape=[jax.ShapeDtypeStruct((1, *block.shape), block.dtype)] + [out] * 4,
        in_specs=[smem, smem, smem, vmem, vmem],
        out_specs=[vmem] * 5,
        scratch_shapes=[pltpu.SMEM((targets,), jnp.int32)],
        cost_estimate=pl.CostEstimate(flops=0, bytes_accessed=4 * tiles.size * 3, transcendentals=0),
        compiler_params=pltpu.CompilerParams(vmem_limit_bytes=8 * 1024 * 1024),
    )(readers.reshape(-1), tile_k, tile_column, tiles, block)


def split_kernel(positions, *refs):
    pieces, split_ref = refs[:-1], refs[-1]
    me = lax.axis_index("bulk")
    for piece, held in zip(pieces, positions):
        for at, position in enumerate(held):
            block = piece[at]
            high = block.astype(jnp.bfloat16)
            low = (block - high.astype(jnp.float32)).astype(jnp.bfloat16)
            k = at if position is None else jnp.bitwise_xor(me, position)
            split_ref[k] = jnp.concatenate([high, low], axis=1)


def split(pieces, positions):
    _, rows, width = pieces[0].shape
    vmem = pl.BlockSpec(memory_space=pltpu.VMEM)
    return pl.pallas_call(
        functools.partial(split_kernel, positions),
        out_shape=jax.ShapeDtypeStruct((KT, rows, 2 * width), jnp.bfloat16),
        in_specs=[vmem] * len(pieces),
        out_specs=vmem,
        compiler_params=pltpu.CompilerParams(vmem_limit_bytes=16 * 1024 * 1024),
    )(*pieces)


def contract_kernel(groups_count, parts_count, split_ref, *refs):
    end = groups_count * parts_count
    groups = [refs[g * parts_count : (g + 1) * parts_count] for g in range(groups_count)]
    residual_ref, out_ref = refs[end : end + 2]
    codes = refs[end + 2 : end + 2 + groups_count]
    sem = refs[-1]
    height = (groups[0][0].shape[1] - META) // SLOT
    width = groups[0][0].shape[2]
    row = lax.axis_index("row")
    fetches = [
        pltpu.make_async_copy(parts[0].at[:, pl.ds(SLOT * height, META), :], codes[g], sem.at[g])
        for g, parts in enumerate(groups)
    ]
    for fetch in fetches:
        fetch.start()
    out_ref[...] = residual_ref[...]
    for fetch in fetches:
        fetch.wait()

    def whole(parts, owner, slot, code):
        k = code // CT
        column = code - k * CT
        ordered = []
        for place in range(parts_count):
            piece = parts[0][owner, slot * height : (slot + 1) * height, :]
            for q in range(1, parts_count):
                other = parts[q][owner, slot * height : (slot + 1) * height, :]
                piece = jnp.where(lax.rem(place + q, parts_count) == row, other, piece)
            ordered.append(piece)
        return jnp.concatenate(ordered, axis=0), k, column

    def multiply(tile, k, column):
        high = tile.astype(jnp.bfloat16)
        low = (tile - high.astype(jnp.float32)).astype(jnp.bfloat16)
        both = jnp.concatenate([high, low], axis=1)
        weights = jnp.concatenate([both, both], axis=0)
        product = jnp.dot(split_ref[k], weights, preferred_element_type=jnp.float32)
        lanes = pl.ds(pl.multiple_of(column * width, width), width)
        out_ref[:, lanes] += product[:, :width] + product[:, width:]

    def add_group(parts, codes_ref):
        owners = parts[0].shape[0]

        def first(owner):
            code = codes_ref[owner, 0, 0].astype(jnp.int32)
            tile, k, column = whole(parts, owner, 0, jnp.maximum(code, 0))
            multiply(jnp.where(code >= 0, tile, 0.0), k, column)

        def later(owner, slot):
            code = codes_ref[owner, 0, slot].astype(jnp.int32)

            @pl.when(code >= 0)
            def _():
                multiply(*whole(parts, owner, slot, code))

        def four(step, carry):
            for i in range(4):
                first(4 * step + i)
            for i in range(4):
                for slot in range(1, SLOT):
                    later(4 * step + i, slot)
            return carry

        lax.fori_loop(0, owners // 4, four, 0)

    for parts, codes_ref in zip(groups, codes):
        add_group(parts, codes_ref)


def contract(split_amplitudes, groups, residual):
    width = groups[0][0].shape[2]
    vmem = pl.BlockSpec(memory_space=pltpu.VMEM)
    arrays = [split_amplitudes, *[part for parts in groups for part in parts], residual]
    return pl.pallas_call(
        functools.partial(contract_kernel, len(groups), len(groups[0])),
        out_shape=jax.ShapeDtypeStruct(residual.shape, jnp.float32),
        in_specs=[vmem] * len(arrays),
        out_specs=vmem,
        scratch_shapes=[
            *[pltpu.SMEM((parts[0].shape[0], META, width), jnp.float32) for parts in groups],
            pltpu.SemaphoreType.DMA((len(groups),)),
        ],
        compiler_params=pltpu.CompilerParams(vmem_limit_bytes=24 * 1024 * 1024),
    )(*arrays)


def send(x, axis, partner):
    size = lax.axis_size(axis)
    return lax.ppermute(x, axis, [(i, partner(i)) for i in range(size)])


def hop(x, step):
    return send(x, "bulk", lambda i: i ^ step)


def gather(block, size):
    held, at = block, (0,)
    bit = size // 2
    while bit > 2:
        held, at = jnp.concatenate([held, hop(held, bit)], axis=0), at + tuple(p ^ bit for p in at)
        bit //= 2
    over_x, over_y = hop(held, 1), hop(held, 2)
    cut = len(at) // 2
    pieces = [held, over_x, over_y, hop(over_x[:cut], 2), hop(over_y[cut:], 1)]
    positions = [at] + [tuple(p ^ step for p in at) for step in (1, 2)]
    positions += [tuple(p ^ 3 for p in at[:cut]), tuple(p ^ 3 for p in at[cut:])]
    return pieces, positions


def across(kept, sent, first, second):
    half = kept.shape[0] // 2
    come = hop(sent, first)
    last = hop(jnp.concatenate([kept[half:], come[half:]], axis=0), second)
    return [jnp.stack([kept[z], come[z], last[z], last[half + z]]) for z in range(half)]


def local(residual_in, amplitudes, integral_tiles, tile_reader, tile_k, tile_column):
    targets = lax.axis_size("bulk")
    rows_axis = lax.axis_size("row")
    width = integral_tiles.shape[2]
    block, even_kept, even_sent, odd_kept, odd_sent = pack(
        integral_tiles, tile_reader, tile_k, tile_column, amplitudes, targets
    )
    pieces, positions = gather(block, targets)
    odd = across(odd_kept, odd_sent, 2, 1)
    even = across(even_kept, even_sent, 1, 2)
    planes = [plane for pair in zip(even, odd) for plane in pair]
    planes = [planes[0]] + [hop(plane, 4 * z) for z, plane in enumerate(planes) if z]
    size = len(planes) // GROUPS
    groups = []
    for g in range(GROUPS):
        mine = jnp.concatenate(planes[g * size : (g + 1) * size], axis=0)
        groups.append(
            [mine] + [send(mine, "row", lambda i: (i + q) % rows_axis) for q in range(1, rows_axis)]
        )
    if amplitudes.shape[1] != width:
        stacked = jnp.concatenate(pieces, axis=0)
        listed = [p for held in positions for p in held]
        place = jnp.asarray([listed.index(p) for p in range(targets)], jnp.int32)
        wanted = jnp.bitwise_xor(jnp.arange(targets, dtype=jnp.int32), lax.axis_index("bulk"))
        stacked = stacked[place[wanted]]
        stacked = stacked.transpose(1, 0, 2).reshape(amplitudes.shape[0], KT, width).transpose(1, 0, 2)
        pieces, positions = [stacked], [(None,) * KT]
    return contract(split(pieces, positions), groups, residual_in)


def solution(mesh):
    placed = (
        P("row", "bulk"),
        P("row", "bulk"),
        P("bulk", "row", None),
        P("bulk", None),
        P("bulk"),
        P("bulk"),
    )
    return jax.shard_map(
        local, mesh=mesh, in_specs=placed, out_specs=P("row", "bulk"), check_vma=False
    )
```

```python
import functools

import jax
import jax.numpy as jnp
from jax import lax
from jax.experimental import pallas as pl
from jax.experimental.pallas import tpu as pltpu
from jax.sharding import PartitionSpec as P

KT = 16
CT = 8
SLOT = 2
HINT = 32 * 1024 * 1024
META = 8


def pack_kernel(reader_any, k_any, column_any, tiles_any, *refs):
    outs = refs[:4]
    reader_ref, k_ref, column_ref, tiles_ref, count_ref, sem = refs[4:]
    fetches = [
        pltpu.make_async_copy(*pair, sem.at[number])
        for number, pair in enumerate(
            (
                (tiles_any, tiles_ref),
                (reader_any, reader_ref),
                (k_any, k_ref),
                (column_any, column_ref),
            )
        )
    ]
    for fetch in fetches:
        fetch.start()
    count, height, width = tiles_ref.shape
    half = outs[0].shape[0] // 2
    targets = 8 * half
    me = lax.axis_index("bulk")
    for out_ref in outs:
        out_ref[:, SLOT * height :, :] = jnp.full((2 * half, META, width), -1.0, jnp.float32)
    for target in range(targets):
        count_ref[target] = 0
    lane = lax.broadcasted_iota(jnp.int32, (META, width), 1)
    for fetch in fetches:
        fetch.wait()

    def place(j, carry):
        position = jnp.bitwise_xor(reader_ref[j], me)
        slot = count_ref[position]
        count_ref[position] = slot + 1
        code = (k_ref[j] * CT + column_ref[j]).astype(jnp.float32)
        x, y, z = position % 2, position // 2 % 2, position // 4
        odd = z % 2
        first, second = jnp.where(odd == 1, y, x), jnp.where(odd == 1, x, y)
        which = 2 * odd + first
        at = second * half + z // 2
        for number, out_ref in enumerate(outs):

            @pl.when(which == number)
            def _():
                out_ref[at, pl.ds(pl.multiple_of(slot * height, height), height), :] = tiles_ref[j]
                codes = out_ref[at, SLOT * height :, :]
                out_ref[at, SLOT * height :, :] = jnp.where(lane == slot, code, codes)

        return carry

    lax.fori_loop(0, count, place, 0)


def pack(tiles, readers, tile_k, tile_column, targets):
    count, height, width = tiles.shape
    out = jax.ShapeDtypeStruct((targets // 4, SLOT * height + META, width), jnp.float32)
    return pl.pallas_call(
        pack_kernel,
        out_shape=[out] * 4,
        in_specs=[pl.BlockSpec(memory_space=pltpu.HBM)] * 4,
        out_specs=[pl.BlockSpec(memory_space=pltpu.VMEM)] * 4,
        scratch_shapes=[
            *[pltpu.SMEM((count,), jnp.int32)] * 3,
            pltpu.VMEM(tiles.shape, tiles.dtype),
            pltpu.SMEM((targets,), jnp.int32),
            pltpu.SemaphoreType.DMA((4,)),
        ],
        cost_estimate=pl.CostEstimate(flops=0, bytes_accessed=4 * tiles.size * 3, transcendentals=0),
        compiler_params=pltpu.CompilerParams(vmem_limit_bytes=8 * 1024 * 1024),
    )(readers.reshape(-1), tile_k, tile_column, tiles)


def split_kernel(positions, *refs):
    pieces, split_ref = refs[:-1], refs[-1]
    me = lax.axis_index("bulk")
    for piece, held in zip(pieces, positions):
        for at, position in enumerate(held):
            block = piece[at]
            high = block.astype(jnp.bfloat16)
            low = (block - high.astype(jnp.float32)).astype(jnp.bfloat16)
            k = at if position is None else jnp.bitwise_xor(me, position)
            split_ref[k] = jnp.concatenate([high, low], axis=1)


def split(pieces, positions):
    _, rows, width = pieces[0].shape
    vmem = pl.BlockSpec(memory_space=pltpu.VMEM)
    return pl.pallas_call(
        functools.partial(split_kernel, positions),
        out_shape=jax.ShapeDtypeStruct((KT, rows, 2 * width), jnp.bfloat16),
        in_specs=[vmem] * len(pieces),
        out_specs=vmem,
        cost_estimate=pl.CostEstimate(flops=0, bytes_accessed=HINT, transcendentals=0),
        compiler_params=pltpu.CompilerParams(vmem_limit_bytes=16 * 1024 * 1024),
    )(*pieces)


def contract_kernel(groups_count, parts_count, split_ref, *refs):
    end = groups_count * parts_count
    groups = [refs[g * parts_count : (g + 1) * parts_count] for g in range(groups_count)]
    residual_ref, out_ref = refs[end : end + 2]
    codes = refs[end + 2 : end + 2 + groups_count]
    sem = refs[-1]
    height = (groups[0][0].shape[1] - META) // SLOT
    width = groups[0][0].shape[2]
    row = lax.axis_index("row")
    fetches = [
        pltpu.make_async_copy(parts[0].at[:, pl.ds(SLOT * height, META), :], codes[g], sem.at[g])
        for g, parts in enumerate(groups)
    ]
    for fetch in fetches:
        fetch.start()
    out_ref[...] = residual_ref[...]
    for fetch in fetches:
        fetch.wait()

    def whole(parts, owner, slot, code):
        k = code // CT
        column = code - k * CT
        ordered = []
        for place in range(parts_count):
            piece = parts[0][owner, slot * height : (slot + 1) * height, :]
            for q in range(1, parts_count):
                other = parts[q][owner, slot * height : (slot + 1) * height, :]
                piece = jnp.where(lax.rem(place + q, parts_count) == row, other, piece)
            ordered.append(piece)
        return jnp.concatenate(ordered, axis=0), k, column

    def multiply(tile, k, column):
        high = tile.astype(jnp.bfloat16)
        low = (tile - high.astype(jnp.float32)).astype(jnp.bfloat16)
        both = jnp.concatenate([high, low], axis=1)
        weights = jnp.concatenate([both, both], axis=0)
        product = jnp.dot(split_ref[k], weights, preferred_element_type=jnp.float32)
        lanes = pl.ds(pl.multiple_of(column * width, width), width)
        out_ref[:, lanes] += product[:, :width] + product[:, width:]

    def add_group(parts, codes_ref):
        owners = parts[0].shape[0]

        def first(owner):
            code = codes_ref[owner, 0, 0].astype(jnp.int32)
            tile, k, column = whole(parts, owner, 0, jnp.maximum(code, 0))
            multiply(jnp.where(code >= 0, tile, 0.0), k, column)

        def later(owner, slot):
            code = codes_ref[owner, 0, slot].astype(jnp.int32)

            @pl.when(code >= 0)
            def _():
                multiply(*whole(parts, owner, slot, code))

        unroll = min(4, owners)

        def some(step, carry):
            for i in range(unroll):
                first(unroll * step + i)
            for i in range(unroll):
                for slot in range(1, SLOT):
                    later(unroll * step + i, slot)
            return carry

        lax.fori_loop(0, owners // unroll, some, 0)

    for parts, codes_ref in zip(groups, codes):
        add_group(parts, codes_ref)


def contract(split_amplitudes, groups, residual):
    width = groups[0][0].shape[2]
    vmem = pl.BlockSpec(memory_space=pltpu.VMEM)
    arrays = [split_amplitudes, *[part for parts in groups for part in parts], residual]
    return pl.pallas_call(
        functools.partial(contract_kernel, len(groups), len(groups[0])),
        out_shape=jax.ShapeDtypeStruct(residual.shape, jnp.float32),
        in_specs=[vmem] * len(arrays),
        out_specs=vmem,
        scratch_shapes=[
            *[pltpu.SMEM((parts[0].shape[0], META, width), jnp.float32) for parts in groups],
            pltpu.SemaphoreType.DMA((len(groups),)),
        ],
        compiler_params=pltpu.CompilerParams(vmem_limit_bytes=24 * 1024 * 1024),
    )(*arrays)


def send(x, axis, partner):
    size = lax.axis_size(axis)
    return lax.ppermute(x, axis, [(i, partner(i)) for i in range(size)])


def hop(x, step):
    return send(x, "bulk", lambda i: i ^ step)


def gather(block, size):
    held, at = block[None], (0,)
    bit = size // 2
    while bit > 2:
        held, at = jnp.concatenate([held, hop(held, bit)], axis=0), at + tuple(p ^ bit for p in at)
        bit //= 2
    over_x, over_y = hop(held, 1), hop(held, 2)
    cut = len(at) // 2
    pieces = [held, over_x, over_y, hop(over_x[:cut], 2), hop(over_y[cut:], 1)]
    positions = [at] + [tuple(p ^ step for p in at) for step in (1, 2)]
    positions += [tuple(p ^ 3 for p in at[:cut]), tuple(p ^ 3 for p in at[cut:])]
    return pieces, positions


def across(kept, sent, first, second):
    half = kept.shape[0] // 2
    come = hop(sent, first)
    last = hop(jnp.concatenate([kept[half:], come[half:]], axis=0), second)
    return (
        [jnp.stack([kept[z], come[z]]) for z in range(half)],
        [jnp.stack([last[z], last[half + z]]) for z in range(half)],
    )


def local(residual_in, amplitudes, integral_tiles, tile_reader, tile_k, tile_column):
    targets = lax.axis_size("bulk")
    rows_axis = lax.axis_size("row")
    width = integral_tiles.shape[2]
    pieces, positions = gather(amplitudes, targets)
    even_kept, even_sent, odd_kept, odd_sent = pack(
        integral_tiles, tile_reader, tile_k, tile_column, targets
    )
    odd = across(odd_kept, odd_sent, 2, 1)
    even = across(even_kept, even_sent, 1, 2)
    waves = [[plane for pair in zip(even[w], odd[w]) for plane in pair] for w in range(2)]
    waves = [[wave[0]] + [hop(plane, 4 * z) for z, plane in enumerate(wave) if z] for wave in waves]
    quarter = targets // 16
    groups = []
    for planes in (
        waves[0],
        waves[1][: 2 * quarter],
        waves[1][2 * quarter : 3 * quarter],
        waves[1][3 * quarter :],
    ):
        mine = jnp.concatenate(planes, axis=0)
        groups.append(
            [mine] + [send(mine, "row", lambda i: (i + q) % rows_axis) for q in range(1, rows_axis)]
        )
    if amplitudes.shape[1] != width:
        stacked = jnp.concatenate(pieces, axis=0)
        listed = [p for held in positions for p in held]
        place = jnp.asarray([listed.index(p) for p in range(targets)], jnp.int32)
        wanted = jnp.bitwise_xor(jnp.arange(targets, dtype=jnp.int32), lax.axis_index("bulk"))
        stacked = stacked[place[wanted]]
        stacked = stacked.transpose(1, 0, 2).reshape(amplitudes.shape[0], KT, width).transpose(1, 0, 2)
        pieces, positions = [stacked], [(None,) * KT]
    return contract(split(pieces, positions), groups, residual_in)


def solution(mesh):
    placed = (
        P("row", "bulk"),
        P("row", "bulk"),
        P("bulk", "row", None),
        P("bulk", None),
        P("bulk"),
        P("bulk"),
    )
    return jax.shard_map(
        local, mesh=mesh, in_specs=placed, out_specs=P("row", "bulk"), check_vma=False
    )
```

```python
import functools

import jax
import jax.numpy as jnp
from jax import lax
from jax.experimental import pallas as pl
from jax.experimental.pallas import tpu as pltpu
from jax.sharding import PartitionSpec as P

KT = 16
CT = 8
SLOT = 2
HINT = 32 * 1024 * 1024
META = 8


def pack_kernel(words_ref, tiles_ref, *refs):
    outs, count_ref = refs[:4], refs[4]
    count, height, width = tiles_ref.shape
    half = outs[0].shape[0] // 2
    targets = 8 * half
    me = lax.axis_index("bulk")
    for out_ref in outs:
        out_ref[:, SLOT * height :, :] = jnp.full((2 * half, META, width), -1.0, jnp.float32)
    for target in range(targets):
        count_ref[target] = 0
    lane = lax.broadcasted_iota(jnp.int32, (META, width), 1)

    def place(j, carry):
        word = words_ref[j]
        reader = word // (KT * CT)
        position = jnp.bitwise_xor(reader, me)
        slot = count_ref[position]
        count_ref[position] = slot + 1
        code = (word - reader * (KT * CT)).astype(jnp.float32)
        x, y, z = position % 2, position // 2 % 2, position // 4
        odd = z % 2
        first, second = jnp.where(odd == 1, y, x), jnp.where(odd == 1, x, y)
        which = 2 * odd + first
        at = second * half + z // 2
        for number, out_ref in enumerate(outs):

            @pl.when(which == number)
            def _():
                out_ref[at, pl.ds(pl.multiple_of(slot * height, height), height), :] = tiles_ref[j]
                codes = out_ref[at, SLOT * height :, :]
                out_ref[at, SLOT * height :, :] = jnp.where(lane == slot, code, codes)

        return carry

    lax.fori_loop(0, count, place, 0)


def pack(tiles, readers, tile_k, tile_column, targets):
    _, height, width = tiles.shape
    vmem = pl.BlockSpec(memory_space=pltpu.VMEM)
    words = (readers.reshape(-1) * KT + tile_k) * CT + tile_column
    out = jax.ShapeDtypeStruct((targets // 4, SLOT * height + META, width), jnp.float32)
    return pl.pallas_call(
        pack_kernel,
        out_shape=[out] * 4,
        in_specs=[pl.BlockSpec(memory_space=pltpu.SMEM), vmem],
        out_specs=[vmem] * 4,
        scratch_shapes=[
            pltpu.SMEM((targets,), jnp.int32),
        ],
        cost_estimate=pl.CostEstimate(flops=0, bytes_accessed=4 * tiles.size * 3, transcendentals=0),
        compiler_params=pltpu.CompilerParams(vmem_limit_bytes=8 * 1024 * 1024),
    )(words, tiles)


def split_kernel(positions, *refs):
    pieces, split_ref = refs[:-1], refs[-1]
    me = lax.axis_index("bulk")
    for piece, held in zip(pieces, positions):
        for at, position in enumerate(held):
            block = piece[at]
            high = block.astype(jnp.bfloat16)
            low = (block - high.astype(jnp.float32)).astype(jnp.bfloat16)
            k = at if position is None else jnp.bitwise_xor(me, position)
            split_ref[k] = jnp.concatenate([high, low], axis=1)


def split(pieces, positions):
    _, rows, width = pieces[0].shape
    vmem = pl.BlockSpec(memory_space=pltpu.VMEM)
    return pl.pallas_call(
        functools.partial(split_kernel, positions),
        out_shape=jax.ShapeDtypeStruct((KT, rows, 2 * width), jnp.bfloat16),
        in_specs=[vmem] * len(pieces),
        out_specs=vmem,
        cost_estimate=pl.CostEstimate(flops=0, bytes_accessed=HINT, transcendentals=0),
        compiler_params=pltpu.CompilerParams(vmem_limit_bytes=16 * 1024 * 1024),
    )(*pieces)


def contract_kernel(groups_count, parts_count, split_ref, *refs):
    end = groups_count * parts_count
    groups = [refs[g * parts_count : (g + 1) * parts_count] for g in range(groups_count)]
    residual_ref, out_ref = refs[end : end + 2]
    codes = refs[end + 2 : end + 2 + groups_count]
    sem = refs[-1]
    height = (groups[0][0].shape[1] - META) // SLOT
    width = groups[0][0].shape[2]
    row = lax.axis_index("row")
    fetches = [
        pltpu.make_async_copy(parts[0].at[:, pl.ds(SLOT * height, META), :], codes[g], sem.at[g])
        for g, parts in enumerate(groups)
    ]
    for fetch in fetches:
        fetch.start()
    out_ref[...] = residual_ref[...]
    for fetch in fetches:
        fetch.wait()

    def whole(parts, owner, slot, code):
        k = code // CT
        column = code - k * CT
        ordered = []
        for place in range(parts_count):
            piece = parts[0][owner, slot * height : (slot + 1) * height, :]
            for q in range(1, parts_count):
                other = parts[q][owner, slot * height : (slot + 1) * height, :]
                piece = jnp.where(lax.rem(place + q, parts_count) == row, other, piece)
            ordered.append(piece)
        return jnp.concatenate(ordered, axis=0), k, column

    def multiply(tile, k, column):
        high = tile.astype(jnp.bfloat16)
        low = (tile - high.astype(jnp.float32)).astype(jnp.bfloat16)
        both = jnp.concatenate([high, low], axis=1)
        weights = jnp.concatenate([both, both], axis=0)
        product = jnp.dot(split_ref[k], weights, preferred_element_type=jnp.float32)
        lanes = pl.ds(pl.multiple_of(column * width, width), width)
        out_ref[:, lanes] += product[:, :width] + product[:, width:]

    def add_group(parts, codes_ref):
        owners = parts[0].shape[0]

        def first(owner):
            code = codes_ref[owner, 0, 0].astype(jnp.int32)
            tile, k, column = whole(parts, owner, 0, jnp.maximum(code, 0))
            multiply(jnp.where(code >= 0, tile, 0.0), k, column)

        def later(owner, slot):
            code = codes_ref[owner, 0, slot].astype(jnp.int32)

            @pl.when(code >= 0)
            def _():
                multiply(*whole(parts, owner, slot, code))

        unroll = min(4, owners)

        def some(step, carry):
            for i in range(unroll):
                first(unroll * step + i)
            for i in range(unroll):
                for slot in range(1, SLOT):
                    later(unroll * step + i, slot)
            return carry

        lax.fori_loop(0, owners // unroll, some, 0)

    for parts, codes_ref in zip(groups, codes):
        add_group(parts, codes_ref)


def contract(split_amplitudes, groups, residual):
    width = groups[0][0].shape[2]
    vmem = pl.BlockSpec(memory_space=pltpu.VMEM)
    arrays = [split_amplitudes, *[part for parts in groups for part in parts], residual]
    return pl.pallas_call(
        functools.partial(contract_kernel, len(groups), len(groups[0])),
        out_shape=jax.ShapeDtypeStruct(residual.shape, jnp.float32),
        in_specs=[vmem] * len(arrays),
        out_specs=vmem,
        scratch_shapes=[
            *[pltpu.SMEM((parts[0].shape[0], META, width), jnp.float32) for parts in groups],
            pltpu.SemaphoreType.DMA((len(groups),)),
        ],
        compiler_params=pltpu.CompilerParams(vmem_limit_bytes=24 * 1024 * 1024),
    )(*arrays)


def send(x, axis, partner):
    size = lax.axis_size(axis)
    return lax.ppermute(x, axis, [(i, partner(i)) for i in range(size)])


def hop(x, step):
    return send(x, "bulk", lambda i: i ^ step)


def gather(block, size):
    held, at = block[None], (0,)
    bit = size // 2
    while bit > 4:
        held, at = jnp.concatenate([held, hop(held, bit)], axis=0), at + tuple(p ^ bit for p in at)
        bit //= 2
    pieces = {0: held, 4: hop(held, 4), 1: hop(held, 1), 2: hop(held, 2)}
    pieces[5] = hop(pieces[4], 1)
    pieces[6] = hop(pieces[4], 2)
    pieces[3] = hop(pieces[2], 1)
    pieces[7] = hop(pieces[5], 2)
    return list(pieces.values()), [tuple(p ^ step for p in at) for step in pieces]


def across(kept, sent, first, second):
    half = kept.shape[0] // 2
    come = hop(sent, first)
    last = hop(jnp.concatenate([kept[half:], come[half:]], axis=0), second)
    return (
        [jnp.stack([kept[z], come[z]]) for z in range(half)],
        [jnp.stack([last[z], last[half + z]]) for z in range(half)],
    )


def local(residual_in, amplitudes, integral_tiles, tile_reader, tile_k, tile_column):
    targets = lax.axis_size("bulk")
    rows_axis = lax.axis_size("row")
    width = integral_tiles.shape[2]
    pieces, positions = gather(amplitudes, targets)
    even_kept, even_sent, odd_kept, odd_sent = pack(
        integral_tiles, tile_reader, tile_k, tile_column, targets
    )
    odd = across(odd_kept, odd_sent, 2, 1)
    even = across(even_kept, even_sent, 1, 2)
    waves = [[plane for pair in zip(even[w], odd[w]) for plane in pair] for w in range(2)]
    waves = [[wave[0]] + [hop(plane, 4 * z) for z, plane in enumerate(wave) if z] for wave in waves]
    quarter = targets // 16
    groups = []
    for planes in (
        waves[0],
        waves[1][: 2 * quarter],
        waves[1][2 * quarter : 3 * quarter],
        waves[1][3 * quarter :],
    ):
        mine = jnp.concatenate(planes, axis=0)
        groups.append(
            [mine] + [send(mine, "row", lambda i: (i + q) % rows_axis) for q in range(1, rows_axis)]
        )
    if amplitudes.shape[1] != width:
        stacked = jnp.concatenate(pieces, axis=0)
        listed = [p for held in positions for p in held]
        place = jnp.asarray([listed.index(p) for p in range(targets)], jnp.int32)
        wanted = jnp.bitwise_xor(jnp.arange(targets, dtype=jnp.int32), lax.axis_index("bulk"))
        stacked = stacked[place[wanted]]
        stacked = stacked.transpose(1, 0, 2).reshape(amplitudes.shape[0], KT, width).transpose(1, 0, 2)
        pieces, positions = [stacked], [(None,) * KT]
    return contract(split(pieces, positions), groups, residual_in)


def solution(mesh):
    placed = (
        P("row", "bulk"),
        P("row", "bulk"),
        P("bulk", "row", None),
        P("bulk", None),
        P("bulk"),
        P("bulk"),
    )
    return jax.shard_map(
        local, mesh=mesh, in_specs=placed, out_specs=P("row", "bulk"), check_vma=False
    )
```

```python
import functools

import jax
import jax.numpy as jnp
from jax import lax
from jax.experimental import pallas as pl
from jax.experimental.pallas import tpu as pltpu
from jax.sharding import PartitionSpec as P

KT = 16
CT = 8
SLOT = 2
HINT = 32 * 1024 * 1024
META = 8


def pack_kernel(words_ref, tiles_ref, *refs):
    outs, count_ref = refs[:4], refs[4]
    count, height, width = tiles_ref.shape
    half = outs[0].shape[0] // 2
    targets = 8 * half
    me = lax.axis_index("bulk")
    for out_ref in outs:
        out_ref[:, SLOT * height :, :] = jnp.full((2 * half, META, width), -1.0, jnp.float32)
    for target in range(targets):
        count_ref[target] = 0
    lane = lax.broadcasted_iota(jnp.int32, (META, width), 1)

    def place(j, carry):
        word = words_ref[j]
        reader = word // (KT * CT)
        position = jnp.bitwise_xor(reader, me)
        slot = count_ref[position]
        count_ref[position] = slot + 1
        code = (word - reader * (KT * CT)).astype(jnp.float32)
        x, y, z = position % 2, position // 2 % 2, position // 4
        odd = z % 2
        first, second = jnp.where(odd == 1, y, x), jnp.where(odd == 1, x, y)
        which = 2 * odd + first
        at = second * half + z // 2
        for number, out_ref in enumerate(outs):

            @pl.when(which == number)
            def _():
                out_ref[at, pl.ds(pl.multiple_of(slot * height, height), height), :] = tiles_ref[j]
                codes = out_ref[at, SLOT * height :, :]
                out_ref[at, SLOT * height :, :] = jnp.where(lane == slot, code, codes)

        return carry

    lax.fori_loop(0, count, place, 0)


def pack(tiles, readers, tile_k, tile_column, targets):
    _, height, width = tiles.shape
    vmem = pl.BlockSpec(memory_space=pltpu.VMEM)
    words = (readers.reshape(-1) * KT + tile_k) * CT + tile_column
    out = jax.ShapeDtypeStruct((targets // 4, SLOT * height + META, width), jnp.float32)
    return pl.pallas_call(
        pack_kernel,
        out_shape=[out] * 4,
        in_specs=[pl.BlockSpec(memory_space=pltpu.SMEM), vmem],
        out_specs=[vmem] * 4,
        scratch_shapes=[
            pltpu.SMEM((targets,), jnp.int32),
        ],
        cost_estimate=pl.CostEstimate(flops=0, bytes_accessed=4 * tiles.size * 3, transcendentals=0),
        compiler_params=pltpu.CompilerParams(vmem_limit_bytes=8 * 1024 * 1024),
    )(words, tiles)


def split_kernel(positions, *refs):
    pieces, split_ref = refs[:-1], refs[-1]
    me = lax.axis_index("bulk")
    for piece, held in zip(pieces, positions):
        for at, position in enumerate(held):
            block = piece[at]
            high = block.astype(jnp.bfloat16)
            low = (block - high.astype(jnp.float32)).astype(jnp.bfloat16)
            k = at if position is None else jnp.bitwise_xor(me, position)
            split_ref[k] = jnp.concatenate([high, low], axis=1)


def split(pieces, positions):
    _, rows, width = pieces[0].shape
    vmem = pl.BlockSpec(memory_space=pltpu.VMEM)
    return pl.pallas_call(
        functools.partial(split_kernel, positions),
        out_shape=jax.ShapeDtypeStruct((KT, rows, 2 * width), jnp.bfloat16),
        in_specs=[vmem] * len(pieces),
        out_specs=vmem,
        cost_estimate=pl.CostEstimate(flops=0, bytes_accessed=HINT, transcendentals=0),
        compiler_params=pltpu.CompilerParams(vmem_limit_bytes=16 * 1024 * 1024),
    )(*pieces)


def contract_kernel(groups_count, parts_count, split_ref, *refs):
    end = groups_count * parts_count
    groups = [refs[g * parts_count : (g + 1) * parts_count] for g in range(groups_count)]
    residual_ref, out_ref = refs[end : end + 2]
    codes = refs[end + 2 : end + 2 + groups_count]
    sem = refs[-1]
    height = (groups[0][0].shape[1] - META) // SLOT
    width = groups[0][0].shape[2]
    row = lax.axis_index("row")
    fetches = [
        pltpu.make_async_copy(parts[0].at[:, pl.ds(SLOT * height, META), :], codes[g], sem.at[g])
        for g, parts in enumerate(groups)
    ]
    for fetch in fetches:
        fetch.start()
    out_ref[...] = residual_ref[...]
    for fetch in fetches:
        fetch.wait()

    def whole(parts, owner, slot, code):
        k = code // CT
        column = code - k * CT
        ordered = []
        for place in range(parts_count):
            piece = parts[0][owner, slot * height : (slot + 1) * height, :]
            for q in range(1, parts_count):
                other = parts[q][owner, slot * height : (slot + 1) * height, :]
                piece = jnp.where(lax.rem(place + q, parts_count) == row, other, piece)
            ordered.append(piece)
        return jnp.concatenate(ordered, axis=0), k, column

    def multiply(tile, k, column):
        high = tile.astype(jnp.bfloat16)
        low = (tile - high.astype(jnp.float32)).astype(jnp.bfloat16)
        both = jnp.concatenate([high, low], axis=1)
        weights = jnp.concatenate([both, both], axis=0)
        product = jnp.dot(split_ref[k], weights, preferred_element_type=jnp.float32)
        lanes = pl.ds(pl.multiple_of(column * width, width), width)
        out_ref[:, lanes] += product[:, :width] + product[:, width:]

    def add_group(parts, codes_ref):
        owners = parts[0].shape[0]

        def first(owner):
            code = codes_ref[owner, 0, 0].astype(jnp.int32)
            tile, k, column = whole(parts, owner, 0, jnp.maximum(code, 0))
            multiply(jnp.where(code >= 0, tile, 0.0), k, column)

        def later(owner, slot):
            code = codes_ref[owner, 0, slot].astype(jnp.int32)

            @pl.when(code >= 0)
            def _():
                multiply(*whole(parts, owner, slot, code))

        unroll = min(4, owners)

        def some(step, carry):
            for i in range(unroll):
                first(unroll * step + i)
            for i in range(unroll):
                for slot in range(1, SLOT):
                    later(unroll * step + i, slot)
            return carry

        lax.fori_loop(0, owners // unroll, some, 0)

    for parts, codes_ref in zip(groups, codes):
        add_group(parts, codes_ref)


def contract(split_amplitudes, groups, residual):
    width = groups[0][0].shape[2]
    vmem = pl.BlockSpec(memory_space=pltpu.VMEM)
    arrays = [split_amplitudes, *[part for parts in groups for part in parts], residual]
    return pl.pallas_call(
        functools.partial(contract_kernel, len(groups), len(groups[0])),
        out_shape=jax.ShapeDtypeStruct(residual.shape, jnp.float32),
        in_specs=[vmem] * len(arrays),
        out_specs=vmem,
        scratch_shapes=[
            *[pltpu.SMEM((parts[0].shape[0], META, width), jnp.float32) for parts in groups],
            pltpu.SemaphoreType.DMA((len(groups),)),
        ],
        compiler_params=pltpu.CompilerParams(vmem_limit_bytes=24 * 1024 * 1024),
    )(*arrays)


def send(x, axis, partner):
    size = lax.axis_size(axis)
    return lax.ppermute(x, axis, [(i, partner(i)) for i in range(size)])


def hop(x, step):
    return send(x, "bulk", lambda i: i ^ step)


def hop(x, step):
    return send(x, "bulk", lambda i: i ^ step)


def hop_both(blocks, other, step):
    count, height, width = blocks.shape
    flat = jnp.concatenate([blocks.reshape(-1, width), other.reshape(-1, width)], axis=0)
    come = hop(flat, step)
    return come[: count * height].reshape(blocks.shape), come[count * height :].reshape(other.shape)


def local(residual_in, amplitudes, integral_tiles, tile_reader, tile_k, tile_column):
    targets = lax.axis_size("bulk")
    rows_axis = lax.axis_size("row")
    width = integral_tiles.shape[2]
    held, at = amplitudes[None], (0,)
    bit = targets // 2
    while bit > 4:
        held, at = jnp.concatenate([held, hop(held, bit)], axis=0), at + tuple(p ^ bit for p in at)
        bit //= 2
    even_kept, even_sent, odd_kept, odd_sent = pack(
        integral_tiles, tile_reader, tile_k, tile_column, targets
    )
    half = targets // 8
    even_come, odd_come = hop(even_sent, 1), hop(odd_sent, 2)
    late = hop(held, 4)
    first = [jnp.stack([even_kept[z], even_come[z]]) for z in range(half)]
    first = [plane for z in range(half) for plane in (first[z], jnp.stack([odd_kept[z], odd_come[z]]))]
    far_first = [hop(first[z], 4 * z) for z in range(half, 2 * half)]
    even_last, over_y = hop_both(jnp.concatenate([even_kept[half:], even_come[half:]]), held, 2)
    odd_last, over_x = hop_both(jnp.concatenate([odd_kept[half:], odd_come[half:]]), held, 1)
    last = [
        jnp.stack([come[z], come[half + z]]) for z in range(half) for come in (even_last, odd_last)
    ]
    near = [jnp.concatenate([first[z], last[z]]) for z in range(half)]
    near = [near[0]] + [hop(plane, 4 * z) for z, plane in enumerate(near) if z]
    far_last = [hop(last[z], 4 * z) for z in range(half, 2 * half)]
    late_x, late_y = hop(late, 1), hop(late, 2)
    pieces = {0: held, 4: late, 1: over_x, 2: over_y, 5: late_x, 6: late_y}
    pieces[3], pieces[7] = hop(over_y, 1), hop(late_x, 2)
    positions = [tuple(p ^ step for p in at) for step in pieces]
    pieces = list(pieces.values())
    groups = []
    for planes in (near[:1] + far_first, near[1:], far_last[: half // 2], far_last[half // 2 :]):
        mine = jnp.concatenate(planes, axis=0)
        groups.append(
            [mine] + [send(mine, "row", lambda i: (i + q) % rows_axis) for q in range(1, rows_axis)]
        )
    if amplitudes.shape[1] != width:
        stacked = jnp.concatenate(pieces, axis=0)
        listed = [p for held in positions for p in held]
        place = jnp.asarray([listed.index(p) for p in range(targets)], jnp.int32)
        wanted = jnp.bitwise_xor(jnp.arange(targets, dtype=jnp.int32), lax.axis_index("bulk"))
        stacked = stacked[place[wanted]]
        stacked = stacked.transpose(1, 0, 2).reshape(amplitudes.shape[0], KT, width).transpose(1, 0, 2)
        pieces, positions = [stacked], [(None,) * KT]
    return contract(split(pieces, positions), groups, residual_in)


def solution(mesh):
    placed = (
        P("row", "bulk"),
        P("row", "bulk"),
        P("bulk", "row", None),
        P("bulk", None),
        P("bulk"),
        P("bulk"),
    )
    return jax.shard_map(
        local, mesh=mesh, in_specs=placed, out_specs=P("row", "bulk"), check_vma=False
    )
```

```python
import functools

import jax
import jax.numpy as jnp
from jax import lax
from jax.experimental import pallas as pl
from jax.experimental.pallas import tpu as pltpu
from jax.sharding import PartitionSpec as P

KT = 16
CT = 8
SLOT = 2
HINT = 32 * 1024 * 1024
META = 8


def pack_kernel(words_ref, tiles_ref, *refs):
    outs, count_ref = refs[:4], refs[4]
    count, height, width = tiles_ref.shape
    half = outs[0].shape[0] // 2
    targets = 8 * half
    me = lax.axis_index("bulk")
    for out_ref in outs:
        out_ref[:, SLOT * height :, :] = jnp.full((2 * half, META, width), -1.0, jnp.float32)
    for target in range(targets):
        count_ref[target] = 0
    lane = lax.broadcasted_iota(jnp.int32, (META, width), 1)

    def place(j, carry):
        word = words_ref[j]
        reader = word // (KT * CT)
        position = jnp.bitwise_xor(reader, me)
        slot = count_ref[position]
        count_ref[position] = slot + 1
        code = (word - reader * (KT * CT)).astype(jnp.float32)
        x, y, z = position % 2, position // 2 % 2, position // 4
        odd = z % 2
        first, second = jnp.where(odd == 1, y, x), jnp.where(odd == 1, x, y)
        which = 2 * odd + first
        at = second * half + z // 2
        for number, out_ref in enumerate(outs):

            @pl.when(which == number)
            def _():
                out_ref[at, pl.ds(pl.multiple_of(slot * height, height), height), :] = tiles_ref[j]
                codes = out_ref[at, SLOT * height :, :]
                out_ref[at, SLOT * height :, :] = jnp.where(lane == slot, code, codes)

        return carry

    lax.fori_loop(0, count, place, 0)


def pack(tiles, readers, tile_k, tile_column, targets):
    _, height, width = tiles.shape
    vmem = pl.BlockSpec(memory_space=pltpu.VMEM)
    words = (readers.reshape(-1) * KT + tile_k) * CT + tile_column
    out = jax.ShapeDtypeStruct((targets // 4, SLOT * height + META, width), jnp.float32)
    return pl.pallas_call(
        pack_kernel,
        out_shape=[out] * 4,
        in_specs=[pl.BlockSpec(memory_space=pltpu.SMEM), vmem],
        out_specs=[vmem] * 4,
        scratch_shapes=[
            pltpu.SMEM((targets,), jnp.int32),
        ],
        cost_estimate=pl.CostEstimate(flops=0, bytes_accessed=4 * tiles.size * 3, transcendentals=0),
        compiler_params=pltpu.CompilerParams(vmem_limit_bytes=8 * 1024 * 1024),
    )(words, tiles)


def split_kernel(positions, *refs):
    pieces, split_ref = refs[:-1], refs[-1]
    me = lax.axis_index("bulk")
    for piece, held in zip(pieces, positions):
        for at, position in enumerate(held):
            block = piece[at]
            high = block.astype(jnp.bfloat16)
            low = (block - high.astype(jnp.float32)).astype(jnp.bfloat16)
            k = at if position is None else jnp.bitwise_xor(me, position)
            split_ref[k] = jnp.concatenate([high, low], axis=1)


def split(pieces, positions):
    _, rows, width = pieces[0].shape
    vmem = pl.BlockSpec(memory_space=pltpu.VMEM)
    return pl.pallas_call(
        functools.partial(split_kernel, positions),
        out_shape=jax.ShapeDtypeStruct((KT, rows, 2 * width), jnp.bfloat16),
        in_specs=[vmem] * len(pieces),
        out_specs=vmem,
        cost_estimate=pl.CostEstimate(flops=0, bytes_accessed=HINT, transcendentals=0),
        compiler_params=pltpu.CompilerParams(vmem_limit_bytes=16 * 1024 * 1024),
    )(*pieces)


def contract_kernel(groups_count, parts_count, split_ref, *refs):
    end = groups_count * parts_count
    groups = [refs[g * parts_count : (g + 1) * parts_count] for g in range(groups_count)]
    residual_ref, out_ref = refs[end : end + 2]
    codes = refs[end + 2 : end + 2 + groups_count]
    sem = refs[-1]
    height = (groups[0][0].shape[1] - META) // SLOT
    width = groups[0][0].shape[2]
    row = lax.axis_index("row")
    fetches = [
        pltpu.make_async_copy(parts[0].at[:, pl.ds(SLOT * height, META), :], codes[g], sem.at[g])
        for g, parts in enumerate(groups)
    ]
    for fetch in fetches:
        fetch.start()
    out_ref[...] = residual_ref[...]
    for fetch in fetches:
        fetch.wait()

    def whole(parts, owner, slot, code):
        k = code // CT
        column = code - k * CT
        ordered = []
        for place in range(parts_count):
            piece = parts[0][owner, slot * height : (slot + 1) * height, :]
            for q in range(1, parts_count):
                other = parts[q][owner, slot * height : (slot + 1) * height, :]
                piece = jnp.where(lax.rem(place + q, parts_count) == row, other, piece)
            ordered.append(piece)
        return jnp.concatenate(ordered, axis=0), k, column

    def multiply(tile, k, column):
        high = tile.astype(jnp.bfloat16)
        low = (tile - high.astype(jnp.float32)).astype(jnp.bfloat16)
        both = jnp.concatenate([high, low], axis=1)
        weights = jnp.concatenate([both, both], axis=0)
        product = jnp.dot(split_ref[k], weights, preferred_element_type=jnp.float32)
        lanes = pl.ds(pl.multiple_of(column * width, width), width)
        out_ref[:, lanes] += product[:, :width] + product[:, width:]

    def add_group(parts, codes_ref):
        owners = parts[0].shape[0]

        def first(owner):
            code = codes_ref[owner, 0, 0].astype(jnp.int32)
            tile, k, column = whole(parts, owner, 0, jnp.maximum(code, 0))
            multiply(jnp.where(code >= 0, tile, 0.0), k, column)

        def later(owner, slot):
            code = codes_ref[owner, 0, slot].astype(jnp.int32)

            @pl.when(code >= 0)
            def _():
                multiply(*whole(parts, owner, slot, code))

        unroll = min(4, owners)

        def some(step, carry):
            for i in range(unroll):
                first(unroll * step + i)
            for i in range(unroll):
                for slot in range(1, SLOT):
                    later(unroll * step + i, slot)
            return carry

        lax.fori_loop(0, owners // unroll, some, 0)

    for parts, codes_ref in zip(groups, codes):
        add_group(parts, codes_ref)


def contract(split_amplitudes, groups, residual):
    width = groups[0][0].shape[2]
    vmem = pl.BlockSpec(memory_space=pltpu.VMEM)
    arrays = [split_amplitudes, *[part for parts in groups for part in parts], residual]
    return pl.pallas_call(
        functools.partial(contract_kernel, len(groups), len(groups[0])),
        out_shape=jax.ShapeDtypeStruct(residual.shape, jnp.float32),
        in_specs=[vmem] * len(arrays),
        out_specs=vmem,
        scratch_shapes=[
            *[pltpu.SMEM((parts[0].shape[0], META, width), jnp.float32) for parts in groups],
            pltpu.SemaphoreType.DMA((len(groups),)),
        ],
        compiler_params=pltpu.CompilerParams(vmem_limit_bytes=24 * 1024 * 1024),
    )(*arrays)


def send(x, axis, partner):
    size = lax.axis_size(axis)
    return lax.ppermute(x, axis, [(i, partner(i)) for i in range(size)])


def hop(x, step):
    return send(x, "bulk", lambda i: i ^ step)


def hop_both(blocks, other, step):
    count, height, width = blocks.shape
    flat = jnp.concatenate([blocks.reshape(-1, width), other.reshape(-1, width)], axis=0)
    come = hop(flat, step)
    return come[: count * height].reshape(blocks.shape), come[count * height :].reshape(other.shape)


def local(residual_in, amplitudes, integral_tiles, tile_reader, tile_k, tile_column):
    targets = lax.axis_size("bulk")
    rows_axis = lax.axis_size("row")
    width = integral_tiles.shape[2]
    held, at = amplitudes[None], (0,)
    bit = targets // 2
    while bit > 4:
        held, at = jnp.concatenate([held, hop(held, bit)], axis=0), at + tuple(p ^ bit for p in at)
        bit //= 2
    even_kept, even_sent, odd_kept, odd_sent = pack(
        integral_tiles, tile_reader, tile_k, tile_column, targets
    )
    half = targets // 8
    even_come, odd_come = hop(even_sent, 1), hop(odd_sent, 2)
    late = hop(held, 4)
    first = [jnp.stack([even_kept[z], even_come[z]]) for z in range(half)]
    first = [plane for z in range(half) for plane in (first[z], jnp.stack([odd_kept[z], odd_come[z]]))]
    far_first = [hop(first[z], 4 * z) for z in range(half, 2 * half)]
    even_last, over_y = hop_both(jnp.concatenate([even_kept[half:], even_come[half:]]), held, 2)
    odd_last, over_x = hop_both(jnp.concatenate([odd_kept[half:], odd_come[half:]]), held, 1)
    last = [
        jnp.stack([come[z], come[half + z]]) for z in range(half) for come in (even_last, odd_last)
    ]
    near = [jnp.concatenate([first[z], last[z]]) for z in range(half)]
    near = [near[0]] + [hop(plane, 4 * z) for z, plane in enumerate(near) if z]
    far_last = [hop(last[z], 4 * z) for z in range(half, 2 * half)]
    cut = len(at) // 2
    come = hop(jnp.concatenate([late, over_y[:cut]]), 1)
    late_x, diagonal_x = come[: len(at)], come[len(at) :]
    come = hop(jnp.concatenate([late, over_x[cut:]]), 2)
    late_y, diagonal_y = come[: len(at)], come[len(at) :]
    pieces = [held, late, over_x, over_y, late_x, late_y, diagonal_x, diagonal_y]
    pieces += [hop(late_y[:cut], 1), hop(late_x[cut:], 2)]
    positions = [tuple(p ^ step for p in at) for step in (0, 4, 1, 2, 5, 6)]
    positions += [tuple(p ^ step for p in part) for step in (3, 7) for part in (at[:cut], at[cut:])]
    groups = []
    for planes in (near + far_first, far_last):
        mine = jnp.concatenate(planes, axis=0)
        groups.append(
            [mine] + [send(mine, "row", lambda i: (i + q) % rows_axis) for q in range(1, rows_axis)]
        )
    if amplitudes.shape[1] != width:
        stacked = jnp.concatenate(pieces, axis=0)
        listed = [p for held in positions for p in held]
        place = jnp.asarray([listed.index(p) for p in range(targets)], jnp.int32)
        wanted = jnp.bitwise_xor(jnp.arange(targets, dtype=jnp.int32), lax.axis_index("bulk"))
        stacked = stacked[place[wanted]]
        stacked = stacked.transpose(1, 0, 2).reshape(amplitudes.shape[0], KT, width).transpose(1, 0, 2)
        pieces, positions = [stacked], [(None,) * KT]
    return contract(split(pieces, positions), groups, residual_in)


def solution(mesh):
    placed = (
        P("row", "bulk"),
        P("row", "bulk"),
        P("bulk", "row", None),
        P("bulk", None),
        P("bulk"),
        P("bulk"),
    )
    return jax.shard_map(
        local, mesh=mesh, in_specs=placed, out_specs=P("row", "bulk"), check_vma=False
    )
```

```python
import functools

import jax
import jax.numpy as jnp
from jax import lax
from jax.experimental import pallas as pl
from jax.experimental.pallas import tpu as pltpu
from jax.sharding import PartitionSpec as P

KT = 16
CT = 8
SLOT = 2
HINT = 256 * 1024 * 1024
META = 8


def pack_kernel(words_ref, tiles_ref, *refs):
    outs, count_ref = refs[:4], refs[4]
    count, height, width = tiles_ref.shape
    half = outs[0].shape[0] // 2
    targets = 8 * half
    me = lax.axis_index("bulk")
    for out_ref in outs:
        out_ref[:, SLOT * height :, :] = jnp.full((2 * half, META, width), -1.0, jnp.float32)
    for target in range(targets):
        count_ref[target] = 0
    lane = lax.broadcasted_iota(jnp.int32, (META, width), 1)

    def place(j, carry):
        word = words_ref[j]
        reader = word // (KT * CT)
        position = jnp.bitwise_xor(reader, me)
        slot = count_ref[position]
        count_ref[position] = slot + 1
        code = (word - reader * (KT * CT)).astype(jnp.float32)
        x, y, z = position % 2, position // 2 % 2, position // 4
        odd = z % 2
        first, second = jnp.where(odd == 1, y, x), jnp.where(odd == 1, x, y)
        which = 2 * odd + first
        at = second * half + z // 2
        for number, out_ref in enumerate(outs):

            @pl.when(which == number)
            def _():
                out_ref[at, pl.ds(pl.multiple_of(slot * height, height), height), :] = tiles_ref[j]
                codes = out_ref[at, SLOT * height :, :]
                out_ref[at, SLOT * height :, :] = jnp.where(lane == slot, code, codes)

        return carry

    lax.fori_loop(0, count, place, 0)


def pack(tiles, readers, tile_k, tile_column, targets):
    _, height, width = tiles.shape
    vmem = pl.BlockSpec(memory_space=pltpu.VMEM)
    words = (readers.reshape(-1) * KT + tile_k) * CT + tile_column
    out = jax.ShapeDtypeStruct((targets // 4, SLOT * height + META, width), jnp.float32)
    return pl.pallas_call(
        pack_kernel,
        out_shape=[out] * 4,
        in_specs=[pl.BlockSpec(memory_space=pltpu.SMEM), vmem],
        out_specs=[vmem] * 4,
        scratch_shapes=[
            pltpu.SMEM((targets,), jnp.int32),
        ],
        cost_estimate=pl.CostEstimate(flops=0, bytes_accessed=4 * tiles.size * 3, transcendentals=0),
        compiler_params=pltpu.CompilerParams(vmem_limit_bytes=8 * 1024 * 1024),
    )(words, tiles)


def split_kernel(positions, *refs):
    pieces, split_ref = refs[:-1], refs[-1]
    me = lax.axis_index("bulk")
    for piece, held in zip(pieces, positions):
        for at, position in enumerate(held):
            block = piece[at]
            high = block.astype(jnp.bfloat16)
            low = (block - high.astype(jnp.float32)).astype(jnp.bfloat16)
            k = at if position is None else jnp.bitwise_xor(me, position)
            split_ref[k] = jnp.concatenate([high, low], axis=1)


def split(pieces, positions):
    _, rows, width = pieces[0].shape
    vmem = pl.BlockSpec(memory_space=pltpu.VMEM)
    return pl.pallas_call(
        functools.partial(split_kernel, positions),
        out_shape=jax.ShapeDtypeStruct((KT, rows, 2 * width), jnp.bfloat16),
        in_specs=[vmem] * len(pieces),
        out_specs=vmem,
        cost_estimate=pl.CostEstimate(flops=0, bytes_accessed=HINT, transcendentals=0),
        compiler_params=pltpu.CompilerParams(vmem_limit_bytes=16 * 1024 * 1024),
    )(*pieces)


def contract_kernel(groups_count, parts_count, split_ref, *refs):
    end = groups_count * parts_count
    groups = [refs[g * parts_count : (g + 1) * parts_count] for g in range(groups_count)]
    residual_ref, out_ref = refs[end : end + 2]
    codes = refs[end + 2 : end + 2 + groups_count]
    sem = refs[-1]
    height = (groups[0][0].shape[1] - META) // SLOT
    width = groups[0][0].shape[2]
    row = lax.axis_index("row")
    fetches = [
        pltpu.make_async_copy(parts[0].at[:, pl.ds(SLOT * height, META), :], codes[g], sem.at[g])
        for g, parts in enumerate(groups)
    ]
    for fetch in fetches:
        fetch.start()
    out_ref[...] = residual_ref[...]
    for fetch in fetches:
        fetch.wait()

    def whole(parts, owner, slot, code):
        k = code // CT
        column = code - k * CT
        ordered = []
        for place in range(parts_count):
            piece = parts[0][owner, slot * height : (slot + 1) * height, :]
            for q in range(1, parts_count):
                other = parts[q][owner, slot * height : (slot + 1) * height, :]
                piece = jnp.where(lax.rem(place + q, parts_count) == row, other, piece)
            ordered.append(piece)
        return jnp.concatenate(ordered, axis=0), k, column

    def multiply(tile, k, column):
        high = tile.astype(jnp.bfloat16)
        low = (tile - high.astype(jnp.float32)).astype(jnp.bfloat16)
        both = jnp.concatenate([high, low], axis=1)
        weights = jnp.concatenate([both, both], axis=0)
        product = jnp.dot(split_ref[k], weights, preferred_element_type=jnp.float32)
        lanes = pl.ds(pl.multiple_of(column * width, width), width)
        out_ref[:, lanes] += product[:, :width] + product[:, width:]

    def add_group(parts, codes_ref):
        owners = parts[0].shape[0]

        def first(owner):
            code = codes_ref[owner, 0, 0].astype(jnp.int32)
            tile, k, column = whole(parts, owner, 0, jnp.maximum(code, 0))
            multiply(jnp.where(code >= 0, tile, 0.0), k, column)

        def later(owner, slot):
            code = codes_ref[owner, 0, slot].astype(jnp.int32)

            @pl.when(code >= 0)
            def _():
                multiply(*whole(parts, owner, slot, code))

        unroll = min(4, owners)

        def some(step, carry):
            for i in range(unroll):
                first(unroll * step + i)
            for i in range(unroll):
                for slot in range(1, SLOT):
                    later(unroll * step + i, slot)
            return carry

        lax.fori_loop(0, owners // unroll, some, 0)

    for parts, codes_ref in zip(groups, codes):
        add_group(parts, codes_ref)


def contract(split_amplitudes, groups, residual):
    width = groups[0][0].shape[2]
    vmem = pl.BlockSpec(memory_space=pltpu.VMEM)
    arrays = [split_amplitudes, *[part for parts in groups for part in parts], residual]
    return pl.pallas_call(
        functools.partial(contract_kernel, len(groups), len(groups[0])),
        out_shape=jax.ShapeDtypeStruct(residual.shape, jnp.float32),
        in_specs=[vmem] * len(arrays),
        out_specs=vmem,
        scratch_shapes=[
            *[pltpu.SMEM((parts[0].shape[0], META, width), jnp.float32) for parts in groups],
            pltpu.SemaphoreType.DMA((len(groups),)),
        ],
        compiler_params=pltpu.CompilerParams(vmem_limit_bytes=24 * 1024 * 1024),
    )(*arrays)


def send(x, axis, partner):
    size = lax.axis_size(axis)
    return lax.ppermute(x, axis, [(i, partner(i)) for i in range(size)])


def hop(x, step):
    return send(x, "bulk", lambda i: i ^ step)


def hop_both(blocks, other, step):
    count, height, width = blocks.shape
    flat = jnp.concatenate([blocks.reshape(-1, width), other.reshape(-1, width)], axis=0)
    come = hop(flat, step)
    return come[: count * height].reshape(blocks.shape), come[count * height :].reshape(other.shape)


def local(residual_in, amplitudes, integral_tiles, tile_reader, tile_k, tile_column):
    targets = lax.axis_size("bulk")
    rows_axis = lax.axis_size("row")
    width = integral_tiles.shape[2]
    held, at = amplitudes[None], (0,)
    bit = targets // 2
    while bit > 4:
        held, at = jnp.concatenate([held, hop(held, bit)], axis=0), at + tuple(p ^ bit for p in at)
        bit //= 2
    even_kept, even_sent, odd_kept, odd_sent = pack(
        integral_tiles, tile_reader, tile_k, tile_column, targets
    )
    half = targets // 8
    even_come, odd_come = hop(even_sent, 1), hop(odd_sent, 2)
    late = hop(held, 4)
    first = [jnp.stack([even_kept[z], even_come[z]]) for z in range(half)]
    first = [plane for z in range(half) for plane in (first[z], jnp.stack([odd_kept[z], odd_come[z]]))]
    far_first = [hop(first[z], 4 * z) for z in range(half, 2 * half)]
    even_last, over_y = hop_both(jnp.concatenate([even_kept[half:], even_come[half:]]), held, 2)
    odd_last, over_x = hop_both(jnp.concatenate([odd_kept[half:], odd_come[half:]]), held, 1)
    last = [
        jnp.stack([come[z], come[half + z]]) for z in range(half) for come in (even_last, odd_last)
    ]
    last, far_first = lax.optimization_barrier((last, far_first))
    far_last = [hop(last[z], 4 * z) for z in range(half, 2 * half)]
    near = [jnp.concatenate([first[z], last[z]]) for z in range(half)]
    near, far_last[: half // 2] = lax.optimization_barrier((near, far_last[: half // 2]))
    near = [near[0]] + [hop(plane, 4 * z) for z, plane in enumerate(near) if z]
    cut = len(at) // 2
    come = hop(jnp.concatenate([late, over_y[:cut]]), 1)
    late_x, diagonal_x = come[: len(at)], come[len(at) :]
    come = hop(jnp.concatenate([late, over_x[cut:]]), 2)
    late_y, diagonal_y = come[: len(at)], come[len(at) :]
    pieces = [held, late, over_x, over_y, late_x, late_y, diagonal_x, diagonal_y]
    pieces += [hop(late_y[:cut], 1), hop(late_x[cut:], 2)]
    positions = [tuple(p ^ step for p in at) for step in (0, 4, 1, 2, 5, 6)]
    positions += [tuple(p ^ step for p in part) for step in (3, 7) for part in (at[:cut], at[cut:])]
    groups = []
    for planes in (near[:1] + far_first, near[1:] + far_last):
        mine = jnp.concatenate(planes, axis=0)
        groups.append(
            [mine] + [send(mine, "row", lambda i: (i + q) % rows_axis) for q in range(1, rows_axis)]
        )
    if amplitudes.shape[1] != width:
        stacked = jnp.concatenate(pieces, axis=0)
        listed = [p for held in positions for p in held]
        place = jnp.asarray([listed.index(p) for p in range(targets)], jnp.int32)
        wanted = jnp.bitwise_xor(jnp.arange(targets, dtype=jnp.int32), lax.axis_index("bulk"))
        stacked = stacked[place[wanted]]
        stacked = stacked.transpose(1, 0, 2).reshape(amplitudes.shape[0], KT, width).transpose(1, 0, 2)
        pieces, positions = [stacked], [(None,) * KT]
    return contract(split(pieces, positions), groups, residual_in)


def solution(mesh):
    placed = (
        P("row", "bulk"),
        P("row", "bulk"),
        P("bulk", "row", None),
        P("bulk", None),
        P("bulk"),
        P("bulk"),
    )
    return jax.shard_map(
        local, mesh=mesh, in_specs=placed, out_specs=P("row", "bulk"), check_vma=False
    )
```

```python
import functools

import jax
import jax.numpy as jnp
from jax import lax
from jax.experimental import pallas as pl
from jax.experimental.pallas import tpu as pltpu
from jax.sharding import PartitionSpec as P

KT = 16
CT = 8
SLOT = 2
HINT = 256 * 1024 * 1024
META = 8


def pack_kernel(words_ref, tiles_ref, *refs):
    outs, count_ref = refs[:4], refs[4]
    count, height, width = tiles_ref.shape
    half = outs[0].shape[0] // 2
    targets = 8 * half
    me = lax.axis_index("bulk")
    for out_ref in outs:
        out_ref[:, SLOT * height :, :] = jnp.full((2 * half, META, width), -1.0, jnp.float32)
    for target in range(targets):
        count_ref[target] = 0
    lane = lax.broadcasted_iota(jnp.int32, (META, width), 1)

    def place(j, carry):
        word = words_ref[j]
        reader = word // (KT * CT)
        position = jnp.bitwise_xor(reader, me)
        slot = count_ref[position]
        count_ref[position] = slot + 1
        code = (word - reader * (KT * CT)).astype(jnp.float32)
        x, y, z = position % 2, position // 2 % 2, position // 4
        odd = z % 2
        first, second = jnp.where(odd == 1, y, x), jnp.where(odd == 1, x, y)
        which = 2 * odd + first
        at = second * half + z // 2
        for number, out_ref in enumerate(outs):

            @pl.when(which == number)
            def _():
                out_ref[at, pl.ds(pl.multiple_of(slot * height, height), height), :] = tiles_ref[j]
                codes = out_ref[at, SLOT * height :, :]
                out_ref[at, SLOT * height :, :] = jnp.where(lane == slot, code, codes)

        return carry

    lax.fori_loop(0, count, place, 0)


def pack(tiles, readers, tile_k, tile_column, targets):
    _, height, width = tiles.shape
    vmem = pl.BlockSpec(memory_space=pltpu.VMEM)
    words = (readers.reshape(-1) * KT + tile_k) * CT + tile_column
    out = jax.ShapeDtypeStruct((targets // 4, SLOT * height + META, width), jnp.float32)
    return pl.pallas_call(
        pack_kernel,
        out_shape=[out] * 4,
        in_specs=[pl.BlockSpec(memory_space=pltpu.SMEM), vmem],
        out_specs=[vmem] * 4,
        scratch_shapes=[
            pltpu.SMEM((targets,), jnp.int32),
        ],
        cost_estimate=pl.CostEstimate(flops=0, bytes_accessed=4 * tiles.size * 3, transcendentals=0),
        compiler_params=pltpu.CompilerParams(vmem_limit_bytes=8 * 1024 * 1024),
    )(words, tiles)


def split_kernel(positions, *refs):
    pieces, split_ref = refs[:-1], refs[-1]
    me = lax.axis_index("bulk")
    for piece, held in zip(pieces, positions):
        for at, position in enumerate(held):
            block = piece[at]
            high = block.astype(jnp.bfloat16)
            low = (block - high.astype(jnp.float32)).astype(jnp.bfloat16)
            k = at if position is None else jnp.bitwise_xor(me, position)
            split_ref[k] = jnp.concatenate([high, low], axis=1)


def split(pieces, positions):
    _, rows, width = pieces[0].shape
    vmem = pl.BlockSpec(memory_space=pltpu.VMEM)
    return pl.pallas_call(
        functools.partial(split_kernel, positions),
        out_shape=jax.ShapeDtypeStruct((KT, rows, 2 * width), jnp.bfloat16),
        in_specs=[vmem] * len(pieces),
        out_specs=vmem,
        cost_estimate=pl.CostEstimate(flops=0, bytes_accessed=HINT, transcendentals=0),
        compiler_params=pltpu.CompilerParams(vmem_limit_bytes=16 * 1024 * 1024),
    )(*pieces)


def contract_kernel(groups_count, parts_count, split_ref, *refs):
    end = groups_count * parts_count
    groups = [refs[g * parts_count : (g + 1) * parts_count] for g in range(groups_count)]
    residual_ref, out_ref = refs[end : end + 2]
    codes = refs[end + 2 : end + 2 + groups_count]
    sem = refs[-1]
    height = (groups[0][0].shape[1] - META) // SLOT
    width = groups[0][0].shape[2]
    row = lax.axis_index("row")
    fetches = [
        pltpu.make_async_copy(parts[0].at[:, pl.ds(SLOT * height, META), :], codes[g], sem.at[g])
        for g, parts in enumerate(groups)
    ]
    for fetch in fetches:
        fetch.start()
    out_ref[...] = residual_ref[...]
    for fetch in fetches:
        fetch.wait()

    def whole(parts, owner, slot, code):
        k = code // CT
        column = code - k * CT
        ordered = []
        for place in range(parts_count):
            piece = parts[0][owner, slot * height : (slot + 1) * height, :]
            for q in range(1, parts_count):
                other = parts[q][owner, slot * height : (slot + 1) * height, :]
                piece = jnp.where(lax.rem(place + q, parts_count) == row, other, piece)
            ordered.append(piece)
        return jnp.concatenate(ordered, axis=0), k, column

    def multiply(tile, k, column):
        high = tile.astype(jnp.bfloat16)
        low = (tile - high.astype(jnp.float32)).astype(jnp.bfloat16)
        both = jnp.concatenate([high, low], axis=1)
        weights = jnp.concatenate([both, both], axis=0)
        product = jnp.dot(split_ref[k], weights, preferred_element_type=jnp.float32)
        lanes = pl.ds(pl.multiple_of(column * width, width), width)
        out_ref[:, lanes] += product[:, :width] + product[:, width:]

    def add_group(parts, codes_ref):
        owners = parts[0].shape[0]

        def first(owner):
            code = codes_ref[owner, 0, 0].astype(jnp.int32)
            tile, k, column = whole(parts, owner, 0, jnp.maximum(code, 0))
            multiply(jnp.where(code >= 0, tile, 0.0), k, column)

        def later(owner, slot):
            code = codes_ref[owner, 0, slot].astype(jnp.int32)

            @pl.when(code >= 0)
            def _():
                multiply(*whole(parts, owner, slot, code))

        unroll = next(u for u in (5, 4, 3, 2, 1) if owners % u == 0)

        def some(step, carry):
            for i in range(unroll):
                first(unroll * step + i)
            for i in range(unroll):
                for slot in range(1, SLOT):
                    later(unroll * step + i, slot)
            return carry

        lax.fori_loop(0, owners // unroll, some, 0)

    for parts, codes_ref in zip(groups, codes):
        add_group(parts, codes_ref)


def contract(split_amplitudes, groups, residual):
    width = groups[0][0].shape[2]
    vmem = pl.BlockSpec(memory_space=pltpu.VMEM)
    arrays = [split_amplitudes, *[part for parts in groups for part in parts], residual]
    return pl.pallas_call(
        functools.partial(contract_kernel, len(groups), len(groups[0])),
        out_shape=jax.ShapeDtypeStruct(residual.shape, jnp.float32),
        in_specs=[vmem] * len(arrays),
        out_specs=vmem,
        scratch_shapes=[
            *[pltpu.SMEM((parts[0].shape[0], META, width), jnp.float32) for parts in groups],
            pltpu.SemaphoreType.DMA((len(groups),)),
        ],
        compiler_params=pltpu.CompilerParams(vmem_limit_bytes=24 * 1024 * 1024),
    )(*arrays)


def fetch_kernel(x_ref, out_ref):
    out_ref[...] = x_ref[...]


def fetch(x):
    vmem = pl.BlockSpec(memory_space=pltpu.VMEM)
    return pl.pallas_call(
        fetch_kernel,
        out_shape=jax.ShapeDtypeStruct(x.shape, x.dtype),
        in_specs=[vmem],
        out_specs=vmem,
        compiler_params=pltpu.CompilerParams(vmem_limit_bytes=8 * 1024 * 1024),
    )(x)


def send(x, axis, partner):
    size = lax.axis_size(axis)
    return lax.ppermute(x, axis, [(i, partner(i)) for i in range(size)])


def hop(x, step):
    return send(x, "bulk", lambda i: i ^ step)


def hop_both(blocks, other, step):
    count, height, width = blocks.shape
    flat = jnp.concatenate([blocks.reshape(-1, width), other.reshape(-1, width)], axis=0)
    come = hop(flat, step)
    return come[: count * height].reshape(blocks.shape), come[count * height :].reshape(other.shape)


def local(residual_in, amplitudes, integral_tiles, tile_reader, tile_k, tile_column):
    targets = lax.axis_size("bulk")
    rows_axis = lax.axis_size("row")
    width = integral_tiles.shape[2]
    held, at = amplitudes[None], (0,)
    bit = targets // 2
    while bit > 4:
        held, at = jnp.concatenate([held, hop(held, bit)], axis=0), at + tuple(p ^ bit for p in at)
        bit //= 2
    even_kept, even_sent, odd_kept, odd_sent = pack(
        integral_tiles, tile_reader, tile_k, tile_column, targets
    )
    half = targets // 8
    even_come, odd_come = hop(even_sent, 1), hop(odd_sent, 2)
    first = [jnp.stack([even_kept[z], even_come[z]]) for z in range(half)]
    first = [plane for z in range(half) for plane in (first[z], jnp.stack([odd_kept[z], odd_come[z]]))]
    near_come, late = hop_both(first[1], held, 4)
    come_first = [near_come] + [hop(plane, 4 * z) for z, plane in enumerate(first) if z > 1]
    even_last, over_y = hop_both(jnp.concatenate([even_kept[half:], even_come[half:]]), held, 2)
    odd_last, over_x = hop_both(jnp.concatenate([odd_kept[half:], odd_come[half:]]), held, 1)
    last = [
        jnp.stack([come[z], come[half + z]]) for z in range(half) for come in (even_last, odd_last)
    ]
    residual = fetch(residual_in)
    last, come_first, residual = lax.optimization_barrier((last, come_first, residual))
    come_last = [hop(plane, 4 * z) for z, plane in enumerate(last) if z]
    cut = len(at) // 2
    come = hop(jnp.concatenate([late, over_y[:cut]]), 1)
    late_x, diagonal_x = come[: len(at)], come[len(at) :]
    come = hop(jnp.concatenate([late, over_x[cut:]]), 2)
    late_y, diagonal_y = come[: len(at)], come[len(at) :]
    pieces = [held, late, over_x, over_y, late_x, late_y, diagonal_x, diagonal_y]
    pieces += [hop(late_y[:cut], 1), hop(late_x[cut:], 2)]
    positions = [tuple(p ^ step for p in at) for step in (0, 4, 1, 2, 5, 6)]
    positions += [tuple(p ^ step for p in part) for step in (3, 7) for part in (at[:cut], at[cut:])]
    groups = []
    for planes in ([first[0], last[0]] + come_first, come_last):
        mine = jnp.concatenate(planes, axis=0)
        groups.append(
            [mine] + [send(mine, "row", lambda i: (i + q) % rows_axis) for q in range(1, rows_axis)]
        )
    if amplitudes.shape[1] != width:
        stacked = jnp.concatenate(pieces, axis=0)
        listed = [p for held in positions for p in held]
        place = jnp.asarray([listed.index(p) for p in range(targets)], jnp.int32)
        wanted = jnp.bitwise_xor(jnp.arange(targets, dtype=jnp.int32), lax.axis_index("bulk"))
        stacked = stacked[place[wanted]]
        stacked = stacked.transpose(1, 0, 2).reshape(amplitudes.shape[0], KT, width).transpose(1, 0, 2)
        pieces, positions = [stacked], [(None,) * KT]
    return contract(split(pieces, positions), groups, residual)


def solution(mesh):
    placed = (
        P("row", "bulk"),
        P("row", "bulk"),
        P("bulk", "row", None),
        P("bulk", None),
        P("bulk"),
        P("bulk"),
    )
    return jax.shard_map(
        local, mesh=mesh, in_specs=placed, out_specs=P("row", "bulk"), check_vma=False
    )
```

```python
import functools

import jax
import jax.numpy as jnp
from jax import lax
from jax.experimental import pallas as pl
from jax.experimental.pallas import tpu as pltpu
from jax.sharding import PartitionSpec as P

KT = 16
CT = 8
SLOT = 2
META = 8


def pack_kernel(words_ref, tiles_ref, *refs):
    outs, count_ref = refs[:4], refs[4]
    count, height, width = tiles_ref.shape
    half = outs[0].shape[0] // 2
    targets = 8 * half
    me = lax.axis_index("bulk")
    for out_ref in outs:
        out_ref[:, SLOT * height :, :] = jnp.full((2 * half, META, width), -1.0, jnp.float32)
    for target in range(targets):
        count_ref[target] = 0
    lane = lax.broadcasted_iota(jnp.int32, (META, width), 1)

    def place(j, carry):
        word = words_ref[j]
        reader = word // (KT * CT)
        position = jnp.bitwise_xor(reader, me)
        slot = count_ref[position]
        count_ref[position] = slot + 1
        code = (word - reader * (KT * CT)).astype(jnp.float32)
        x, y, z = position % 2, position // 2 % 2, position // 4
        odd = z % 2
        first, second = jnp.where(odd == 1, y, x), jnp.where(odd == 1, x, y)
        which = 2 * odd + first
        at = second * half + z // 2
        for number, out_ref in enumerate(outs):

            @pl.when(which == number)
            def _():
                out_ref[at, pl.ds(pl.multiple_of(slot * height, height), height), :] = tiles_ref[j]
                codes = out_ref[at, SLOT * height :, :]
                out_ref[at, SLOT * height :, :] = jnp.where(lane == slot, code, codes)

        return carry

    lax.fori_loop(0, count, place, 0)


def pack(tiles, readers, tile_k, tile_column, targets):
    _, height, width = tiles.shape
    vmem = pl.BlockSpec(memory_space=pltpu.VMEM)
    words = (readers.reshape(-1) * KT + tile_k) * CT + tile_column
    out = jax.ShapeDtypeStruct((targets // 4, SLOT * height + META, width), jnp.float32)
    return pl.pallas_call(
        pack_kernel,
        out_shape=[out] * 4,
        in_specs=[pl.BlockSpec(memory_space=pltpu.SMEM), vmem],
        out_specs=[vmem] * 4,
        scratch_shapes=[
            pltpu.SMEM((targets,), jnp.int32),
        ],
        cost_estimate=pl.CostEstimate(flops=0, bytes_accessed=4 * tiles.size * 3, transcendentals=0),
        compiler_params=pltpu.CompilerParams(vmem_limit_bytes=8 * 1024 * 1024),
    )(words, tiles)


def split_kernel(positions, *refs):
    pieces, split_ref = refs[:-1], refs[-1]
    me = lax.axis_index("bulk")
    for piece, held in zip(pieces, positions):
        for at, position in enumerate(held):
            block = piece[at]
            high = block.astype(jnp.bfloat16)
            low = (block - high.astype(jnp.float32)).astype(jnp.bfloat16)
            k = at if position is None else jnp.bitwise_xor(me, position)
            split_ref[k] = jnp.concatenate([high, low], axis=1)


def split(pieces, positions):
    _, rows, width = pieces[0].shape
    vmem = pl.BlockSpec(memory_space=pltpu.VMEM)
    return pl.pallas_call(
        functools.partial(split_kernel, positions),
        out_shape=jax.ShapeDtypeStruct((KT, rows, 2 * width), jnp.bfloat16),
        in_specs=[vmem] * len(pieces),
        out_specs=vmem,
        cost_estimate=pl.CostEstimate(
            flops=0, bytes_accessed=8 * KT * rows * width, transcendentals=0
        ),
        compiler_params=pltpu.CompilerParams(vmem_limit_bytes=16 * 1024 * 1024),
    )(*pieces)


def contract_kernel(groups_count, parts_count, split_ref, *refs):
    end = groups_count * parts_count
    groups = [refs[g * parts_count : (g + 1) * parts_count] for g in range(groups_count)]
    residual_ref, out_ref = refs[end : end + 2]
    codes = refs[end + 2 : end + 2 + groups_count]
    sem = refs[-1]
    height = (groups[0][0].shape[1] - META) // SLOT
    width = groups[0][0].shape[2]
    row = lax.axis_index("row")
    fetches = [
        pltpu.make_async_copy(parts[0].at[:, pl.ds(SLOT * height, META), :], codes[g], sem.at[g])
        for g, parts in enumerate(groups)
    ]
    for fetch in fetches:
        fetch.start()
    out_ref[...] = residual_ref[...]
    for fetch in fetches:
        fetch.wait()

    def whole(parts, owner, slot, code):
        k = code // CT
        column = code - k * CT
        ordered = []
        for place in range(parts_count):
            piece = parts[0][owner, slot * height : (slot + 1) * height, :]
            for q in range(1, parts_count):
                other = parts[q][owner, slot * height : (slot + 1) * height, :]
                piece = jnp.where(lax.rem(place + q, parts_count) == row, other, piece)
            ordered.append(piece)
        return jnp.concatenate(ordered, axis=0), k, column

    def multiply(tile, k, column):
        high = tile.astype(jnp.bfloat16)
        low = (tile - high.astype(jnp.float32)).astype(jnp.bfloat16)
        both = jnp.concatenate([high, low], axis=1)
        weights = jnp.concatenate([both, both], axis=0)
        product = jnp.dot(split_ref[k], weights, preferred_element_type=jnp.float32)
        lanes = pl.ds(pl.multiple_of(column * width, width), width)
        out_ref[:, lanes] += product[:, :width] + product[:, width:]

    def add_group(parts, codes_ref):
        owners = parts[0].shape[0]

        def first(owner):
            code = codes_ref[owner, 0, 0].astype(jnp.int32)
            tile, k, column = whole(parts, owner, 0, jnp.maximum(code, 0))
            multiply(jnp.where(code >= 0, tile, 0.0), k, column)

        def later(owner, slot):
            code = codes_ref[owner, 0, slot].astype(jnp.int32)

            @pl.when(code >= 0)
            def _():
                multiply(*whole(parts, owner, slot, code))

        unroll = next(u for u in (5, 4, 3, 2, 1) if owners % u == 0)

        def some(step, carry):
            for i in range(unroll):
                first(unroll * step + i)
            for i in range(unroll):
                for slot in range(1, SLOT):
                    later(unroll * step + i, slot)
            return carry

        lax.fori_loop(0, owners // unroll, some, 0)

    for parts, codes_ref in zip(groups, codes):
        add_group(parts, codes_ref)


def contract(split_amplitudes, groups, residual):
    width = groups[0][0].shape[2]
    vmem = pl.BlockSpec(memory_space=pltpu.VMEM)
    arrays = [split_amplitudes, *[part for parts in groups for part in parts], residual]
    return pl.pallas_call(
        functools.partial(contract_kernel, len(groups), len(groups[0])),
        out_shape=jax.ShapeDtypeStruct(residual.shape, jnp.float32),
        in_specs=[vmem] * len(arrays),
        out_specs=vmem,
        scratch_shapes=[
            *[pltpu.SMEM((parts[0].shape[0], META, width), jnp.float32) for parts in groups],
            pltpu.SemaphoreType.DMA((len(groups),)),
        ],
        compiler_params=pltpu.CompilerParams(vmem_limit_bytes=24 * 1024 * 1024),
    )(*arrays)


def fetch_kernel(x_ref, out_ref):
    out_ref[...] = x_ref[...]


def fetch(x):
    vmem = pl.BlockSpec(memory_space=pltpu.VMEM)
    return pl.pallas_call(
        fetch_kernel,
        out_shape=jax.ShapeDtypeStruct(x.shape, x.dtype),
        in_specs=[vmem],
        out_specs=vmem,
        compiler_params=pltpu.CompilerParams(vmem_limit_bytes=8 * 1024 * 1024),
    )(x)


def send(x, axis, partner):
    size = lax.axis_size(axis)
    return lax.ppermute(x, axis, [(i, partner(i)) for i in range(size)])


def hop(x, step):
    return send(x, "bulk", lambda i: i ^ step)


def hop_both(blocks, other, step):
    count, height, width = blocks.shape
    flat = jnp.concatenate([blocks.reshape(-1, width), other.reshape(-1, width)], axis=0)
    come = hop(flat, step)
    return come[: count * height].reshape(blocks.shape), come[count * height :].reshape(other.shape)


def local(residual_in, amplitudes, integral_tiles, tile_reader, tile_k, tile_column):
    targets = lax.axis_size("bulk")
    rows_axis = lax.axis_size("row")
    width = integral_tiles.shape[2]
    held, at = amplitudes[None], (0,)
    bit = targets // 2
    while bit > 4:
        held, at = jnp.concatenate([held, hop(held, bit)], axis=0), at + tuple(p ^ bit for p in at)
        bit //= 2
    even_kept, even_sent, odd_kept, odd_sent = pack(
        integral_tiles, tile_reader, tile_k, tile_column, targets
    )
    half = targets // 8
    even_come, odd_come = hop(even_sent, 1), hop(odd_sent, 2)
    late = hop(held, 4)
    first = [jnp.stack([even_kept[z], even_come[z]]) for z in range(half)]
    first = [plane for z in range(half) for plane in (first[z], jnp.stack([odd_kept[z], odd_come[z]]))]
    come_first = [hop(plane, 4 * z) for z, plane in enumerate(first) if z >= half]
    even_last, over_y = hop_both(jnp.concatenate([even_kept[half:], even_come[half:]]), held, 2)
    odd_last, over_x = hop_both(jnp.concatenate([odd_kept[half:], odd_come[half:]]), held, 1)
    last = [
        jnp.stack([come[z], come[half + z]]) for z in range(half) for come in (even_last, odd_last)
    ]
    residual = fetch(residual_in)
    last, come_first, residual = lax.optimization_barrier((last, come_first, residual))
    near = [jnp.concatenate([first[z], last[z]]) for z in range(half)]
    near = [near[0]] + [hop(plane, 4 * z) for z, plane in enumerate(near) if z]
    come_last = [hop(last[z], 4 * z) for z in range(half, 2 * half)]
    cut = len(at) // 2
    come = hop(jnp.concatenate([late, over_y[:cut]]), 1)
    late_x, diagonal_x = come[: len(at)], come[len(at) :]
    come = hop(jnp.concatenate([late, over_x[cut:]]), 2)
    late_y, diagonal_y = come[: len(at)], come[len(at) :]
    pieces = [held, late, over_x, over_y, late_x, late_y, diagonal_x, diagonal_y]
    pieces += [hop(late_y[:cut], 1), hop(late_x[cut:], 2)]
    positions = [tuple(p ^ step for p in at) for step in (0, 4, 1, 2, 5, 6)]
    positions += [tuple(p ^ step for p in part) for step in (3, 7) for part in (at[:cut], at[cut:])]
    groups = []
    for planes in (near[:1] + come_first, near[1:] + come_last):
        mine = jnp.concatenate(planes, axis=0)
        groups.append(
            [mine] + [send(mine, "row", lambda i: (i + q) % rows_axis) for q in range(1, rows_axis)]
        )
    if amplitudes.shape[1] != width:
        stacked = jnp.concatenate(pieces, axis=0)
        listed = [p for held in positions for p in held]
        place = jnp.asarray([listed.index(p) for p in range(targets)], jnp.int32)
        wanted = jnp.bitwise_xor(jnp.arange(targets, dtype=jnp.int32), lax.axis_index("bulk"))
        stacked = stacked[place[wanted]]
        stacked = stacked.transpose(1, 0, 2).reshape(amplitudes.shape[0], KT, width).transpose(1, 0, 2)
        pieces, positions = [stacked], [(None,) * KT]
    return contract(split(pieces, positions), groups, residual)


def solution(mesh):
    placed = (
        P("row", "bulk"),
        P("row", "bulk"),
        P("bulk", "row", None),
        P("bulk", None),
        P("bulk"),
        P("bulk"),
    )
    return jax.shard_map(
        local, mesh=mesh, in_specs=placed, out_specs=P("row", "bulk"), check_vma=False
    )
```

```python
import functools

import jax
import jax.numpy as jnp
from jax import lax
from jax.experimental import pallas as pl
from jax.experimental.pallas import tpu as pltpu
from jax.sharding import PartitionSpec as P

KT = 16
CT = 8
SLOT = 2
META = 8


def pack_kernel(words_ref, tiles_ref, *refs):
    outs, count_ref = refs[:4], refs[4]
    count, height, width = tiles_ref.shape
    half = outs[0].shape[0] // 2
    targets = 8 * half
    me = lax.axis_index("bulk")
    for out_ref in outs:
        out_ref[:, SLOT * height :, :] = jnp.full((2 * half, META, width), -1.0, jnp.float32)
    for target in range(targets):
        count_ref[target] = 0
    lane = lax.broadcasted_iota(jnp.int32, (META, width), 1)

    def place(j, carry):
        word = words_ref[j]
        reader = word // (KT * CT)
        position = jnp.bitwise_xor(reader, me)
        slot = count_ref[position]
        count_ref[position] = slot + 1
        code = (word - reader * (KT * CT)).astype(jnp.float32)
        x, y, z = position % 2, position // 2 % 2, position // 4
        odd = z % 2
        first, second = jnp.where(odd == 1, y, x), jnp.where(odd == 1, x, y)
        which = 2 * odd + first
        at = second * half + z // 2
        for number, out_ref in enumerate(outs):

            @pl.when(which == number)
            def _():
                out_ref[at, pl.ds(pl.multiple_of(slot * height, height), height), :] = tiles_ref[j]
                codes = out_ref[at, SLOT * height :, :]
                out_ref[at, SLOT * height :, :] = jnp.where(lane == slot, code, codes)

        return carry

    lax.fori_loop(0, count, place, 0)


def pack(tiles, readers, tile_k, tile_column, targets):
    _, height, width = tiles.shape
    vmem = pl.BlockSpec(memory_space=pltpu.VMEM)
    words = (readers.reshape(-1) * KT + tile_k) * CT + tile_column
    out = jax.ShapeDtypeStruct((targets // 4, SLOT * height + META, width), jnp.float32)
    return pl.pallas_call(
        pack_kernel,
        out_shape=[out] * 4,
        in_specs=[pl.BlockSpec(memory_space=pltpu.SMEM), vmem],
        out_specs=[vmem] * 4,
        scratch_shapes=[
            pltpu.SMEM((targets,), jnp.int32),
        ],
        cost_estimate=pl.CostEstimate(flops=0, bytes_accessed=4 * tiles.size * 3, transcendentals=0),
        compiler_params=pltpu.CompilerParams(vmem_limit_bytes=8 * 1024 * 1024),
    )(words, tiles)


def split_kernel(positions, *refs):
    pieces, split_ref = refs[:-1], refs[-1]
    me = lax.axis_index("bulk")
    for piece, held in zip(pieces, positions):
        for at, position in enumerate(held):
            block = piece[at]
            high = block.astype(jnp.bfloat16)
            low = (block - high.astype(jnp.float32)).astype(jnp.bfloat16)
            k = at if position is None else jnp.bitwise_xor(me, position)
            split_ref[k] = jnp.concatenate([high, low], axis=1)


def split(pieces, positions):
    _, rows, width = pieces[0].shape
    vmem = pl.BlockSpec(memory_space=pltpu.VMEM)
    return pl.pallas_call(
        functools.partial(split_kernel, positions),
        out_shape=jax.ShapeDtypeStruct((KT, rows, 2 * width), jnp.bfloat16),
        in_specs=[vmem] * len(pieces),
        out_specs=vmem,
        cost_estimate=pl.CostEstimate(
            flops=0, bytes_accessed=8 * KT * rows * width, transcendentals=0
        ),
        compiler_params=pltpu.CompilerParams(vmem_limit_bytes=16 * 1024 * 1024),
    )(*pieces)


def contract_kernel(groups_count, parts_count, split_ref, *refs):
    end = groups_count * parts_count
    groups = [refs[g * parts_count : (g + 1) * parts_count] for g in range(groups_count)]
    residual_ref, out_ref = refs[end : end + 2]
    codes = refs[end + 2 : end + 2 + groups_count]
    sem = refs[-1]
    height = (groups[0][0].shape[1] - META) // SLOT
    width = groups[0][0].shape[2]
    row = lax.axis_index("row")
    fetches = [
        pltpu.make_async_copy(parts[0].at[:, pl.ds(SLOT * height, META), :], codes[g], sem.at[g])
        for g, parts in enumerate(groups)
    ]
    for fetch in fetches:
        fetch.start()
    out_ref[...] = residual_ref[...]
    for fetch in fetches:
        fetch.wait()

    def whole(parts, owner, slot, code):
        k = code // CT
        column = code - k * CT
        ordered = []
        for place in range(parts_count):
            piece = parts[0][owner, slot * height : (slot + 1) * height, :]
            for q in range(1, parts_count):
                other = parts[q][owner, slot * height : (slot + 1) * height, :]
                piece = jnp.where(lax.rem(place + q, parts_count) == row, other, piece)
            ordered.append(piece)
        return jnp.concatenate(ordered, axis=0), k, column

    def multiply(tile, k, column):
        high = tile.astype(jnp.bfloat16)
        low = (tile - high.astype(jnp.float32)).astype(jnp.bfloat16)
        both = jnp.concatenate([high, low], axis=1)
        weights = jnp.concatenate([both, both], axis=0)
        product = jnp.dot(split_ref[k], weights, preferred_element_type=jnp.float32)
        lanes = pl.ds(pl.multiple_of(column * width, width), width)
        out_ref[:, lanes] += product[:, :width] + product[:, width:]

    def add_group(parts, codes_ref):
        owners = parts[0].shape[0]

        def first(owner):
            code = codes_ref[owner, 0, 0].astype(jnp.int32)
            tile, k, column = whole(parts, owner, 0, jnp.maximum(code, 0))
            multiply(jnp.where(code >= 0, tile, 0.0), k, column)

        def later(owner, slot):
            code = codes_ref[owner, 0, slot].astype(jnp.int32)

            @pl.when(code >= 0)
            def _():
                multiply(*whole(parts, owner, slot, code))

        unroll = next(u for u in (5, 4, 3, 2, 1) if owners % u == 0)

        def some(step, carry):
            for i in range(unroll):
                first(unroll * step + i)
            for i in range(unroll):
                for slot in range(1, SLOT):
                    later(unroll * step + i, slot)
            return carry

        lax.fori_loop(0, owners // unroll, some, 0)

    for parts, codes_ref in zip(groups, codes):
        add_group(parts, codes_ref)


def contract(split_amplitudes, groups, residual):
    width = groups[0][0].shape[2]
    vmem = pl.BlockSpec(memory_space=pltpu.VMEM)
    arrays = [split_amplitudes, *[part for parts in groups for part in parts], residual]
    return pl.pallas_call(
        functools.partial(contract_kernel, len(groups), len(groups[0])),
        out_shape=jax.ShapeDtypeStruct(residual.shape, jnp.float32),
        in_specs=[vmem] * len(arrays),
        out_specs=vmem,
        scratch_shapes=[
            *[pltpu.SMEM((parts[0].shape[0], META, width), jnp.float32) for parts in groups],
            pltpu.SemaphoreType.DMA((len(groups),)),
        ],
        compiler_params=pltpu.CompilerParams(vmem_limit_bytes=24 * 1024 * 1024),
    )(*arrays)


def fetch_kernel(x_ref, out_ref):
    out_ref[...] = x_ref[...]


def fetch(x):
    vmem = pl.BlockSpec(memory_space=pltpu.VMEM)
    return pl.pallas_call(
        fetch_kernel,
        out_shape=jax.ShapeDtypeStruct(x.shape, x.dtype),
        in_specs=[vmem],
        out_specs=vmem,
        compiler_params=pltpu.CompilerParams(vmem_limit_bytes=8 * 1024 * 1024),
    )(x)


def send(x, axis, partner):
    size = lax.axis_size(axis)
    return lax.ppermute(x, axis, [(i, partner(i)) for i in range(size)])


def hop(x, step):
    return send(x, "bulk", lambda i: i ^ step)


def hop_both(blocks, other, step):
    count, height, width = blocks.shape
    flat = jnp.concatenate([blocks.reshape(-1, width), other.reshape(-1, width)], axis=0)
    come = hop(flat, step)
    return come[: count * height].reshape(blocks.shape), come[count * height :].reshape(other.shape)


def local(residual_in, amplitudes, integral_tiles, tile_reader, tile_k, tile_column):
    targets = lax.axis_size("bulk")
    rows_axis = lax.axis_size("row")
    width = integral_tiles.shape[2]
    held, at = amplitudes[None], (0,)
    bit = targets // 2
    while bit > 4:
        held, at = jnp.concatenate([held, hop(held, bit)], axis=0), at + tuple(p ^ bit for p in at)
        bit //= 2
    even_kept, even_sent, odd_kept, odd_sent = pack(
        integral_tiles, tile_reader, tile_k, tile_column, targets
    )
    half = targets // 8
    even_come, odd_come = hop(even_sent, 1), hop(odd_sent, 2)
    late = hop(held, 4)
    first = [jnp.stack([even_kept[z], even_come[z]]) for z in range(half)]
    first = [plane for z in range(half) for plane in (first[z], jnp.stack([odd_kept[z], odd_come[z]]))]
    come_first = [hop(plane, 4 * z) for z, plane in enumerate(first) if z >= half]
    cut = len(at) // 2
    late_a, late_b = late[:cut], late[cut:]
    even_last, over_y = hop_both(
        jnp.concatenate([even_kept[half:], even_come[half:]]), jnp.concatenate([held, late_b]), 2
    )
    odd_last, over_x = hop_both(
        jnp.concatenate([odd_kept[half:], odd_come[half:]]), jnp.concatenate([held, late_a]), 1
    )
    last = [
        jnp.stack([come[z], come[half + z]]) for z in range(half) for come in (even_last, odd_last)
    ]
    residual = fetch(residual_in)
    last, come_first, residual = lax.optimization_barrier((last, come_first, residual))
    near = [jnp.concatenate([first[z], last[z]]) for z in range(half)]
    near = [near[0]] + [hop(plane, 4 * z) for z, plane in enumerate(near) if z]
    come_last = [hop(last[z], 4 * z) for z in range(half, 2 * half)]
    size = len(at)
    last_x = hop(jnp.concatenate([late_b, over_y[:cut], over_y[size:]]), 1)
    last_y = hop(jnp.concatenate([late_a, over_x[cut:]]), 2)
    at_a, at_b = tuple(p ^ 4 for p in at[:cut]), tuple(p ^ 4 for p in at[cut:])
    places = (
        (held, 0, at),
        (late, 0, at_a + at_b),
        (over_x, 1, at + at_a),
        (over_y, 2, at + at_b),
        (last_x[: size - cut], 1, at_b),
        (last_x[size - cut :], 3, at[:cut] + at_b),
        (last_y[:cut], 2, at_a),
        (last_y[cut:], 3, at[cut:] + at_a),
    )
    pieces = [piece for piece, _, _ in places]
    positions = [tuple(p ^ step for p in part) for _, step, part in places]
    groups = []
    for planes in (near[:1] + come_first, near[1:] + come_last):
        mine = jnp.concatenate(planes, axis=0)
        groups.append(
            [mine] + [send(mine, "row", lambda i: (i + q) % rows_axis) for q in range(1, rows_axis)]
        )
    if amplitudes.shape[1] != width:
        stacked = jnp.concatenate(pieces, axis=0)
        listed = [p for held in positions for p in held]
        place = jnp.asarray([listed.index(p) for p in range(targets)], jnp.int32)
        wanted = jnp.bitwise_xor(jnp.arange(targets, dtype=jnp.int32), lax.axis_index("bulk"))
        stacked = stacked[place[wanted]]
        stacked = stacked.transpose(1, 0, 2).reshape(amplitudes.shape[0], KT, width).transpose(1, 0, 2)
        pieces, positions = [stacked], [(None,) * KT]
    return contract(split(pieces, positions), groups, residual)


def solution(mesh):
    placed = (
        P("row", "bulk"),
        P("row", "bulk"),
        P("bulk", "row", None),
        P("bulk", None),
        P("bulk"),
        P("bulk"),
    )
    return jax.shard_map(
        local, mesh=mesh, in_specs=placed, out_specs=P("row", "bulk"), check_vma=False
    )
```

```python
import functools

import jax
import jax.numpy as jnp
from jax import lax
from jax.experimental import pallas as pl
from jax.experimental.pallas import tpu as pltpu
from jax.sharding import PartitionSpec as P

KT = 16
CT = 8
SLOT = 2
META = 8


def pack_kernel(words_ref, tiles_ref, *refs):
    outs, count_ref = refs[:4], refs[4]
    count, height, width = tiles_ref.shape
    half = outs[0].shape[0] // 2
    targets = 8 * half
    me = lax.axis_index("bulk")
    for out_ref in outs:
        out_ref[:, SLOT * height :, :] = jnp.full((2 * half, META, width), -1.0, jnp.float32)
    for target in range(targets):
        count_ref[target] = 0
    lane = lax.broadcasted_iota(jnp.int32, (META, width), 1)

    def place(j, carry):
        word = words_ref[j]
        reader = word // (KT * CT)
        position = jnp.bitwise_xor(reader, me)
        slot = count_ref[position]
        count_ref[position] = slot + 1
        code = (word - reader * (KT * CT)).astype(jnp.float32)
        x, y, z = position % 2, position // 2 % 2, position // 4
        odd = z % 2
        first, second = jnp.where(odd == 1, y, x), jnp.where(odd == 1, x, y)
        which = 2 * odd + first
        at = second * half + z // 2
        for number, out_ref in enumerate(outs):

            @pl.when(which == number)
            def _():
                out_ref[at, pl.ds(pl.multiple_of(slot * height, height), height), :] = tiles_ref[j]
                codes = out_ref[at, SLOT * height :, :]
                out_ref[at, SLOT * height :, :] = jnp.where(lane == slot, code, codes)

        return carry

    lax.fori_loop(0, count, place, 0)


def pack(tiles, readers, tile_k, tile_column, targets):
    _, height, width = tiles.shape
    vmem = pl.BlockSpec(memory_space=pltpu.VMEM)
    words = (readers.reshape(-1) * KT + tile_k) * CT + tile_column
    out = jax.ShapeDtypeStruct((targets // 4, SLOT * height + META, width), jnp.float32)
    return pl.pallas_call(
        pack_kernel,
        out_shape=[out] * 4,
        in_specs=[pl.BlockSpec(memory_space=pltpu.SMEM), vmem],
        out_specs=[vmem] * 4,
        scratch_shapes=[
            pltpu.SMEM((targets,), jnp.int32),
        ],
        cost_estimate=pl.CostEstimate(flops=0, bytes_accessed=4 * tiles.size * 3, transcendentals=0),
        compiler_params=pltpu.CompilerParams(vmem_limit_bytes=8 * 1024 * 1024),
    )(words, tiles)


def split_kernel(positions, *refs):
    pieces, split_ref = refs[:-1], refs[-1]
    me = lax.axis_index("bulk")
    for piece, held in zip(pieces, positions):
        for at, position in enumerate(held):
            block = piece[at]
            high = block.astype(jnp.bfloat16)
            low = (block - high.astype(jnp.float32)).astype(jnp.bfloat16)
            k = at if position is None else jnp.bitwise_xor(me, position)
            split_ref[k] = jnp.concatenate([high, low], axis=1)


def split(pieces, positions):
    _, rows, width = pieces[0].shape
    vmem = pl.BlockSpec(memory_space=pltpu.VMEM)
    return pl.pallas_call(
        functools.partial(split_kernel, positions),
        out_shape=jax.ShapeDtypeStruct((KT, rows, 2 * width), jnp.bfloat16),
        in_specs=[vmem] * len(pieces),
        out_specs=vmem,
        cost_estimate=pl.CostEstimate(
            flops=0, bytes_accessed=8 * KT * rows * width, transcendentals=0
        ),
        compiler_params=pltpu.CompilerParams(vmem_limit_bytes=16 * 1024 * 1024),
    )(*pieces)


def contract_kernel(groups_count, parts_count, split_ref, *refs):
    end = groups_count * parts_count
    groups = [refs[g * parts_count : (g + 1) * parts_count] for g in range(groups_count)]
    residual_ref, out_ref = refs[end : end + 2]
    codes = refs[end + 2 : end + 2 + groups_count]
    sem = refs[-1]
    height = (groups[0][0].shape[1] - META) // SLOT
    width = groups[0][0].shape[2]
    row = lax.axis_index("row")
    fetches = [
        pltpu.make_async_copy(parts[0].at[:, pl.ds(SLOT * height, META), :], codes[g], sem.at[g])
        for g, parts in enumerate(groups)
    ]
    for fetch in fetches:
        fetch.start()
    out_ref[...] = residual_ref[...]
    for fetch in fetches:
        fetch.wait()

    def whole(parts, owner, slot, code):
        k = code // CT
        column = code - k * CT
        ordered = []
        for place in range(parts_count):
            piece = parts[0][owner, slot * height : (slot + 1) * height, :]
            for q in range(1, parts_count):
                other = parts[q][owner, slot * height : (slot + 1) * height, :]
                piece = jnp.where(lax.rem(place + q, parts_count) == row, other, piece)
            ordered.append(piece)
        return jnp.concatenate(ordered, axis=0), k, column

    def multiply(tile, k, column):
        high = tile.astype(jnp.bfloat16)
        low = (tile - high.astype(jnp.float32)).astype(jnp.bfloat16)
        both = jnp.concatenate([high, low], axis=1)
        weights = jnp.concatenate([both, both], axis=0)
        product = jnp.dot(split_ref[k], weights, preferred_element_type=jnp.float32)
        lanes = pl.ds(pl.multiple_of(column * width, width), width)
        out_ref[:, lanes] += product[:, :width] + product[:, width:]

    def add_group(parts, codes_ref):
        owners = parts[0].shape[0]

        def first(owner):
            code = codes_ref[owner, 0, 0].astype(jnp.int32)
            tile, k, column = whole(parts, owner, 0, jnp.maximum(code, 0))
            multiply(jnp.where(code >= 0, tile, 0.0), k, column)

        def later(owner, slot):
            code = codes_ref[owner, 0, slot].astype(jnp.int32)

            @pl.when(code >= 0)
            def _():
                multiply(*whole(parts, owner, slot, code))

        unroll = next(u for u in (5, 4, 3, 2, 1) if owners % u == 0)

        def some(step, carry):
            for i in range(unroll):
                first(unroll * step + i)
            for i in range(unroll):
                for slot in range(1, SLOT):
                    later(unroll * step + i, slot)
            return carry

        lax.fori_loop(0, owners // unroll, some, 0)

    for parts, codes_ref in zip(groups, codes):
        add_group(parts, codes_ref)


def contract(split_amplitudes, groups, residual):
    width = groups[0][0].shape[2]
    vmem = pl.BlockSpec(memory_space=pltpu.VMEM)
    arrays = [split_amplitudes, *[part for parts in groups for part in parts], residual]
    return pl.pallas_call(
        functools.partial(contract_kernel, len(groups), len(groups[0])),
        out_shape=jax.ShapeDtypeStruct(residual.shape, jnp.float32),
        in_specs=[vmem] * len(arrays),
        out_specs=vmem,
        scratch_shapes=[
            *[pltpu.SMEM((parts[0].shape[0], META, width), jnp.float32) for parts in groups],
            pltpu.SemaphoreType.DMA((len(groups),)),
        ],
        compiler_params=pltpu.CompilerParams(vmem_limit_bytes=24 * 1024 * 1024),
    )(*arrays)


def fetch_kernel(x_ref, out_ref):
    out_ref[...] = x_ref[...]


def fetch(x):
    vmem = pl.BlockSpec(memory_space=pltpu.VMEM)
    return pl.pallas_call(
        fetch_kernel,
        out_shape=jax.ShapeDtypeStruct(x.shape, x.dtype),
        in_specs=[vmem],
        out_specs=vmem,
        compiler_params=pltpu.CompilerParams(vmem_limit_bytes=8 * 1024 * 1024),
    )(x)


def send(x, axis, partner):
    size = lax.axis_size(axis)
    return lax.ppermute(x, axis, [(i, partner(i)) for i in range(size)])


def hop(x, step):
    return send(x, "bulk", lambda i: i ^ step)


def hop_both(blocks, other, step):
    count, height, width = blocks.shape
    flat = jnp.concatenate([blocks.reshape(-1, width), other.reshape(-1, width)], axis=0)
    come = hop(flat, step)
    return come[: count * height].reshape(blocks.shape), come[count * height :].reshape(other.shape)


def local(residual_in, amplitudes, integral_tiles, tile_reader, tile_k, tile_column):
    targets = lax.axis_size("bulk")
    rows_axis = lax.axis_size("row")
    width = integral_tiles.shape[2]
    held, at = amplitudes[None], (0,)
    bit = targets // 2
    while bit > 4:
        held, at = jnp.concatenate([held, hop(held, bit)], axis=0), at + tuple(p ^ bit for p in at)
        bit //= 2
    even_kept, even_sent, odd_kept, odd_sent = pack(
        integral_tiles, tile_reader, tile_k, tile_column, targets
    )
    half = targets // 8
    even_come, odd_come = hop(even_sent, 1), hop(odd_sent, 2)
    late = hop(held, 4)
    first = [jnp.stack([even_kept[z], even_come[z]]) for z in range(half)]
    first = [plane for z in range(half) for plane in (first[z], jnp.stack([odd_kept[z], odd_come[z]]))]
    come_first = [hop(plane, 4 * z) for z, plane in enumerate(first) if z >= half]
    cut = len(at) // 2
    late_a, late_b = late[:cut], late[cut:]
    even_last, over_y = hop_both(
        jnp.concatenate([even_kept[half:], even_come[half:]]), jnp.concatenate([held, late_b]), 2
    )
    odd_last, over_x = hop_both(
        jnp.concatenate([odd_kept[half:], odd_come[half:]]), jnp.concatenate([held, late_a]), 1
    )
    last = [
        jnp.stack([come[z], come[half + z]]) for z in range(half) for come in (even_last, odd_last)
    ]
    residual = fetch(residual_in)
    last, come_first, residual = lax.optimization_barrier((last, come_first, residual))
    near = [jnp.concatenate([first[z], last[z]]) for z in range(half)]
    near = [near[0]] + [hop(plane, 4 * z) for z, plane in enumerate(near) if z]
    come_last = [hop(last[z], 4 * z) for z in range(half, 2 * half)]
    size = len(at)
    last_x = hop(jnp.concatenate([late_b, over_y[:cut], over_y[size:]]), 1)
    last_y = hop(jnp.concatenate([late_a, over_x[cut:]]), 2)
    come_last, last_x, last_y = lax.optimization_barrier((come_last, last_x, last_y))
    at_a, at_b = tuple(p ^ 4 for p in at[:cut]), tuple(p ^ 4 for p in at[cut:])
    places = (
        (held, 0, at),
        (late, 0, at_a + at_b),
        (over_x, 1, at + at_a),
        (over_y, 2, at + at_b),
        (last_x[: size - cut], 1, at_b),
        (last_x[size - cut :], 3, at[:cut] + at_b),
        (last_y[:cut], 2, at_a),
        (last_y[cut:], 3, at[cut:] + at_a),
    )
    pieces = [piece for piece, _, _ in places]
    positions = [tuple(p ^ step for p in part) for _, step, part in places]
    groups = []
    for planes in (near[:1] + come_first, near[1:], come_last):
        mine = jnp.concatenate(planes, axis=0)
        groups.append(
            [mine] + [send(mine, "row", lambda i: (i + q) % rows_axis) for q in range(1, rows_axis)]
        )
    if amplitudes.shape[1] != width:
        stacked = jnp.concatenate(pieces, axis=0)
        listed = [p for held in positions for p in held]
        place = jnp.asarray([listed.index(p) for p in range(targets)], jnp.int32)
        wanted = jnp.bitwise_xor(jnp.arange(targets, dtype=jnp.int32), lax.axis_index("bulk"))
        stacked = stacked[place[wanted]]
        stacked = stacked.transpose(1, 0, 2).reshape(amplitudes.shape[0], KT, width).transpose(1, 0, 2)
        pieces, positions = [stacked], [(None,) * KT]
    return contract(split(pieces, positions), groups, residual)


def solution(mesh):
    placed = (
        P("row", "bulk"),
        P("row", "bulk"),
        P("bulk", "row", None),
        P("bulk", None),
        P("bulk"),
        P("bulk"),
    )
    return jax.shard_map(
        local, mesh=mesh, in_specs=placed, out_specs=P("row", "bulk"), check_vma=False
    )
```

```python
import functools

import jax
import jax.numpy as jnp
from jax import lax
from jax.experimental import pallas as pl
from jax.experimental.pallas import tpu as pltpu
from jax.sharding import PartitionSpec as P

KT = 16
CT = 8
SLOT = 2
META = 8


def pack_kernel(words_ref, tiles_ref, *refs):
    outs, count_ref = refs[:4], refs[4]
    count, height, width = tiles_ref.shape
    half = outs[0].shape[0] // 2
    targets = 8 * half
    me = lax.axis_index("bulk")
    for out_ref in outs:
        out_ref[:, SLOT * height :, :] = jnp.full((2 * half, META, width), -1.0, jnp.float32)
    for target in range(targets):
        count_ref[target] = 0
    lane = lax.broadcasted_iota(jnp.int32, (META, width), 1)

    def place(j, carry):
        word = words_ref[j]
        reader = word // (KT * CT)
        position = jnp.bitwise_xor(reader, me)
        slot = count_ref[position]
        count_ref[position] = slot + 1
        code = (word - reader * (KT * CT)).astype(jnp.float32)
        x, y, z = position % 2, position // 2 % 2, position // 4
        odd = z % 2
        first, second = jnp.where(odd == 1, y, x), jnp.where(odd == 1, x, y)
        which = 2 * odd + first
        at = second * half + z // 2
        for number, out_ref in enumerate(outs):

            @pl.when(which == number)
            def _():
                out_ref[at, pl.ds(pl.multiple_of(slot * height, height), height), :] = tiles_ref[j]
                codes = out_ref[at, SLOT * height :, :]
                out_ref[at, SLOT * height :, :] = jnp.where(lane == slot, code, codes)

        return carry

    lax.fori_loop(0, count, place, 0)


def pack(tiles, readers, tile_k, tile_column, targets):
    _, height, width = tiles.shape
    vmem = pl.BlockSpec(memory_space=pltpu.VMEM)
    words = (readers.reshape(-1) * KT + tile_k) * CT + tile_column
    out = jax.ShapeDtypeStruct((targets // 4, SLOT * height + META, width), jnp.float32)
    return pl.pallas_call(
        pack_kernel,
        out_shape=[out] * 4,
        in_specs=[pl.BlockSpec(memory_space=pltpu.SMEM), vmem],
        out_specs=[vmem] * 4,
        scratch_shapes=[
            pltpu.SMEM((targets,), jnp.int32),
        ],
        cost_estimate=pl.CostEstimate(flops=0, bytes_accessed=4 * tiles.size * 3, transcendentals=0),
        compiler_params=pltpu.CompilerParams(vmem_limit_bytes=8 * 1024 * 1024),
    )(words, tiles)


def split_kernel(positions, *refs):
    pieces, split_ref = refs[:-1], refs[-1]
    me = lax.axis_index("bulk")
    for piece, held in zip(pieces, positions):
        for at, position in enumerate(held):
            block = piece[at]
            high = block.astype(jnp.bfloat16)
            low = (block - high.astype(jnp.float32)).astype(jnp.bfloat16)
            k = at if position is None else jnp.bitwise_xor(me, position)
            split_ref[k] = jnp.concatenate([high, low], axis=1)


def split(pieces, positions):
    _, rows, width = pieces[0].shape
    vmem = pl.BlockSpec(memory_space=pltpu.VMEM)
    return pl.pallas_call(
        functools.partial(split_kernel, positions),
        out_shape=jax.ShapeDtypeStruct((KT, rows, 2 * width), jnp.bfloat16),
        in_specs=[vmem] * len(pieces),
        out_specs=vmem,
        cost_estimate=pl.CostEstimate(
            flops=0, bytes_accessed=8 * KT * rows * width, transcendentals=0
        ),
        compiler_params=pltpu.CompilerParams(vmem_limit_bytes=16 * 1024 * 1024),
    )(*pieces)


def contract_kernel(groups_count, parts_count, split_ref, *refs):
    end = groups_count * parts_count
    groups = [refs[g * parts_count : (g + 1) * parts_count] for g in range(groups_count)]
    residual_ref, out_ref = refs[end : end + 2]
    codes = refs[end + 2 : end + 2 + groups_count]
    sem = refs[-1]
    height = (groups[0][0].shape[1] - META) // SLOT
    width = groups[0][0].shape[2]
    row = lax.axis_index("row")
    fetches = [
        pltpu.make_async_copy(parts[0].at[:, pl.ds(SLOT * height, META), :], codes[g], sem.at[g])
        for g, parts in enumerate(groups)
    ]
    for fetch in fetches:
        fetch.start()
    out_ref[...] = residual_ref[...]
    for fetch in fetches:
        fetch.wait()

    def whole(parts, owner, slot, code):
        k = code // CT
        column = code - k * CT
        ordered = []
        for place in range(parts_count):
            piece = parts[0][owner, slot * height : (slot + 1) * height, :]
            for q in range(1, parts_count):
                other = parts[q][owner, slot * height : (slot + 1) * height, :]
                piece = jnp.where(lax.rem(place + q, parts_count) == row, other, piece)
            ordered.append(piece)
        return jnp.concatenate(ordered, axis=0), k, column

    def multiply(tile, k, column):
        high = tile.astype(jnp.bfloat16)
        low = (tile - high.astype(jnp.float32)).astype(jnp.bfloat16)
        both = jnp.concatenate([high, low], axis=1)
        weights = jnp.concatenate([both, both], axis=0)
        product = jnp.dot(split_ref[k], weights, preferred_element_type=jnp.float32)
        lanes = pl.ds(pl.multiple_of(column * width, width), width)
        out_ref[:, lanes] += product[:, :width] + product[:, width:]

    def add_group(parts, codes_ref):
        owners = parts[0].shape[0]

        def first(owner):
            code = codes_ref[owner, 0, 0].astype(jnp.int32)
            tile, k, column = whole(parts, owner, 0, jnp.maximum(code, 0))
            multiply(jnp.where(code >= 0, tile, 0.0), k, column)

        def later(owner, slot):
            code = codes_ref[owner, 0, slot].astype(jnp.int32)

            @pl.when(code >= 0)
            def _():
                multiply(*whole(parts, owner, slot, code))

        unroll = next(u for u in (5, 4, 3, 2, 1) if owners % u == 0)

        def some(step, carry):
            for i in range(unroll):
                first(unroll * step + i)
            for i in range(unroll):
                for slot in range(1, SLOT):
                    later(unroll * step + i, slot)
            return carry

        lax.fori_loop(0, owners // unroll, some, 0)

    for parts, codes_ref in zip(groups, codes):
        add_group(parts, codes_ref)


def contract(split_amplitudes, groups, residual):
    width = groups[0][0].shape[2]
    vmem = pl.BlockSpec(memory_space=pltpu.VMEM)
    arrays = [split_amplitudes, *[part for parts in groups for part in parts], residual]
    return pl.pallas_call(
        functools.partial(contract_kernel, len(groups), len(groups[0])),
        out_shape=jax.ShapeDtypeStruct(residual.shape, jnp.float32),
        in_specs=[vmem] * len(arrays),
        out_specs=vmem,
        scratch_shapes=[
            *[pltpu.SMEM((parts[0].shape[0], META, width), jnp.float32) for parts in groups],
            pltpu.SemaphoreType.DMA((len(groups),)),
        ],
        compiler_params=pltpu.CompilerParams(vmem_limit_bytes=24 * 1024 * 1024),
    )(*arrays)


def fetch_kernel(x_ref, out_ref):
    out_ref[...] = x_ref[...]


def fetch(x):
    vmem = pl.BlockSpec(memory_space=pltpu.VMEM)
    return pl.pallas_call(
        fetch_kernel,
        out_shape=jax.ShapeDtypeStruct(x.shape, x.dtype),
        in_specs=[vmem],
        out_specs=vmem,
        compiler_params=pltpu.CompilerParams(vmem_limit_bytes=8 * 1024 * 1024),
    )(x)


def send(x, axis, partner):
    size = lax.axis_size(axis)
    return lax.ppermute(x, axis, [(i, partner(i)) for i in range(size)])


def hop(x, step):
    return send(x, "bulk", lambda i: i ^ step)


def hop_both(blocks, other, step):
    count, height, width = blocks.shape
    flat = jnp.concatenate([blocks.reshape(-1, width), other.reshape(-1, width)], axis=0)
    come = hop(flat, step)
    return come[: count * height].reshape(blocks.shape), come[count * height :].reshape(other.shape)


def local(residual_in, amplitudes, integral_tiles, tile_reader, tile_k, tile_column):
    targets = lax.axis_size("bulk")
    rows_axis = lax.axis_size("row")
    width = integral_tiles.shape[2]
    held, at = amplitudes[None], (0,)
    bit = targets // 2
    while bit > 4:
        held, at = jnp.concatenate([held, hop(held, bit)], axis=0), at + tuple(p ^ bit for p in at)
        bit //= 2
    even_kept, even_sent, odd_kept, odd_sent = pack(
        integral_tiles, tile_reader, tile_k, tile_column, targets
    )
    half = targets // 8
    even_come, odd_come = hop(even_sent, 1), hop(odd_sent, 2)
    late = hop(held, 4)
    first = [jnp.stack([even_kept[z], even_come[z]]) for z in range(half)]
    first = [plane for z in range(half) for plane in (first[z], jnp.stack([odd_kept[z], odd_come[z]]))]
    come_first = [hop(plane, 4 * z) for z, plane in enumerate(first) if z >= half]
    cut = len(at) // 2
    late_a, late_b = late[:cut], late[cut:]
    even_last, over_y = hop_both(
        jnp.concatenate([even_kept[half:], even_come[half:]]), jnp.concatenate([held, late_b]), 2
    )
    odd_last, over_x = hop_both(
        jnp.concatenate([odd_kept[half:], odd_come[half:]]), jnp.concatenate([held, late_a]), 1
    )
    last = [
        jnp.stack([come[z], come[half + z]]) for z in range(half) for come in (even_last, odd_last)
    ]
    residual = fetch(residual_in)
    last, come_first, residual = lax.optimization_barrier((last, come_first, residual))
    near = [jnp.concatenate([first[z], last[z]]) for z in range(half)]
    near = [near[0]] + [hop(plane, 4 * z) for z, plane in enumerate(near) if z]
    come_last = [hop(last[z], 4 * z) for z in range(half, 2 * half)]
    size = len(at)
    last_x = hop(jnp.concatenate([late_b, over_y[:cut], over_y[size:]]), 1)
    last_y = hop(jnp.concatenate([late_a, over_x[cut:]]), 2)
    at_a, at_b = tuple(p ^ 4 for p in at[:cut]), tuple(p ^ 4 for p in at[cut:])
    places = (
        (held, 0, at),
        (late, 0, at_a + at_b),
        (over_x, 1, at + at_a),
        (over_y, 2, at + at_b),
        (last_x[: size - cut], 1, at_b),
        (last_x[size - cut :], 3, at[:cut] + at_b),
        (last_y[:cut], 2, at_a),
        (last_y[cut:], 3, at[cut:] + at_a),
    )
    pieces = [piece for piece, _, _ in places]
    positions = [tuple(p ^ step for p in part) for _, step, part in places]
    groups = []
    for planes in (near[:1], come_first, near[1:], come_last[: half // 2], come_last[half // 2 :]):
        mine = jnp.concatenate(planes, axis=0)
        groups.append(
            [mine] + [send(mine, "row", lambda i: (i + q) % rows_axis) for q in range(1, rows_axis)]
        )
    if amplitudes.shape[1] != width:
        stacked = jnp.concatenate(pieces, axis=0)
        listed = [p for held in positions for p in held]
        place = jnp.asarray([listed.index(p) for p in range(targets)], jnp.int32)
        wanted = jnp.bitwise_xor(jnp.arange(targets, dtype=jnp.int32), lax.axis_index("bulk"))
        stacked = stacked[place[wanted]]
        stacked = stacked.transpose(1, 0, 2).reshape(amplitudes.shape[0], KT, width).transpose(1, 0, 2)
        pieces, positions = [stacked], [(None,) * KT]
    return contract(split(pieces, positions), groups, residual)


def solution(mesh):
    placed = (
        P("row", "bulk"),
        P("row", "bulk"),
        P("bulk", "row", None),
        P("bulk", None),
        P("bulk"),
        P("bulk"),
    )
    return jax.shard_map(
        local, mesh=mesh, in_specs=placed, out_specs=P("row", "bulk"), check_vma=False
    )
```

```python
import functools

import jax
import jax.numpy as jnp
from jax import lax
from jax.experimental import pallas as pl
from jax.experimental.pallas import tpu as pltpu
from jax.sharding import PartitionSpec as P

KT = 16
CT = 8
SLOT = 2
META = 8


def pack_kernel(words_ref, tiles_ref, *refs):
    outs, count_ref = refs[:4], refs[4]
    count, height, width = tiles_ref.shape
    half = outs[0].shape[0] // 2
    targets = 8 * half
    me = lax.axis_index("bulk")
    for out_ref in outs:
        out_ref[:, SLOT * height :, :] = jnp.full((2 * half, META, width), -1.0, jnp.float32)
    for target in range(targets):
        count_ref[target] = 0
    lane = lax.broadcasted_iota(jnp.int32, (META, width), 1)

    def place(j, carry):
        word = words_ref[j]
        reader = word // (KT * CT)
        position = jnp.bitwise_xor(reader, me)
        slot = count_ref[position]
        count_ref[position] = slot + 1
        code = (word - reader * (KT * CT)).astype(jnp.float32)
        x, y, z = position % 2, position // 2 % 2, position // 4
        odd = z % 2
        first, second = jnp.where(odd == 1, y, x), jnp.where(odd == 1, x, y)
        which = 2 * odd + first
        at = second * half + z // 2
        for number, out_ref in enumerate(outs):

            @pl.when(which == number)
            def _():
                out_ref[at, pl.ds(pl.multiple_of(slot * height, height), height), :] = tiles_ref[j]
                codes = out_ref[at, SLOT * height :, :]
                out_ref[at, SLOT * height :, :] = jnp.where(lane == slot, code, codes)

        return carry

    lax.fori_loop(0, count, place, 0)


def pack(tiles, readers, tile_k, tile_column, targets):
    _, height, width = tiles.shape
    vmem = pl.BlockSpec(memory_space=pltpu.VMEM)
    words = (readers.reshape(-1) * KT + tile_k) * CT + tile_column
    out = jax.ShapeDtypeStruct((targets // 4, SLOT * height + META, width), jnp.float32)
    return pl.pallas_call(
        pack_kernel,
        out_shape=[out] * 4,
        in_specs=[pl.BlockSpec(memory_space=pltpu.SMEM), vmem],
        out_specs=[vmem] * 4,
        scratch_shapes=[
            pltpu.SMEM((targets,), jnp.int32),
        ],
        cost_estimate=pl.CostEstimate(flops=0, bytes_accessed=4 * tiles.size * 3, transcendentals=0),
        compiler_params=pltpu.CompilerParams(vmem_limit_bytes=8 * 1024 * 1024),
    )(words, tiles)


def split_kernel(positions, *refs):
    pieces, split_ref = refs[:-1], refs[-1]
    me = lax.axis_index("bulk")
    for piece, held in zip(pieces, positions):
        for at, position in enumerate(held):
            block = piece[at]
            high = block.astype(jnp.bfloat16)
            low = (block - high.astype(jnp.float32)).astype(jnp.bfloat16)
            k = at if position is None else jnp.bitwise_xor(me, position)
            split_ref[k] = jnp.concatenate([high, low], axis=1)


def split(pieces, positions):
    _, rows, width = pieces[0].shape
    vmem = pl.BlockSpec(memory_space=pltpu.VMEM)
    return pl.pallas_call(
        functools.partial(split_kernel, positions),
        out_shape=jax.ShapeDtypeStruct((KT, rows, 2 * width), jnp.bfloat16),
        in_specs=[vmem] * len(pieces),
        out_specs=vmem,
        cost_estimate=pl.CostEstimate(
            flops=0, bytes_accessed=8 * KT * rows * width, transcendentals=0
        ),
        compiler_params=pltpu.CompilerParams(vmem_limit_bytes=16 * 1024 * 1024),
    )(*pieces)


def contract_kernel(groups_count, parts_count, split_ref, *refs):
    end = groups_count * parts_count
    groups = [refs[g * parts_count : (g + 1) * parts_count] for g in range(groups_count)]
    residual_ref, out_ref = refs[end : end + 2]
    codes = refs[end + 2 : end + 2 + groups_count]
    sem = refs[-1]
    height = (groups[0][0].shape[1] - META) // SLOT
    width = groups[0][0].shape[2]
    row = lax.axis_index("row")
    fetches = [
        pltpu.make_async_copy(parts[0].at[:, pl.ds(SLOT * height, META), :], codes[g], sem.at[g])
        for g, parts in enumerate(groups)
    ]
    for fetch in fetches:
        fetch.start()
    out_ref[...] = residual_ref[...]
    for fetch in fetches:
        fetch.wait()

    def whole(parts, owner, slot, code):
        k = code // CT
        column = code - k * CT
        ordered = []
        for place in range(parts_count):
            piece = parts[0][owner, slot * height : (slot + 1) * height, :]
            for q in range(1, parts_count):
                other = parts[q][owner, slot * height : (slot + 1) * height, :]
                piece = jnp.where(lax.rem(place + q, parts_count) == row, other, piece)
            ordered.append(piece)
        return jnp.concatenate(ordered, axis=0), k, column

    def multiply(tile, k, column):
        high = tile.astype(jnp.bfloat16)
        low = (tile - high.astype(jnp.float32)).astype(jnp.bfloat16)
        both = jnp.concatenate([high, low], axis=1)
        weights = jnp.concatenate([both, both], axis=0)
        product = jnp.dot(split_ref[k], weights, preferred_element_type=jnp.float32)
        lanes = pl.ds(pl.multiple_of(column * width, width), width)
        out_ref[:, lanes] += product[:, :width] + product[:, width:]

    def add_group(parts, codes_ref):
        owners = parts[0].shape[0]

        def first(owner):
            code = codes_ref[owner, 0, 0].astype(jnp.int32)
            tile, k, column = whole(parts, owner, 0, jnp.maximum(code, 0))
            multiply(jnp.where(code >= 0, tile, 0.0), k, column)

        def later(owner, slot):
            code = codes_ref[owner, 0, slot].astype(jnp.int32)

            @pl.when(code >= 0)
            def _():
                multiply(*whole(parts, owner, slot, code))

        unroll = next(u for u in (5, 4, 3, 2, 1) if owners % u == 0)

        def some(step, carry):
            for i in range(unroll):
                first(unroll * step + i)
            for i in range(unroll):
                for slot in range(1, SLOT):
                    later(unroll * step + i, slot)
            return carry

        lax.fori_loop(0, owners // unroll, some, 0)

    for parts, codes_ref in zip(groups, codes):
        add_group(parts, codes_ref)


def contract(split_amplitudes, groups, residual):
    width = groups[0][0].shape[2]
    vmem = pl.BlockSpec(memory_space=pltpu.VMEM)
    arrays = [split_amplitudes, *[part for parts in groups for part in parts], residual]
    return pl.pallas_call(
        functools.partial(contract_kernel, len(groups), len(groups[0])),
        out_shape=jax.ShapeDtypeStruct(residual.shape, jnp.float32),
        in_specs=[vmem] * len(arrays),
        out_specs=vmem,
        scratch_shapes=[
            *[pltpu.SMEM((parts[0].shape[0], META, width), jnp.float32) for parts in groups],
            pltpu.SemaphoreType.DMA((len(groups),)),
        ],
        compiler_params=pltpu.CompilerParams(vmem_limit_bytes=24 * 1024 * 1024),
    )(*arrays)


def fetch_kernel(x_ref, out_ref):
    out_ref[...] = x_ref[...]


def fetch(x):
    vmem = pl.BlockSpec(memory_space=pltpu.VMEM)
    return pl.pallas_call(
        fetch_kernel,
        out_shape=jax.ShapeDtypeStruct(x.shape, x.dtype),
        in_specs=[vmem],
        out_specs=vmem,
        compiler_params=pltpu.CompilerParams(vmem_limit_bytes=8 * 1024 * 1024),
    )(x)


def send(x, axis, partner):
    size = lax.axis_size(axis)
    return lax.ppermute(x, axis, [(i, partner(i)) for i in range(size)])


def hop(x, step):
    return send(x, "bulk", lambda i: i ^ step)


def hop_both(blocks, other, step):
    count, height, width = blocks.shape
    flat = jnp.concatenate([blocks.reshape(-1, width), other.reshape(-1, width)], axis=0)
    come = hop(flat, step)
    return come[: count * height].reshape(blocks.shape), come[count * height :].reshape(other.shape)


def local(residual_in, amplitudes, integral_tiles, tile_reader, tile_k, tile_column):
    targets = lax.axis_size("bulk")
    rows_axis = lax.axis_size("row")
    width = integral_tiles.shape[2]
    held, at = amplitudes[None], (0,)
    bit = targets // 2
    while bit > 4:
        held, at = jnp.concatenate([held, hop(held, bit)], axis=0), at + tuple(p ^ bit for p in at)
        bit //= 2
    even_kept, even_sent, odd_kept, odd_sent = pack(
        integral_tiles, tile_reader, tile_k, tile_column, targets
    )
    half = targets // 8
    even_come, odd_come = hop(even_sent, 1), hop(odd_sent, 2)
    late = hop(held, 4)
    first = [jnp.stack([even_kept[z], even_come[z]]) for z in range(half)]
    first = [plane for z in range(half) for plane in (first[z], jnp.stack([odd_kept[z], odd_come[z]]))]
    come_first = [hop(plane, 4 * z) for z, plane in enumerate(first) if z >= half]
    even_last, over_y = hop_both(jnp.concatenate([even_kept[half:], even_come[half:]]), held, 2)
    odd_last, over_x = hop_both(jnp.concatenate([odd_kept[half:], odd_come[half:]]), held, 1)
    last = [
        jnp.stack([come[z], come[half + z]]) for z in range(half) for come in (even_last, odd_last)
    ]
    residual = fetch(residual_in)
    last, come_first, residual = lax.optimization_barrier((last, come_first, residual))
    near = [jnp.concatenate([first[z], last[z]]) for z in range(half)]
    near = [near[0]] + [hop(plane, 4 * z) for z, plane in enumerate(near) if z]
    come_last = [hop(last[z], 4 * z) for z in range(half, 2 * half)]
    cut = len(at) // 2
    come = hop(jnp.concatenate([late, over_y[:cut]]), 1)
    late_x, diagonal_x = come[: len(at)], come[len(at) :]
    come = hop(jnp.concatenate([late, over_x[cut:]]), 2)
    late_y, diagonal_y = come[: len(at)], come[len(at) :]
    pieces = [held, late, over_x, over_y, late_x, late_y, diagonal_x, diagonal_y]
    pieces += [hop(late_y[:cut], 1), hop(late_x[cut:], 2)]
    positions = [tuple(p ^ step for p in at) for step in (0, 4, 1, 2, 5, 6)]
    positions += [tuple(p ^ step for p in part) for step in (3, 7) for part in (at[:cut], at[cut:])]
    ends = (come_last, near[1:], pieces[-2], pieces[-1])
    come_last, near[1:], pieces[-2], pieces[-1] = lax.optimization_barrier(ends)
    groups = []
    for planes in (near[:1] + come_first, near[1:], come_last):
        mine = jnp.concatenate(planes, axis=0)
        groups.append(
            [mine] + [send(mine, "row", lambda i: (i + q) % rows_axis) for q in range(1, rows_axis)]
        )
    if amplitudes.shape[1] != width:
        stacked = jnp.concatenate(pieces, axis=0)
        listed = [p for held in positions for p in held]
        place = jnp.asarray([listed.index(p) for p in range(targets)], jnp.int32)
        wanted = jnp.bitwise_xor(jnp.arange(targets, dtype=jnp.int32), lax.axis_index("bulk"))
        stacked = stacked[place[wanted]]
        stacked = stacked.transpose(1, 0, 2).reshape(amplitudes.shape[0], KT, width).transpose(1, 0, 2)
        pieces, positions = [stacked], [(None,) * KT]
    return contract(split(pieces, positions), groups, residual)


def solution(mesh):
    placed = (
        P("row", "bulk"),
        P("row", "bulk"),
        P("bulk", "row", None),
        P("bulk", None),
        P("bulk"),
        P("bulk"),
    )
    return jax.shard_map(
        local, mesh=mesh, in_specs=placed, out_specs=P("row", "bulk"), check_vma=False
    )
```

```python
import functools

import jax
import jax.numpy as jnp
from jax import lax
from jax.experimental import pallas as pl
from jax.experimental.pallas import tpu as pltpu
from jax.sharding import PartitionSpec as P

KT = 16
CT = 8
SLOT = 2
META = 8


def pack_kernel(words_ref, tiles_ref, *refs):
    outs, count_ref = refs[:4], refs[4]
    count, height, width = tiles_ref.shape
    half = outs[0].shape[0] // 2
    targets = 8 * half
    me = lax.axis_index("bulk")
    for out_ref in outs:
        out_ref[:, SLOT * height :, :] = jnp.full((2 * half, META, width), -1.0, jnp.float32)
    for target in range(targets):
        count_ref[target] = 0
    lane = lax.broadcasted_iota(jnp.int32, (META, width), 1)

    def place(j, carry):
        word = words_ref[j]
        reader = word // (KT * CT)
        position = jnp.bitwise_xor(reader, me)
        slot = count_ref[position]
        count_ref[position] = slot + 1
        code = (word - reader * (KT * CT)).astype(jnp.float32)
        x, y, z = position % 2, position // 2 % 2, position // 4
        odd = z % 2
        first, second = jnp.where(odd == 1, y, x), jnp.where(odd == 1, x, y)
        which = 2 * odd + first
        at = second * half + z // 2
        for number, out_ref in enumerate(outs):

            @pl.when(which == number)
            def _():
                out_ref[at, pl.ds(pl.multiple_of(slot * height, height), height), :] = tiles_ref[j]
                codes = out_ref[at, SLOT * height :, :]
                out_ref[at, SLOT * height :, :] = jnp.where(lane == slot, code, codes)

        return carry

    lax.fori_loop(0, count, place, 0)


def pack(tiles, readers, tile_k, tile_column, targets):
    _, height, width = tiles.shape
    vmem = pl.BlockSpec(memory_space=pltpu.VMEM)
    words = (readers.reshape(-1) * KT + tile_k) * CT + tile_column
    out = jax.ShapeDtypeStruct((targets // 4, SLOT * height + META, width), jnp.float32)
    return pl.pallas_call(
        pack_kernel,
        out_shape=[out] * 4,
        in_specs=[pl.BlockSpec(memory_space=pltpu.SMEM), vmem],
        out_specs=[vmem] * 4,
        scratch_shapes=[
            pltpu.SMEM((targets,), jnp.int32),
        ],
        cost_estimate=pl.CostEstimate(flops=0, bytes_accessed=4 * tiles.size * 3, transcendentals=0),
        compiler_params=pltpu.CompilerParams(vmem_limit_bytes=8 * 1024 * 1024),
    )(words, tiles)


def split_kernel(positions, *refs):
    pieces, split_ref = refs[:-1], refs[-1]
    me = lax.axis_index("bulk")
    for piece, held in zip(pieces, positions):
        for at, position in enumerate(held):
            block = piece[at]
            high = block.astype(jnp.bfloat16)
            low = (block - high.astype(jnp.float32)).astype(jnp.bfloat16)
            k = at if position is None else jnp.bitwise_xor(me, position)
            split_ref[k] = jnp.concatenate([high, low], axis=1)


def split(pieces, positions):
    _, rows, width = pieces[0].shape
    vmem = pl.BlockSpec(memory_space=pltpu.VMEM)
    return pl.pallas_call(
        functools.partial(split_kernel, positions),
        out_shape=jax.ShapeDtypeStruct((KT, rows, 2 * width), jnp.bfloat16),
        in_specs=[vmem] * len(pieces),
        out_specs=vmem,
        cost_estimate=pl.CostEstimate(
            flops=0, bytes_accessed=8 * KT * rows * width, transcendentals=0
        ),
        compiler_params=pltpu.CompilerParams(vmem_limit_bytes=16 * 1024 * 1024),
    )(*pieces)


def contract_kernel(groups_count, parts_count, split_ref, *refs):
    end = groups_count * parts_count
    groups = [refs[g * parts_count : (g + 1) * parts_count] for g in range(groups_count)]
    residual_ref, out_ref = refs[end : end + 2]
    codes = refs[end + 2 : end + 2 + groups_count]
    sem = refs[-1]
    height = (groups[0][0].shape[1] - META) // SLOT
    width = groups[0][0].shape[2]
    row = lax.axis_index("row")
    fetches = [
        pltpu.make_async_copy(parts[0].at[:, pl.ds(SLOT * height, META), :], codes[g], sem.at[g])
        for g, parts in enumerate(groups)
    ]
    for fetch in fetches:
        fetch.start()
    out_ref[...] = residual_ref[...]
    for fetch in fetches:
        fetch.wait()

    def whole(parts, owner, slot, code):
        k = code // CT
        column = code - k * CT
        ordered = []
        for place in range(parts_count):
            piece = parts[0][owner, slot * height : (slot + 1) * height, :]
            for q in range(1, parts_count):
                other = parts[q][owner, slot * height : (slot + 1) * height, :]
                piece = jnp.where(lax.rem(place + q, parts_count) == row, other, piece)
            ordered.append(piece)
        return jnp.concatenate(ordered, axis=0), k, column

    def multiply(tile, k, column):
        high = tile.astype(jnp.bfloat16)
        low = (tile - high.astype(jnp.float32)).astype(jnp.bfloat16)
        both = jnp.concatenate([high, low], axis=1)
        weights = jnp.concatenate([both, both], axis=0)
        product = jnp.dot(split_ref[k], weights, preferred_element_type=jnp.float32)
        lanes = pl.ds(pl.multiple_of(column * width, width), width)
        out_ref[:, lanes] += product[:, :width] + product[:, width:]

    def add_group(parts, codes_ref):
        owners = parts[0].shape[0]

        def first(owner):
            code = codes_ref[owner, 0, 0].astype(jnp.int32)
            tile, k, column = whole(parts, owner, 0, jnp.maximum(code, 0))
            multiply(jnp.where(code >= 0, tile, 0.0), k, column)

        def later(owner, slot):
            code = codes_ref[owner, 0, slot].astype(jnp.int32)

            @pl.when(code >= 0)
            def _():
                multiply(*whole(parts, owner, slot, code))

        unroll = next(u for u in (5, 4, 3, 2, 1) if owners % u == 0)

        def some(step, carry):
            for i in range(unroll):
                first(unroll * step + i)
            for i in range(unroll):
                for slot in range(1, SLOT):
                    later(unroll * step + i, slot)
            return carry

        lax.fori_loop(0, owners // unroll, some, 0)

    for parts, codes_ref in zip(groups, codes):
        add_group(parts, codes_ref)


def contract(split_amplitudes, groups, residual):
    width = groups[0][0].shape[2]
    vmem = pl.BlockSpec(memory_space=pltpu.VMEM)
    arrays = [split_amplitudes, *[part for parts in groups for part in parts], residual]
    return pl.pallas_call(
        functools.partial(contract_kernel, len(groups), len(groups[0])),
        out_shape=jax.ShapeDtypeStruct(residual.shape, jnp.float32),
        in_specs=[vmem] * len(arrays),
        out_specs=vmem,
        scratch_shapes=[
            *[pltpu.SMEM((parts[0].shape[0], META, width), jnp.float32) for parts in groups],
            pltpu.SemaphoreType.DMA((len(groups),)),
        ],
        compiler_params=pltpu.CompilerParams(vmem_limit_bytes=24 * 1024 * 1024),
    )(*arrays)


def fetch_kernel(x_ref, out_ref):
    out_ref[...] = x_ref[...]


def fetch(x):
    vmem = pl.BlockSpec(memory_space=pltpu.VMEM)
    return pl.pallas_call(
        fetch_kernel,
        out_shape=jax.ShapeDtypeStruct(x.shape, x.dtype),
        in_specs=[vmem],
        out_specs=vmem,
        compiler_params=pltpu.CompilerParams(vmem_limit_bytes=8 * 1024 * 1024),
    )(x)


def send(x, axis, partner):
    size = lax.axis_size(axis)
    return lax.ppermute(x, axis, [(i, partner(i)) for i in range(size)])


def hop(x, step):
    return send(x, "bulk", lambda i: i ^ step)


def hop_both(blocks, other, step):
    count, height, width = blocks.shape
    flat = jnp.concatenate([blocks.reshape(-1, width), other.reshape(-1, width)], axis=0)
    come = hop(flat, step)
    return come[: count * height].reshape(blocks.shape), come[count * height :].reshape(other.shape)


def local(residual_in, amplitudes, integral_tiles, tile_reader, tile_k, tile_column):
    targets = lax.axis_size("bulk")
    rows_axis = lax.axis_size("row")
    width = integral_tiles.shape[2]
    held, at = amplitudes[None], (0,)
    bit = targets // 2
    while bit > 4:
        held, at = jnp.concatenate([held, hop(held, bit)], axis=0), at + tuple(p ^ bit for p in at)
        bit //= 2
    even_kept, even_sent, odd_kept, odd_sent = pack(
        integral_tiles, tile_reader, tile_k, tile_column, targets
    )
    half = targets // 8
    even_come, odd_come = hop(even_sent, 1), hop(odd_sent, 2)
    late = hop(held, 4)
    first = [jnp.stack([even_kept[z], even_come[z]]) for z in range(half)]
    first = [plane for z in range(half) for plane in (first[z], jnp.stack([odd_kept[z], odd_come[z]]))]
    come_first = [hop(plane, 4 * z) for z, plane in enumerate(first) if z >= half]
    even_last, over_y = hop_both(jnp.concatenate([even_kept[half:], even_come[half:]]), held, 2)
    odd_last, over_x = hop_both(jnp.concatenate([odd_kept[half:], odd_come[half:]]), held, 1)
    last = [
        jnp.stack([come[z], come[half + z]]) for z in range(half) for come in (even_last, odd_last)
    ]
    residual = fetch(residual_in)
    last, come_first, residual = lax.optimization_barrier((last, come_first, residual))
    near = [jnp.concatenate([first[z], last[z]]) for z in range(half)]
    near = [near[0]] + [hop(plane, 4 * z) for z, plane in enumerate(near) if z]
    come_last = [hop(last[z], 4 * z) for z in range(half, 2 * half)]
    cut = len(at) // 2
    come = hop(jnp.concatenate([late, over_y[:cut]]), 1)
    late_x, diagonal_x = come[: len(at)], come[len(at) :]
    come = hop(jnp.concatenate([late, over_x[cut:]]), 2)
    late_y, diagonal_y = come[: len(at)], come[len(at) :]
    pieces = [held, late, over_x, over_y, late_x, late_y, diagonal_x, diagonal_y]
    pieces += [hop(late_y[:cut], 1), hop(late_x[cut:], 2)]
    positions = [tuple(p ^ step for p in at) for step in (0, 4, 1, 2, 5, 6)]
    positions += [tuple(p ^ step for p in part) for step in (3, 7) for part in (at[:cut], at[cut:])]
    ends = (come_last, near[1:], pieces[-2], pieces[-1])
    come_last, near[1:], pieces[-2], pieces[-1] = lax.optimization_barrier(ends)
    groups = []
    for planes in (near[:1], come_first, near[1:], come_last):
        mine = jnp.concatenate(planes, axis=0)
        groups.append(
            [mine] + [send(mine, "row", lambda i: (i + q) % rows_axis) for q in range(1, rows_axis)]
        )
    if amplitudes.shape[1] != width:
        stacked = jnp.concatenate(pieces, axis=0)
        listed = [p for held in positions for p in held]
        place = jnp.asarray([listed.index(p) for p in range(targets)], jnp.int32)
        wanted = jnp.bitwise_xor(jnp.arange(targets, dtype=jnp.int32), lax.axis_index("bulk"))
        stacked = stacked[place[wanted]]
        stacked = stacked.transpose(1, 0, 2).reshape(amplitudes.shape[0], KT, width).transpose(1, 0, 2)
        pieces, positions = [stacked], [(None,) * KT]
    return contract(split(pieces, positions), groups, residual)


def solution(mesh):
    placed = (
        P("row", "bulk"),
        P("row", "bulk"),
        P("bulk", "row", None),
        P("bulk", None),
        P("bulk"),
        P("bulk"),
    )
    return jax.shard_map(
        local, mesh=mesh, in_specs=placed, out_specs=P("row", "bulk"), check_vma=False
    )
```

```python
import functools

import jax
import jax.numpy as jnp
from jax import lax
from jax.experimental import pallas as pl
from jax.experimental.pallas import tpu as pltpu
from jax.sharding import PartitionSpec as P

KT = 16
CT = 8
SLOT = 2
META = 8


def pack_kernel(words_ref, tiles_ref, *refs):
    outs, count_ref = refs[:4], refs[4]
    count, height, width = tiles_ref.shape
    half = outs[0].shape[0] // 2
    targets = 8 * half
    me = lax.axis_index("bulk")
    for out_ref in outs:
        out_ref[:, SLOT * height :, :] = jnp.full((2 * half, META, width), -1.0, jnp.float32)
    for target in range(targets):
        count_ref[target] = 0
    lane = lax.broadcasted_iota(jnp.int32, (META, width), 1)

    def place(j, carry):
        word = words_ref[j]
        reader = word // (KT * CT)
        position = jnp.bitwise_xor(reader, me)
        slot = count_ref[position]
        count_ref[position] = slot + 1
        code = (word - reader * (KT * CT)).astype(jnp.float32)
        x, y, z = position % 2, position // 2 % 2, position // 4
        odd = z % 2
        first, second = jnp.where(odd == 1, y, x), jnp.where(odd == 1, x, y)
        which = 2 * odd + first
        at = second * half + z // 2
        for number, out_ref in enumerate(outs):

            @pl.when(which == number)
            def _():
                out_ref[at, pl.ds(pl.multiple_of(slot * height, height), height), :] = tiles_ref[j]
                codes = out_ref[at, SLOT * height :, :]
                out_ref[at, SLOT * height :, :] = jnp.where(lane == slot, code, codes)

        return carry

    lax.fori_loop(0, count, place, 0)


def pack(tiles, readers, tile_k, tile_column, targets):
    _, height, width = tiles.shape
    vmem = pl.BlockSpec(memory_space=pltpu.VMEM)
    words = (readers.reshape(-1) * KT + tile_k) * CT + tile_column
    out = jax.ShapeDtypeStruct((targets // 4, SLOT * height + META, width), jnp.float32)
    return pl.pallas_call(
        pack_kernel,
        out_shape=[out] * 4,
        in_specs=[pl.BlockSpec(memory_space=pltpu.SMEM), vmem],
        out_specs=[vmem] * 4,
        scratch_shapes=[
            pltpu.SMEM((targets,), jnp.int32),
        ],
        cost_estimate=pl.CostEstimate(flops=0, bytes_accessed=4 * tiles.size * 3, transcendentals=0),
        compiler_params=pltpu.CompilerParams(vmem_limit_bytes=8 * 1024 * 1024),
    )(words, tiles)


def split_kernel(positions, *refs):
    pieces, split_ref = refs[:-1], refs[-1]
    me = lax.axis_index("bulk")
    for piece, held in zip(pieces, positions):
        for at, position in enumerate(held):
            block = piece[at]
            high = block.astype(jnp.bfloat16)
            low = (block - high.astype(jnp.float32)).astype(jnp.bfloat16)
            k = at if position is None else jnp.bitwise_xor(me, position)
            split_ref[k] = jnp.concatenate([high, low], axis=1)


def split(pieces, positions):
    _, rows, width = pieces[0].shape
    vmem = pl.BlockSpec(memory_space=pltpu.VMEM)
    return pl.pallas_call(
        functools.partial(split_kernel, positions),
        out_shape=jax.ShapeDtypeStruct((KT, rows, 2 * width), jnp.bfloat16),
        in_specs=[vmem] * len(pieces),
        out_specs=vmem,
        cost_estimate=pl.CostEstimate(
            flops=0, bytes_accessed=8 * KT * rows * width, transcendentals=0
        ),
        compiler_params=pltpu.CompilerParams(vmem_limit_bytes=16 * 1024 * 1024),
    )(*pieces)


def contract_kernel(groups_count, parts_count, split_ref, *refs):
    end = groups_count * parts_count
    groups = [refs[g * parts_count : (g + 1) * parts_count] for g in range(groups_count)]
    residual_ref, out_ref = refs[end : end + 2]
    codes = refs[end + 2 : end + 2 + groups_count]
    sem = refs[-1]
    height = (groups[0][0].shape[1] - META) // SLOT
    width = groups[0][0].shape[2]
    row = lax.axis_index("row")
    fetches = [
        pltpu.make_async_copy(parts[0].at[:, pl.ds(SLOT * height, META), :], codes[g], sem.at[g])
        for g, parts in enumerate(groups)
    ]
    for fetch in fetches:
        fetch.start()
    out_ref[...] = residual_ref[...]
    for fetch in fetches:
        fetch.wait()

    def whole(parts, owner, slot, code):
        k = code // CT
        column = code - k * CT
        ordered = []
        for place in range(parts_count):
            piece = parts[0][owner, slot * height : (slot + 1) * height, :]
            for q in range(1, parts_count):
                other = parts[q][owner, slot * height : (slot + 1) * height, :]
                piece = jnp.where(lax.rem(place + q, parts_count) == row, other, piece)
            ordered.append(piece)
        return jnp.concatenate(ordered, axis=0), k, column

    def multiply(tile, k, column):
        high = tile.astype(jnp.bfloat16)
        low = (tile - high.astype(jnp.float32)).astype(jnp.bfloat16)
        both = jnp.concatenate([high, low], axis=1)
        weights = jnp.concatenate([both, both], axis=0)
        product = jnp.dot(split_ref[k], weights, preferred_element_type=jnp.float32)
        lanes = pl.ds(pl.multiple_of(column * width, width), width)
        out_ref[:, lanes] += product[:, :width] + product[:, width:]

    def add_group(parts, codes_ref):
        owners = parts[0].shape[0]

        def first(owner):
            code = codes_ref[owner, 0, 0].astype(jnp.int32)
            tile, k, column = whole(parts, owner, 0, jnp.maximum(code, 0))
            multiply(jnp.where(code >= 0, tile, 0.0), k, column)

        def later(owner, slot):
            code = codes_ref[owner, 0, slot].astype(jnp.int32)

            @pl.when(code >= 0)
            def _():
                multiply(*whole(parts, owner, slot, code))

        unroll = next(u for u in (5, 4, 3, 2, 1) if owners % u == 0)

        def some(step, carry):
            for i in range(unroll):
                first(unroll * step + i)
            for i in range(unroll):
                for slot in range(1, SLOT):
                    later(unroll * step + i, slot)
            return carry

        lax.fori_loop(0, owners // unroll, some, 0)

    for parts, codes_ref in zip(groups, codes):
        add_group(parts, codes_ref)


def contract(split_amplitudes, groups, residual):
    width = groups[0][0].shape[2]
    vmem = pl.BlockSpec(memory_space=pltpu.VMEM)
    arrays = [split_amplitudes, *[part for parts in groups for part in parts], residual]
    return pl.pallas_call(
        functools.partial(contract_kernel, len(groups), len(groups[0])),
        out_shape=jax.ShapeDtypeStruct(residual.shape, jnp.float32),
        in_specs=[vmem] * len(arrays),
        out_specs=vmem,
        scratch_shapes=[
            *[pltpu.SMEM((parts[0].shape[0], META, width), jnp.float32) for parts in groups],
            pltpu.SemaphoreType.DMA((len(groups),)),
        ],
        compiler_params=pltpu.CompilerParams(vmem_limit_bytes=24 * 1024 * 1024),
    )(*arrays)


def fetch_kernel(x_ref, out_ref):
    out_ref[...] = x_ref[...]


def fetch(x):
    vmem = pl.BlockSpec(memory_space=pltpu.VMEM)
    return pl.pallas_call(
        fetch_kernel,
        out_shape=jax.ShapeDtypeStruct(x.shape, x.dtype),
        in_specs=[vmem],
        out_specs=vmem,
        compiler_params=pltpu.CompilerParams(vmem_limit_bytes=8 * 1024 * 1024),
    )(x)


def send(x, axis, partner):
    size = lax.axis_size(axis)
    return lax.ppermute(x, axis, [(i, partner(i)) for i in range(size)])


def hop(x, step):
    return send(x, "bulk", lambda i: i ^ step)


def hop_both(blocks, other, step):
    count, height, width = blocks.shape
    flat = jnp.concatenate([blocks.reshape(-1, width), other.reshape(-1, width)], axis=0)
    come = hop(flat, step)
    return come[: count * height].reshape(blocks.shape), come[count * height :].reshape(other.shape)


def local(residual_in, amplitudes, integral_tiles, tile_reader, tile_k, tile_column):
    targets = lax.axis_size("bulk")
    rows_axis = lax.axis_size("row")
    width = integral_tiles.shape[2]
    held, at = amplitudes[None], (0,)
    bit = targets // 2
    while bit > 4:
        held, at = jnp.concatenate([held, hop(held, bit)], axis=0), at + tuple(p ^ bit for p in at)
        bit //= 2
    even_kept, even_sent, odd_kept, odd_sent = pack(
        integral_tiles, tile_reader, tile_k, tile_column, targets
    )
    half = targets // 8
    even_come, odd_come = hop(even_sent, 1), hop(odd_sent, 2)
    late = hop(held, 4)
    first = [jnp.stack([even_kept[z], even_come[z]]) for z in range(half)]
    first = [plane for z in range(half) for plane in (first[z], jnp.stack([odd_kept[z], odd_come[z]]))]
    come_first = [hop(plane, 4 * z) for z, plane in enumerate(first) if z >= half]
    even_last, over_y = hop_both(jnp.concatenate([even_kept[half:], even_come[half:]]), held, 2)
    odd_last, over_x = hop_both(jnp.concatenate([odd_kept[half:], odd_come[half:]]), held, 1)
    last = [
        jnp.stack([come[z], come[half + z]]) for z in range(half) for come in (even_last, odd_last)
    ]
    residual = fetch(residual_in)
    last, come_first, residual = lax.optimization_barrier((last, come_first, residual))
    near = [jnp.concatenate([first[z], last[z]]) for z in range(half)]
    near = [near[0]] + [hop(plane, 4 * z) for z, plane in enumerate(near) if z]
    come_last = [hop(last[z], 4 * z) for z in range(half, 2 * half)]
    cut = len(at) // 2
    come = hop(jnp.concatenate([late, over_y[:cut]]), 1)
    late_x, diagonal_x = come[: len(at)], come[len(at) :]
    come = hop(jnp.concatenate([late, over_x[cut:]]), 2)
    late_y, diagonal_y = come[: len(at)], come[len(at) :]
    pieces = [held, late, over_x, over_y, late_x, late_y, diagonal_x, diagonal_y]
    pieces += [hop(late_y[:cut], 1), hop(late_x[cut:], 2)]
    positions = [tuple(p ^ step for p in at) for step in (0, 4, 1, 2, 5, 6)]
    positions += [tuple(p ^ step for p in part) for step in (3, 7) for part in (at[:cut], at[cut:])]
    ends = (come_last, near[1:], pieces[-2], pieces[-1])
    come_last, near[1:], pieces[-2], pieces[-1] = lax.optimization_barrier(ends)
    groups = []
    for planes in (near[:1], come_first, near[1:], come_last):
        mine = jnp.concatenate(planes, axis=0)
        groups.append(
            [mine] + [send(mine, "row", lambda i: (i + q) % rows_axis) for q in range(1, rows_axis)]
        )
    if amplitudes.shape[1] != width:
        stacked = jnp.concatenate(pieces, axis=0)
        listed = [p for held in positions for p in held]
        place = jnp.asarray([listed.index(p) for p in range(targets)], jnp.int32)
        wanted = jnp.bitwise_xor(jnp.arange(targets, dtype=jnp.int32), lax.axis_index("bulk"))
        stacked = stacked[place[wanted]]
        stacked = stacked.transpose(1, 0, 2).reshape(amplitudes.shape[0], KT, width).transpose(1, 0, 2)
        pieces, positions = [stacked], [(None,) * KT]
    split_amplitudes = split(pieces, positions)
    early = contract(split_amplitudes, groups[:2], residual)
    return contract(split_amplitudes, groups[2:], early)


def solution(mesh):
    placed = (
        P("row", "bulk"),
        P("row", "bulk"),
        P("bulk", "row", None),
        P("bulk", None),
        P("bulk"),
        P("bulk"),
    )
    return jax.shard_map(
        local, mesh=mesh, in_specs=placed, out_specs=P("row", "bulk"), check_vma=False
    )
```

```python
import functools

import jax
import jax.numpy as jnp
from jax import lax
from jax.experimental import pallas as pl
from jax.experimental.pallas import tpu as pltpu
from jax.sharding import PartitionSpec as P

KT = 16
CT = 8
SLOT = 2
META = 8


def pack_kernel(words_ref, tiles_ref, *refs):
    outs, count_ref = refs[:4], refs[4]
    count, height, width = tiles_ref.shape
    half = outs[0].shape[0] // 2
    targets = 8 * half
    me = lax.axis_index("bulk")
    for out_ref in outs:
        out_ref[:, SLOT * height :, :] = jnp.full((2 * half, META, width), -1.0, jnp.float32)
    for target in range(targets):
        count_ref[target] = 0
    lane = lax.broadcasted_iota(jnp.int32, (META, width), 1)

    def place(j, carry):
        word = words_ref[j]
        reader = word // (KT * CT)
        position = jnp.bitwise_xor(reader, me)
        slot = count_ref[position]
        count_ref[position] = slot + 1
        code = (word - reader * (KT * CT)).astype(jnp.float32)
        x, y, z = position % 2, position // 2 % 2, position // 4
        odd = z % 2
        first, second = jnp.where(odd == 1, y, x), jnp.where(odd == 1, x, y)
        which = 2 * odd + first
        at = second * half + z // 2
        for number, out_ref in enumerate(outs):

            @pl.when(which == number)
            def _():
                out_ref[at, pl.ds(pl.multiple_of(slot * height, height), height), :] = tiles_ref[j]
                codes = out_ref[at, SLOT * height :, :]
                out_ref[at, SLOT * height :, :] = jnp.where(lane == slot, code, codes)

        return carry

    lax.fori_loop(0, count, place, 0)


def pack(tiles, readers, tile_k, tile_column, targets):
    _, height, width = tiles.shape
    vmem = pl.BlockSpec(memory_space=pltpu.VMEM)
    words = (readers.reshape(-1) * KT + tile_k) * CT + tile_column
    out = jax.ShapeDtypeStruct((targets // 4, SLOT * height + META, width), jnp.float32)
    return pl.pallas_call(
        pack_kernel,
        out_shape=[out] * 4,
        in_specs=[pl.BlockSpec(memory_space=pltpu.SMEM), vmem],
        out_specs=[vmem] * 4,
        scratch_shapes=[
            pltpu.SMEM((targets,), jnp.int32),
        ],
        cost_estimate=pl.CostEstimate(flops=0, bytes_accessed=4 * tiles.size * 3, transcendentals=0),
        compiler_params=pltpu.CompilerParams(vmem_limit_bytes=8 * 1024 * 1024),
    )(words, tiles)


def split_kernel(positions, *refs):
    pieces, split_ref = refs[:-1], refs[-1]
    me = lax.axis_index("bulk")
    for piece, held in zip(pieces, positions):
        for at, position in enumerate(held):
            block = piece[at]
            high = block.astype(jnp.bfloat16)
            low = (block - high.astype(jnp.float32)).astype(jnp.bfloat16)
            k = at if position is None else jnp.bitwise_xor(me, position)
            split_ref[k] = jnp.concatenate([high, low], axis=1)


def split(pieces, positions):
    _, rows, width = pieces[0].shape
    vmem = pl.BlockSpec(memory_space=pltpu.VMEM)
    return pl.pallas_call(
        functools.partial(split_kernel, positions),
        out_shape=jax.ShapeDtypeStruct((KT, rows, 2 * width), jnp.bfloat16),
        in_specs=[vmem] * len(pieces),
        out_specs=vmem,
        cost_estimate=pl.CostEstimate(
            flops=0, bytes_accessed=8 * KT * rows * width, transcendentals=0
        ),
        compiler_params=pltpu.CompilerParams(vmem_limit_bytes=16 * 1024 * 1024),
    )(*pieces)


def contract_kernel(groups_count, parts_count, split_ref, *refs):
    end = groups_count * parts_count
    groups = [refs[g * parts_count : (g + 1) * parts_count] for g in range(groups_count)]
    residual_ref, out_ref = refs[end : end + 2]
    codes = refs[end + 2 : end + 2 + groups_count]
    sem = refs[-1]
    height = (groups[0][0].shape[1] - META) // SLOT
    width = groups[0][0].shape[2]
    row = lax.axis_index("row")
    fetches = [
        pltpu.make_async_copy(parts[0].at[:, pl.ds(SLOT * height, META), :], codes[g], sem.at[g])
        for g, parts in enumerate(groups)
    ]
    for fetch in fetches:
        fetch.start()
    out_ref[...] = residual_ref[...]
    for fetch in fetches:
        fetch.wait()

    def whole(parts, owner, slot, code):
        k = code // CT
        column = code - k * CT
        ordered = []
        for place in range(parts_count):
            piece = parts[0][owner, slot * height : (slot + 1) * height, :]
            for q in range(1, parts_count):
                other = parts[q][owner, slot * height : (slot + 1) * height, :]
                piece = jnp.where(lax.rem(place + q, parts_count) == row, other, piece)
            ordered.append(piece)
        return jnp.concatenate(ordered, axis=0), k, column

    def multiply(tile, k, column):
        high = tile.astype(jnp.bfloat16)
        low = (tile - high.astype(jnp.float32)).astype(jnp.bfloat16)
        both = jnp.concatenate([high, low], axis=1)
        weights = jnp.concatenate([both, both], axis=0)
        product = jnp.dot(split_ref[k], weights, preferred_element_type=jnp.float32)
        lanes = pl.ds(pl.multiple_of(column * width, width), width)
        out_ref[:, lanes] += product[:, :width] + product[:, width:]

    def add_group(parts, codes_ref):
        owners = parts[0].shape[0]

        def first(owner):
            code = codes_ref[owner, 0, 0].astype(jnp.int32)
            tile, k, column = whole(parts, owner, 0, jnp.maximum(code, 0))
            multiply(jnp.where(code >= 0, tile, 0.0), k, column)

        def later(owner, slot):
            code = codes_ref[owner, 0, slot].astype(jnp.int32)

            @pl.when(code >= 0)
            def _():
                multiply(*whole(parts, owner, slot, code))

        unroll = next(u for u in (5, 4, 3, 2, 1) if owners % u == 0)

        def some(step, carry):
            for i in range(unroll):
                first(unroll * step + i)
            for i in range(unroll):
                for slot in range(1, SLOT):
                    later(unroll * step + i, slot)
            return carry

        lax.fori_loop(0, owners // unroll, some, 0)

    for parts, codes_ref in zip(groups, codes):
        add_group(parts, codes_ref)


def contract(split_amplitudes, groups, residual):
    width = groups[0][0].shape[2]
    vmem = pl.BlockSpec(memory_space=pltpu.VMEM)
    arrays = [split_amplitudes, *[part for parts in groups for part in parts], residual]
    return pl.pallas_call(
        functools.partial(contract_kernel, len(groups), len(groups[0])),
        out_shape=jax.ShapeDtypeStruct(residual.shape, jnp.float32),
        in_specs=[vmem] * len(arrays),
        out_specs=vmem,
        scratch_shapes=[
            *[pltpu.SMEM((parts[0].shape[0], META, width), jnp.float32) for parts in groups],
            pltpu.SemaphoreType.DMA((len(groups),)),
        ],
        compiler_params=pltpu.CompilerParams(vmem_limit_bytes=24 * 1024 * 1024),
    )(*arrays)


def fetch_kernel(x_ref, out_ref):
    out_ref[...] = x_ref[...]


def fetch(x):
    vmem = pl.BlockSpec(memory_space=pltpu.VMEM)
    return pl.pallas_call(
        fetch_kernel,
        out_shape=jax.ShapeDtypeStruct(x.shape, x.dtype),
        in_specs=[vmem],
        out_specs=vmem,
        compiler_params=pltpu.CompilerParams(vmem_limit_bytes=8 * 1024 * 1024),
    )(x)


def send(x, axis, partner):
    size = lax.axis_size(axis)
    return lax.ppermute(x, axis, [(i, partner(i)) for i in range(size)])


def hop(x, step):
    return send(x, "bulk", lambda i: i ^ step)


def hop_both(blocks, other, step):
    count, height, width = blocks.shape
    flat = jnp.concatenate([blocks.reshape(-1, width), other.reshape(-1, width)], axis=0)
    come = hop(flat, step)
    return come[: count * height].reshape(blocks.shape), come[count * height :].reshape(other.shape)


def local(residual_in, amplitudes, integral_tiles, tile_reader, tile_k, tile_column):
    targets = lax.axis_size("bulk")
    rows_axis = lax.axis_size("row")
    width = integral_tiles.shape[2]
    held, at = amplitudes[None], (0,)
    bit = targets // 2
    while bit > 4:
        held, at = jnp.concatenate([held, hop(held, bit)], axis=0), at + tuple(p ^ bit for p in at)
        bit //= 2
    even_kept, even_sent, odd_kept, odd_sent = pack(
        integral_tiles, tile_reader, tile_k, tile_column, targets
    )
    half = targets // 8
    even_come, odd_come = hop(even_sent, 1), hop(odd_sent, 2)
    late = hop(held, 4)
    first = [jnp.stack([even_kept[z], even_come[z]]) for z in range(half)]
    first = [plane for z in range(half) for plane in (first[z], jnp.stack([odd_kept[z], odd_come[z]]))]
    come_first = [hop(plane, 4 * z) for z, plane in enumerate(first) if z >= half]
    even_last, over_y = hop_both(jnp.concatenate([even_kept[half:], even_come[half:]]), held, 2)
    odd_last, over_x = hop_both(jnp.concatenate([odd_kept[half:], odd_come[half:]]), held, 1)
    last = [
        jnp.stack([come[z], come[half + z]]) for z in range(half) for come in (even_last, odd_last)
    ]
    residual = fetch(residual_in)
    last, come_first, residual = lax.optimization_barrier((last, come_first, residual))
    near = [jnp.concatenate([first[z], last[z]]) for z in range(half)]
    near = [near[0]] + [hop(plane, 4 * z) for z, plane in enumerate(near) if z]
    come_last = [hop(last[z], 4 * z) for z in range(half, 2 * half)]
    cut = len(at) // 2
    come = hop(jnp.concatenate([late, over_y[:cut]]), 1)
    late_x, diagonal_x = come[: len(at)], come[len(at) :]
    come = hop(jnp.concatenate([late, over_x[cut:]]), 2)
    late_y, diagonal_y = come[: len(at)], come[len(at) :]
    pieces = [held, late, over_x, over_y, late_x, late_y, diagonal_x, diagonal_y]
    pieces += [hop(late_y[:cut], 1), hop(late_x[cut:], 2)]
    positions = [tuple(p ^ step for p in at) for step in (0, 4, 1, 2, 5, 6)]
    positions += [tuple(p ^ step for p in part) for step in (3, 7) for part in (at[:cut], at[cut:])]
    ends = (come_last, pieces[-2], pieces[-1])
    come_last, pieces[-2], pieces[-1] = lax.optimization_barrier(ends)

    def swap(planes):
        mine = jnp.concatenate(planes, axis=0)
        others = [send(mine, "row", lambda i: (i + q) % rows_axis) for q in range(1, rows_axis)]
        return [mine] + others

    groups = [swap(planes) for planes in (near[:1], come_first, come_last)]
    if amplitudes.shape[1] != width:
        stacked = jnp.concatenate(pieces, axis=0)
        listed = [p for held in positions for p in held]
        place = jnp.asarray([listed.index(p) for p in range(targets)], jnp.int32)
        wanted = jnp.bitwise_xor(jnp.arange(targets, dtype=jnp.int32), lax.axis_index("bulk"))
        stacked = stacked[place[wanted]]
        stacked = stacked.transpose(1, 0, 2).reshape(amplitudes.shape[0], KT, width).transpose(1, 0, 2)
        pieces, positions = [stacked], [(None,) * KT]
    split_amplitudes = split(pieces, positions)
    early = contract(split_amplitudes, groups[:2], residual)
    last_near, early = lax.optimization_barrier((near[1:], early))
    return contract(split_amplitudes, [groups[2], swap(last_near)], early)


def solution(mesh):
    placed = (
        P("row", "bulk"),
        P("row", "bulk"),
        P("bulk", "row", None),
        P("bulk", None),
        P("bulk"),
        P("bulk"),
    )
    return jax.shard_map(
        local, mesh=mesh, in_specs=placed, out_specs=P("row", "bulk"), check_vma=False
    )
```

```python
import functools

import jax
import jax.numpy as jnp
from jax import lax
from jax.experimental import pallas as pl
from jax.experimental.pallas import tpu as pltpu
from jax.sharding import PartitionSpec as P

KT = 16
CT = 8
SLOT = 2
META = 8


def pack_kernel(words_ref, tiles_ref, *refs):
    outs, count_ref = refs[:4], refs[4]
    count, height, width = tiles_ref.shape
    half = outs[0].shape[0] // 2
    targets = 8 * half
    me = lax.axis_index("bulk")
    for out_ref in outs:
        out_ref[:, SLOT * height :, :] = jnp.full((2 * half, META, width), -1.0, jnp.float32)
    for target in range(targets):
        count_ref[target] = 0
    lane = lax.broadcasted_iota(jnp.int32, (META, width), 1)

    def place(j, carry):
        word = words_ref[j]
        reader = word // (KT * CT)
        position = jnp.bitwise_xor(reader, me)
        slot = count_ref[position]
        count_ref[position] = slot + 1
        code = (word - reader * (KT * CT)).astype(jnp.float32)
        x, y, z = position % 2, position // 2 % 2, position // 4
        odd = z % 2
        first, second = jnp.where(odd == 1, y, x), jnp.where(odd == 1, x, y)
        which = 2 * odd + first
        at = second * half + z // 2
        for number, out_ref in enumerate(outs):

            @pl.when(which == number)
            def _():
                out_ref[at, pl.ds(pl.multiple_of(slot * height, height), height), :] = tiles_ref[j]
                codes = out_ref[at, SLOT * height :, :]
                out_ref[at, SLOT * height :, :] = jnp.where(lane == slot, code, codes)

        return carry

    lax.fori_loop(0, count, place, 0)


def pack(tiles, readers, tile_k, tile_column, targets):
    _, height, width = tiles.shape
    vmem = pl.BlockSpec(memory_space=pltpu.VMEM)
    words = (readers.reshape(-1) * KT + tile_k) * CT + tile_column
    out = jax.ShapeDtypeStruct((targets // 4, SLOT * height + META, width), jnp.float32)
    return pl.pallas_call(
        pack_kernel,
        out_shape=[out] * 4,
        in_specs=[pl.BlockSpec(memory_space=pltpu.SMEM), vmem],
        out_specs=[vmem] * 4,
        scratch_shapes=[
            pltpu.SMEM((targets,), jnp.int32),
        ],
        cost_estimate=pl.CostEstimate(flops=0, bytes_accessed=4 * tiles.size * 3, transcendentals=0),
        compiler_params=pltpu.CompilerParams(vmem_limit_bytes=8 * 1024 * 1024),
    )(words, tiles)


def split_kernel(positions, *refs):
    pieces, split_ref = refs[:-1], refs[-1]
    me = lax.axis_index("bulk")
    for piece, held in zip(pieces, positions):
        for at, position in enumerate(held):
            block = piece[at]
            high = block.astype(jnp.bfloat16)
            low = (block - high.astype(jnp.float32)).astype(jnp.bfloat16)
            k = at if position is None else jnp.bitwise_xor(me, position)
            split_ref[k] = jnp.concatenate([high, low], axis=1)


def split(pieces, positions):
    _, rows, width = pieces[0].shape
    vmem = pl.BlockSpec(memory_space=pltpu.VMEM)
    return pl.pallas_call(
        functools.partial(split_kernel, positions),
        out_shape=jax.ShapeDtypeStruct((KT, rows, 2 * width), jnp.bfloat16),
        in_specs=[vmem] * len(pieces),
        out_specs=vmem,
        cost_estimate=pl.CostEstimate(
            flops=0, bytes_accessed=8 * KT * rows * width, transcendentals=0
        ),
        compiler_params=pltpu.CompilerParams(vmem_limit_bytes=16 * 1024 * 1024),
    )(*pieces)


def contract_kernel(groups_count, parts_count, split_ref, *refs):
    end = groups_count * parts_count
    groups = [refs[g * parts_count : (g + 1) * parts_count] for g in range(groups_count)]
    residual_ref, out_ref = refs[end : end + 2]
    codes = refs[end + 2 : end + 2 + groups_count]
    sem = refs[-1]
    height = (groups[0][0].shape[1] - META) // SLOT
    width = groups[0][0].shape[2]
    row = lax.axis_index("row")
    fetches = [
        pltpu.make_async_copy(parts[0].at[:, pl.ds(SLOT * height, META), :], codes[g], sem.at[g])
        for g, parts in enumerate(groups)
    ]
    for fetch in fetches:
        fetch.start()
    out_ref[...] = residual_ref[...]
    for fetch in fetches:
        fetch.wait()

    def whole(parts, owner, slot, code):
        k = code // CT
        column = code - k * CT
        ordered = []
        for place in range(parts_count):
            piece = parts[0][owner, slot * height : (slot + 1) * height, :]
            for q in range(1, parts_count):
                other = parts[q][owner, slot * height : (slot + 1) * height, :]
                piece = jnp.where(lax.rem(place + q, parts_count) == row, other, piece)
            ordered.append(piece)
        return jnp.concatenate(ordered, axis=0), k, column

    def multiply(tile, k, column):
        high = tile.astype(jnp.bfloat16)
        low = (tile - high.astype(jnp.float32)).astype(jnp.bfloat16)
        both = jnp.concatenate([high, low], axis=1)
        weights = jnp.concatenate([both, both], axis=0)
        product = jnp.dot(split_ref[k], weights, preferred_element_type=jnp.float32)
        lanes = pl.ds(pl.multiple_of(column * width, width), width)
        out_ref[:, lanes] += product[:, :width] + product[:, width:]

    def add_group(parts, codes_ref):
        owners = parts[0].shape[0]

        def first(owner):
            code = codes_ref[owner, 0, 0].astype(jnp.int32)
            tile, k, column = whole(parts, owner, 0, jnp.maximum(code, 0))
            multiply(jnp.where(code >= 0, tile, 0.0), k, column)

        def later(owner, slot):
            code = codes_ref[owner, 0, slot].astype(jnp.int32)

            @pl.when(code >= 0)
            def _():
                multiply(*whole(parts, owner, slot, code))

        unroll = next(u for u in (5, 4, 3, 2, 1) if owners % u == 0)

        def some(step, carry):
            for i in range(unroll):
                first(unroll * step + i)
            for i in range(unroll):
                for slot in range(1, SLOT):
                    later(unroll * step + i, slot)
            return carry

        lax.fori_loop(0, owners // unroll, some, 0)

    for parts, codes_ref in zip(groups, codes):
        add_group(parts, codes_ref)


def contract(split_amplitudes, groups, residual):
    width = groups[0][0].shape[2]
    vmem = pl.BlockSpec(memory_space=pltpu.VMEM)
    arrays = [split_amplitudes, *[part for parts in groups for part in parts], residual]
    return pl.pallas_call(
        functools.partial(contract_kernel, len(groups), len(groups[0])),
        out_shape=jax.ShapeDtypeStruct(residual.shape, jnp.float32),
        in_specs=[vmem] * len(arrays),
        out_specs=vmem,
        scratch_shapes=[
            *[pltpu.SMEM((parts[0].shape[0], META, width), jnp.float32) for parts in groups],
            pltpu.SemaphoreType.DMA((len(groups),)),
        ],
        compiler_params=pltpu.CompilerParams(vmem_limit_bytes=24 * 1024 * 1024),
    )(*arrays)


def fetch_kernel(x_ref, out_ref):
    out_ref[...] = x_ref[...]


def fetch(x):
    vmem = pl.BlockSpec(memory_space=pltpu.VMEM)
    return pl.pallas_call(
        fetch_kernel,
        out_shape=jax.ShapeDtypeStruct(x.shape, x.dtype),
        in_specs=[vmem],
        out_specs=vmem,
        compiler_params=pltpu.CompilerParams(vmem_limit_bytes=8 * 1024 * 1024),
    )(x)


def send(x, axis, partner):
    size = lax.axis_size(axis)
    return lax.ppermute(x, axis, [(i, partner(i)) for i in range(size)])


def hop(x, step):
    return send(x, "bulk", lambda i: i ^ step)


def hop_both(blocks, other, step):
    count, height, width = blocks.shape
    flat = jnp.concatenate([blocks.reshape(-1, width), other.reshape(-1, width)], axis=0)
    come = hop(flat, step)
    return come[: count * height].reshape(blocks.shape), come[count * height :].reshape(other.shape)


def local(residual_in, amplitudes, integral_tiles, tile_reader, tile_k, tile_column):
    targets = lax.axis_size("bulk")
    rows_axis = lax.axis_size("row")
    width = integral_tiles.shape[2]
    held, at = amplitudes[None], (0,)
    bit = targets // 2
    while bit > 4:
        held, at = jnp.concatenate([held, hop(held, bit)], axis=0), at + tuple(p ^ bit for p in at)
        bit //= 2
    even_kept, even_sent, odd_kept, odd_sent = pack(
        integral_tiles, tile_reader, tile_k, tile_column, targets
    )
    half = targets // 8
    even_come, odd_come = hop(even_sent, 1), hop(odd_sent, 2)
    late = hop(held, 4)
    first = [jnp.stack([even_kept[z], even_come[z]]) for z in range(half)]
    first = [plane for z in range(half) for plane in (first[z], jnp.stack([odd_kept[z], odd_come[z]]))]
    come_first = [hop(plane, 4 * z) for z, plane in enumerate(first) if z >= half]
    even_last, over_y = hop_both(jnp.concatenate([even_kept[half:], even_come[half:]]), held, 2)
    odd_last, over_x = hop_both(jnp.concatenate([odd_kept[half:], odd_come[half:]]), held, 1)
    last = [
        jnp.stack([come[z], come[half + z]]) for z in range(half) for come in (even_last, odd_last)
    ]
    residual = fetch(residual_in)
    last, come_first, residual = lax.optimization_barrier((last, come_first, residual))
    near = [jnp.concatenate([first[z], last[z]]) for z in range(half)]
    come_last = [hop(last[z], 4 * z) for z in range(half, 2 * half)]
    near = [near[0]] + [hop(plane, 4 * z) for z, plane in enumerate(near) if z]
    cut = len(at) // 2
    come = hop(jnp.concatenate([late, over_y[:cut]]), 1)
    late_x, diagonal_x = come[: len(at)], come[len(at) :]
    come = hop(jnp.concatenate([late, over_x[cut:]]), 2)
    late_y, diagonal_y = come[: len(at)], come[len(at) :]
    pieces = [held, late, over_x, over_y, late_x, late_y, diagonal_x, diagonal_y]
    pieces += [hop(late_y[:cut], 1), hop(late_x[cut:], 2)]
    positions = [tuple(p ^ step for p in at) for step in (0, 4, 1, 2, 5, 6)]
    positions += [tuple(p ^ step for p in part) for step in (3, 7) for part in (at[:cut], at[cut:])]
    ends = (near[1:], come_last, pieces[-2], pieces[-1])
    near[1:], come_last, pieces[-2], pieces[-1] = lax.optimization_barrier(ends)
    groups = []
    for planes in (near[:1], come_first, come_last, near[1:]):
        mine = jnp.concatenate(planes, axis=0)
        groups.append(
            [mine] + [send(mine, "row", lambda i: (i + q) % rows_axis) for q in range(1, rows_axis)]
        )
    if amplitudes.shape[1] != width:
        stacked = jnp.concatenate(pieces, axis=0)
        listed = [p for held in positions for p in held]
        place = jnp.asarray([listed.index(p) for p in range(targets)], jnp.int32)
        wanted = jnp.bitwise_xor(jnp.arange(targets, dtype=jnp.int32), lax.axis_index("bulk"))
        stacked = stacked[place[wanted]]
        stacked = stacked.transpose(1, 0, 2).reshape(amplitudes.shape[0], KT, width).transpose(1, 0, 2)
        pieces, positions = [stacked], [(None,) * KT]
    split_amplitudes = split(pieces, positions)
    early = contract(split_amplitudes, groups[:2], residual)
    return contract(split_amplitudes, groups[2:], early)


def solution(mesh):
    placed = (
        P("row", "bulk"),
        P("row", "bulk"),
        P("bulk", "row", None),
        P("bulk", None),
        P("bulk"),
        P("bulk"),
    )
    return jax.shard_map(
        local, mesh=mesh, in_specs=placed, out_specs=P("row", "bulk"), check_vma=False
    )
```
